32 devices in a mesh: region: 32 (over z, y, x, core).
Axes of the slice: x: 2, y: 2, z: 4, core: 2. Of those that a mesh axis runs over, the one named last changes fastest.
Arguments:
- sample_points: float32 [8192, 3, 128], P('region'), may hold values from -6 to 6
- sample_spacing: float32 [8192, 128], P('region'), may hold values from 0.004 to 0.04
- crossed: int32 [8192, 4], P('region'), may hold values from 0 to 31, all different within a row; in each aligned block of 256 rows (0 to 255, 256 to 511, ...) at most 80 rows name the same one
- colour_grad: float32 [3, 8192], P(None, 'region'), may hold values from -24 to 24
- freq: bfloat16 [32, 3, 64], P('region'), may hold values from -18 to 18
- w_hidden: bfloat16 [32, 128, 256], P('region'), may hold values from -0.5 to 0.5
- w_head: bfloat16 [32, 4, 256], P('region'), may hold values from -0.375 to 0.375
Outputs:
- rendered: float32 [3, 8192], P(None, 'region')
- head_grad: float32 [32, 4, 256], P('region')
The draws below stay inside these ranges and needn't reach their ends.
Inputs may be any that keep to these rules, and one draw needn't show every extreme that they name: `crossed`: row r lists 4 distinct regions, in the order ray r meets them. In each aligned block of 256 rays (the rays of one device) no region is listed by more than 80 rays; in some block some region is listed by exactly 80 rays. Every region is listed by some ray.
All inputs are finite; a program needn't handle non-finite values.
Results may differ from the reference program's by a relative error of at most 0.0019.
Values may be sent and summed in bfloat16 or wider, within the bound.
No kernel may reach another device: no remote copies, remote signals or barrier semaphores. Data moves between devices by JAX's collectives and lax.ppermute only.
A program may use at most 192 MiB of HBM per device.

```python
import math
import jax
import jax.numpy as jnp
import numpy as np
from jax import lax

RAYS_DEV = 256
K = 4
S = 32
FREQ = 64
HID = 256
FEAT = 128
REGIONS = 32
RAYS = 8192
CAP = 80


def level_of(own_key, extent, pieces, low, high):
    loudness = 1.0
    for axis_at, shards_of in pieces:
        steps = jax.random.uniform(jax.random.fold_in(jax.random.fold_in(own_key, 6), axis_at), (shards_of,), jnp.float32, low / len(pieces), high / len(pieces))
        loudness = loudness * jnp.repeat(jnp.exp(steps), extent[axis_at] // shards_of).reshape((-1,) + (1,) * (len(extent) - 1 - axis_at))
    return loudness


def shared_out(key, own, number, rows, count, top, reach, lean):
    order = jax.random.permutation(key, count)
    crowded, common = portions_of(count, rows * top, reach, lean, True), portions_of(count, rows * top, reach, lean, False)
    places = jnp.arange(count)

    def named(sizes, rotation):
        used = int((sizes > 0).sum())
        fixed = max(1, used // 4)
        passed = fixed + (places - fixed + rotation * (used - fixed)) % max(1, count - fixed)
        return jnp.zeros((count,), jnp.int32).at[order[jnp.where(places < fixed, places, passed)]].set(jnp.asarray(sizes, jnp.int32))

    sizes = jnp.where(number % 4 == 0, named(crowded, number // 4), named(common, number - number // 4 - 1))
    mixed = jax.random.permutation(jax.random.fold_in(own, 3), count)
    source_of, receiver = mixed[0:count // 2 * 2:2], mixed[1:count // 2 * 2:2]
    room = jnp.minimum(sizes[source_of] - 1, reach - sizes[receiver]) // 2
    room = jnp.where((source_of == order[0]) | (receiver == order[0]) | (sizes[receiver] == 0), 0, jnp.maximum(room, 0))
    passed = jax.random.randint(jax.random.fold_in(own, 4), (count // 2,), 0, 1 << 20) % (room + 1)
    sizes = sizes.at[source_of].add(-passed).at[receiver].add(passed)
    items = jnp.searchsorted(jnp.cumsum(sizes), jnp.arange(rows * top), side="right").astype(jnp.int32)
    grid = items.reshape(top, rows).T
    grid = grid[jax.random.permutation(jax.random.fold_in(own, 1), rows)]
    rotation = jax.random.randint(jax.random.fold_in(own, 2), (rows, 1), 0, top)
    return jnp.take_along_axis(grid, (jnp.arange(top)[None, :] + rotation) % top, axis=1)


def portions_of(count, total, reach, slope, full):
    loads = [(1 << 20) // math.isqrt(standing ** slope) + 1 for standing in range(1, count + 1)]
    largest = reach if full else min(reach, max(-(-total // count), total * loads[0] // sum(loads)))
    least = 1 if total - largest >= count - 1 else 0
    counts, spare = [largest] + [least] * (count - 1), total - largest - least * (count - 1)
    while spare > 0:
        free = [i for i in range(1, count) if counts[i] < largest] or [i for i in range(1, count) if counts[i] < reach]
        whole, left = sum([loads[i] for i in free]), spare
        for i in free:
            more = min(reach - counts[i], max(1, left * loads[i] // whole), spare)
            counts[i] = counts[i] + more
            spare = spare - more
    return np.array(counts)


def scatter_about(stream_key, dims, width, bound, cuts=(), held_as=jnp.bfloat16):
    array = jax.random.normal(stream_key, dims, jnp.float32) * width
    if len(cuts) > 0:
        array = level_of(stream_key, dims, cuts, -0.22, 0.18) * array
    return jnp.clip(array, min=-bound, max=bound).astype(held_as)


def setup_inputs(seed: int = 0) -> dict:
    streams_of = jax.random.split(jax.random.key(seed), 8)
    sample_points = scatter_about(streams_of[0], (RAYS, 3, K * S), 1.0, 6.0, ((0, 32),), jnp.float32)
    sample_spacing = jnp.clip(jnp.exp(math.log(0.04) - 2.30258502 * jax.random.uniform(streams_of[1], (RAYS, K * S), jnp.float32) ** level_of(streams_of[1], (RAYS, K * S), ((0, 32),), -0.2, 0.2)), 0.004, 0.04)
    crossed_keys = jax.random.split(jax.random.fold_in(streams_of[2], 1), RAYS // RAYS_DEV)
    crossed_turns = jax.random.permutation(jax.random.fold_in(streams_of[2], 3), RAYS // RAYS_DEV)
    crossed = jax.vmap(lambda own, number: shared_out(jax.random.fold_in(streams_of[2], 2), own, number, RAYS_DEV, REGIONS, K, CAP, 1))(crossed_keys, crossed_turns).reshape((RAYS, K))
    colour_grad = scatter_about(streams_of[3], (3, RAYS), 4.0, 24.0, ((1, 32),), jnp.float32)
    freq = scatter_about(streams_of[4], (REGIONS, 3, FREQ), 3.0, 18.0, ((0, 32),))
    w_hidden = scatter_about(streams_of[5], (REGIONS, FEAT, HID), FEAT ** -0.5, 0.5, ((0, 32),))
    w_head = scatter_about(streams_of[6], (REGIONS, 4, HID), HID ** -0.5, 0.375, ((0, 32),))
    return {"sample_points": sample_points, "sample_spacing": sample_spacing, "crossed": crossed, "colour_grad": colour_grad, "freq": freq, "w_hidden": w_hidden, "w_head": w_head}


def features(points, freq, w_hidden):
    coords = points.reshape(points.shape[0], 3, -1).astype(jnp.float32)
    freq32 = freq.astype(jnp.float32)
    phases = coords[:, 0, :, None] * freq32[:, 0][:, None, :]
    phases = phases + coords[:, 1, :, None] * freq32[:, 1][:, None, :]
    phases = phases + coords[:, 2, :, None] * freq32[:, 2][:, None, :]
    feature = jnp.concatenate([jnp.sin(phases), jnp.cos(phases)], axis=-1).astype(jnp.bfloat16)
    feature = lax.optimization_barrier(feature)
    hidden = jnp.einsum('bsf,bfh->bsh', feature.astype(jnp.float32), w_hidden.astype(jnp.float32), precision=lax.Precision.HIGHEST)
    hidden = jnp.maximum(hidden, 0.0).astype(jnp.bfloat16)
    return lax.optimization_barrier(hidden)

def outputs(hidden, w_head):
    return jnp.einsum('bsh,boh->obs', hidden.astype(jnp.float32), w_head.astype(jnp.float32), precision=lax.Precision.HIGHEST)

def render(raw_out, spacing):
    density = jax.nn.softplus(raw_out[0])
    colour = jax.nn.sigmoid(raw_out[1:])
    optical = density * spacing
    running = jnp.cumsum(optical, axis=-1)
    transmit = jnp.exp(optical - running)
    weight = transmit * (1.0 - jnp.exp(-optical))
    seg_colour = lax.optimization_barrier(jnp.sum(weight[None] * colour, axis=-1))
    seg_trans = jnp.exp(-running[:, -1])
    return jnp.concatenate([seg_colour, seg_trans[None]], axis=0).T

def composite(partials, colour_grad):
    upstream = colour_grad.T
    crossings = partials.shape[1]
    before = jnp.ones(partials.shape[:1], partials.dtype)
    befores = []
    rendered = jnp.zeros_like(upstream)
    for k in range(crossings):
        befores.append(before)
        rendered = rendered + before[:, None] * partials[:, k, :3]
        before = before * partials[:, k, 3]
    behind = jnp.zeros_like(upstream)
    seg_grads = [None] * crossings
    for k in range(crossings - 1, -1, -1):
        grad_colour = befores[k][:, None] * upstream
        grad_trans = befores[k] * lax.optimization_barrier(jnp.sum(upstream * behind, axis=-1))
        seg_grads[k] = jnp.concatenate([grad_colour, grad_trans[:, None]], axis=-1)
        behind = partials[:, k, :3] + partials[:, k, 3][:, None] * behind
    return (rendered.T, jnp.stack(seg_grads, axis=1))

def reference(sample_points, sample_spacing, crossed, colour_grad, freq, w_hidden, w_head):
    seg_total = RAYS * K
    row_block = min(256, seg_total)
    blocks = seg_total // row_block
    points_seg = sample_points.reshape(RAYS, 3, K, S).transpose(0, 2, 1, 3)
    points_in = points_seg.reshape(blocks, row_block, 3 * S)
    spacing_in = sample_spacing.reshape(blocks, row_block, S)
    region_in = crossed.reshape(blocks, row_block).astype(jnp.int32)

    def forward(item_data):
        points, spacing, owner = item_data
        hidden = features(points, freq[owner], w_hidden[owner])
        return render(outputs(hidden, w_head[owner]), spacing)
    partials = lax.map(forward, (points_in, spacing_in, region_in)).reshape(RAYS, K, 4)
    rendered, seg_grads = composite(partials, colour_grad)
    grads_in = seg_grads.reshape(blocks, row_block, 4)

    def backward(accum, item_data):
        points, spacing, owner, upstream = item_data
        hidden = features(points, freq[owner], w_hidden[owner])
        raw_out = outputs(hidden, w_head[owner])
        unused, pullback = jax.vjp(lambda value: render(value, spacing), raw_out)
        raw_grad = pullback(upstream)[0].astype(jnp.bfloat16)
        raw_grad = lax.optimization_barrier(raw_grad)
        contrib = jnp.einsum('obs,bsh->boh', raw_grad.astype(jnp.float32), hidden.astype(jnp.float32), precision=lax.Precision.HIGHEST)
        return (accum.at[owner].add(contrib), None)
    start = jnp.zeros((REGIONS, 4, HID), jnp.float32)
    head_grad, unused = lax.scan(backward, start, (points_in, spacing_in, region_in, grads_in))
    return (rendered, head_grad)
```

```python
import functools
import jax
import jax.numpy as jnp
from jax import lax
from jax.experimental import pallas as pl
from jax.experimental.pallas import tpu as pltpu
from jax.sharding import PartitionSpec as P

F32 = jnp.float32
BF16 = jnp.bfloat16
GROUP = 8
UNROLL = 16
SIN_HALF = (4.44288292, -7.3082457, 3.60635441, -0.84611289, 0.10982699)
TURN = 0.15915494309189535
ROUNDER = 12582912.0


def pieces(value, count):
    parts = []
    for _ in range(count - 1):
        parts.append(value.astype(BF16).astype(F32))
        value = value - parts[-1]
    return parts + [value]


def stacked(value, axis, count):
    return jnp.concatenate(pieces(value, count), axis=axis).astype(BF16)


def folded(value, count):
    rows = value.shape[0] // count
    return functools.reduce(jnp.add, [value[i * rows : (i + 1) * rows] for i in range(count)])


def dot(a, b):
    return lax.dot_general(a, b, (((1,), (0,)), ((), ())), preferred_element_type=F32)


def dot_nt(a, b):
    return lax.dot_general(a, b, (((1,), (1,)), ((), ())), preferred_element_type=F32)


def iota(shape, axis):
    return lax.broadcasted_iota(jnp.int32, shape, axis)


def joined(ref, at):
    return jnp.concatenate([ref[half, at, :] for half in range(ref.shape[0])], axis=1)


def ones_where(condition):
    return jnp.where(condition, 1.0, 0.0).astype(BF16)


def order_kernel(
    dims,
    crossed_ref,
    points_ref,
    spacing_ref,
    freq_ref,
    hidden_w_ref,
    head_w_ref,
    slots_ref,
    meta_ref,
    rows_ref,
    turned_ref,
    small_ref,
):
    regions, rays, crossings, samples, tiles = dims
    lanes = crossings * samples
    width = meta_ref.shape[1]
    turned_ref[...] = hidden_w_ref[...].astype(F32).T.astype(BF16)
    freqs = freq_ref.shape[1]
    small_ref[...] = jnp.zeros(small_ref.shape, BF16)
    for region in range(regions):
        small_ref[region, :4, :] = head_w_ref[...]
        small_ref[region, 4:7, :freqs] = freq_ref[...]

    region_at = iota((regions, rays), 0)
    named = [jnp.where(crossed_ref[k : k + 1, :] == region_at, 1.0, 0.0) for k in range(crossings)]
    listed = functools.reduce(jnp.add, named)
    earlier = ones_where(iota((rays, rays), 0) < iota((rays, rays), 1))
    rank = dot(listed.astype(BF16), earlier)
    count = jnp.sum(listed, axis=1, keepdims=True)
    tile_count = jnp.floor((count + (GROUP - 1)) * (1.0 / GROUP))
    below = ones_where(iota((regions, regions), 1) < iota((regions, regions), 0))
    tile_count = jnp.broadcast_to(tile_count, (regions, width))
    start = dot(below, tile_count.astype(BF16))
    slot = GROUP * start[:, :1] + rank
    slot_rows = [jnp.sum(one * slot, axis=0, keepdims=True) for one in named]
    slots_ref[...] = jnp.concatenate(slot_rows, axis=0)
    ended = jnp.where(start + tile_count <= iota((regions, width), 1).astype(F32), 1.0, 0.0)
    owner = jnp.minimum(jnp.sum(ended, axis=0, keepdims=True), regions - 1.0)
    used = jnp.sum(tile_count, axis=0, keepdims=True)
    meta_ref[...] = jnp.concatenate([owner, used], axis=0).astype(jnp.int32)

    slot_row = jnp.concatenate(slot_rows, axis=1)
    parts = [points_ref[d] * TURN for d in range(3)] + [spacing_ref[...]]
    lane_group = iota((rays, lanes), 1) // samples
    by_segment = []
    for k in range(crossings):
        row = jnp.zeros((rays, lanes), F32)
        for d in range(4):
            moved = pltpu.roll(parts[d], (samples * (d - k)) % lanes, 1) if d != k else parts[d]
            row = jnp.where(lane_group == d, moved, row)
        by_segment.append(row)
    source = stacked(jnp.concatenate(by_segment, axis=0), 1, 3)
    tile_row = jnp.floor(slot_row * (1.0 / GROUP))
    place_row = slot_row - GROUP * tile_row
    in_tile = ones_where(iota((tiles, rays * crossings), 0).astype(F32) == tile_row)
    out_group = iota((tiles, lanes), 1) // samples
    per_row = lanes // samples
    halves = GROUP // per_row
    dense = [[None] * halves for _ in range(4)]
    for s in range(GROUP):
        got = dot(in_tile * ones_where(place_row == s), source)
        got = got[:, :lanes] + got[:, lanes : 2 * lanes] + got[:, 2 * lanes :]
        at, half = s % per_row, s // per_row
        for d in range(4):
            moved = pltpu.roll(got, (samples * (at - d)) % lanes, 1) if d != at else got
            if at == 0:
                dense[d][half] = moved
            else:
                dense[d][half] = jnp.where(out_group == at, moved, dense[d][half])
    rows_ref[...] = jnp.zeros(rows_ref.shape, F32)
    for d in range(4):
        for half in range(halves):
            rows_ref[half, pl.ds(4 + d, tiles, stride=8), :] = dense[d][half]


def steps_used(meta, step):
    return jnp.minimum(step, (meta[1, 0] - 1) // UNROLL)


def feature_kernel(first, meta_ref, rows_ref, small_ref, *refs):
    feature_ref = refs[-1]
    used = meta_ref[1, 0]
    step = first + pl.program_id(0)
    rows = feature_ref.shape[0] // UNROLL
    half = rows // 2

    def phases(index):
        small = small_ref[meta_ref[0, step * UNROLL + index]][:, :128].astype(F32)
        freq = jnp.concatenate([small] * 3, axis=0).T[:half].astype(BF16)
        return dot(freq, stacked(joined(rows_ref, pl.ds(index * 8, 8)), 0, 3))

    def store(index, turns):
        for at in range(0, half, 16):
            part = turns[at : at + 16]
            rest = part - ((part + ROUNDER) - ROUNDER)
            square = rest * rest
            sine = jnp.full_like(square, SIN_HALF[-1])
            for c in SIN_HALF[-2::-1]:
                sine = sine * square + c
            sine = sine * rest
            twice = sine * sine
            left = jnp.maximum(2.0 - twice, 1e-30)
            first = index * rows + at
            feature_ref[first : first + 16, :] = (sine * (left * lax.rsqrt(left))).astype(BF16)
            first = first + half
            feature_ref[first : first + 16, :] = (1.0 - twice).astype(BF16)

    @pl.when(step * UNROLL < used)
    def _():
        ahead = phases(0)
        for index in range(UNROLL):
            turns = ahead
            if index + 1 < UNROLL:
                ahead = phases(index + 1)
            store(index, turns)


def main_kernel(
    dims,
    stages,
    parts,
    meta_ref,
    me_ref,
    slots_ref,
    rows_ref,
    colour_grad_ref,
    head_ref,
    feature_ref,
    *refs,
):
    part_refs = refs[:parts]
    rendered_ref, head_grad_ref = refs[parts : parts + 2]
    hidden_ref, raw_ref, grad_ref, weight_ref, slab_ref, weight_sems, slab_sems = refs[parts + 2 :]
    regions, rays, crossings, samples, tiles = dims
    width = GROUP * samples
    halves, lanes = raw_ref.shape[0], raw_ref.shape[2]
    used = meta_ref[1, 0]
    me = me_ref[0]
    rounds = (used + (UNROLL - 1)) // UNROLL
    units = hidden_ref.shape[0] // tiles
    depth = slab_ref.shape[1] // UNROLL
    held = regions // parts

    def fetch(step, slot):
        at = pl.multiple_of(step * (UNROLL * depth), UNROLL * depth)
        return pltpu.make_async_copy(
            feature_ref.at[pl.ds(at, UNROLL * depth), :], slab_ref.at[slot], slab_sems.at[slot]
        )

    copies = [
        pltpu.make_async_copy(
            part_refs[p], weight_ref.at[p * held : (p + 1) * held], weight_sems.at[p]
        )
        for p in range(parts)
    ]
    fetch(0, 0).start()
    for copy in copies:
        copy.start()
    for copy in copies:
        copy.wait()

    def rows_of(tile, height):
        return pl.ds(pl.multiple_of(tile * height, height), height)

    def forward(step, _):
        slot = lax.rem(step, 2)

        @pl.when(step + 1 < rounds)
        def _():
            fetch(step + 1, 1 - slot).start()

        fetch(step, slot).wait()
        first = step * UNROLL
        named = [meta_ref[0, first + index] for index in range(UNROLL)]

        def layer(index):
            weights = weight_ref[place(named[index] ^ me, stages)]
            return dot(weights, slab_ref[slot, index * depth : (index + 1) * depth, :])

        ahead = layer(0)
        for index in range(UNROLL):
            result = ahead
            if index + 1 < UNROLL:
                ahead = layer(index + 1)
            head(jnp.maximum(first - UNROLL, 0) + index)
            hidden_ref[rows_of(first + index, units), :] = jnp.maximum(result.astype(BF16), 0)
        return 0

    def head(tile):
        raw = dot(head_ref[meta_ref[0, tile]], hidden_ref[rows_of(tile, units), :])
        for half in range(halves):
            raw_ref[half, rows_of(tile, 8), :] = raw[:, half * lanes : (half + 1) * lanes]

    lax.fori_loop(0, rounds, forward, 0)
    for index in range(UNROLL):
        head((rounds - 1) * UNROLL + index)

    valid = iota((tiles, width), 0) < used
    raw = [
        jnp.where(valid, joined(raw_ref, pl.ds(c, tiles, stride=8)), 0.0) for c in range(4)
    ]
    spacing = joined(rows_ref, pl.ds(7, tiles, stride=8))
    decay = jnp.exp(-jnp.abs(raw[0]))
    density = jnp.maximum(raw[0], 0.0) + jnp.log1p(decay)
    slope = jnp.where(raw[0] >= 0, 1.0, decay) / (1.0 + decay)
    colour = [1.0 / (1.0 + jnp.exp(-raw[c])) for c in (1, 2, 3)]
    optical = density * spacing
    lane_a, lane_b = iota((width, width), 0), iota((width, width), 1)
    same = (lane_a // samples) == (lane_b // samples)
    up_to = ones_where(same & (lane_a <= lane_b))
    after = ones_where(same & (lane_a > lane_b))

    def by_pieces(value, matrix):
        return functools.reduce(jnp.add, [dot(p.astype(BF16), matrix) for p in pieces(value, 2)])

    running = by_pieces(optical, up_to)
    passed = jnp.exp(-running)
    weight = jnp.exp(optical - running) * (1.0 - jnp.exp(-optical))
    weighted = [weight * one for one in colour]

    member = ones_where(iota((GROUP, width), 0) == iota((GROUP, width), 1) // samples)
    sums = []
    for value in weighted + [optical]:
        sums.append(functools.reduce(jnp.add, [dot_nt(member, p.astype(BF16)) for p in pieces(value, 2)]))
    segments = rays * crossings
    slot_row = jnp.concatenate([slots_ref[k : k + 1, :] for k in range(crossings)], axis=1)
    tile_row = jnp.floor(slot_row * (1.0 / GROUP))
    place_row = slot_row - GROUP * tile_row
    lists = ones_where(iota((tiles, segments), 0).astype(F32) == tile_row)
    mine = iota((GROUP, segments), 0).astype(F32) == place_row
    in_tile = folded(dot(stacked(jnp.concatenate(sums, axis=0), 0, 2), lists), 2)
    by_ray = [
        jnp.sum(jnp.where(mine, in_tile[c * GROUP : (c + 1) * GROUP], 0.0), axis=0, keepdims=True)
        for c in range(4)
    ]
    seg_colour = jnp.concatenate(by_ray[:3], axis=0)
    seg_trans = jnp.exp(-by_ray[3])

    upstream = colour_grad_ref[...]
    colours = [seg_colour[:, k * rays : (k + 1) * rays] for k in range(crossings)]
    transes = [seg_trans[:, k * rays : (k + 1) * rays] for k in range(crossings)]
    before = jnp.ones((1, rays), F32)
    befores = []
    rendered = jnp.zeros_like(upstream)
    for k in range(crossings):
        befores.append(before)
        rendered = rendered + before * colours[k]
        before = before * transes[k]
    rendered_ref[...] = rendered
    behind = jnp.zeros_like(upstream)
    grads = [None] * crossings
    for k in range(crossings - 1, -1, -1):
        grad_trans = befores[k] * jnp.sum(upstream * behind, axis=0, keepdims=True)
        grads[k] = jnp.concatenate([befores[k] * upstream, grad_trans * transes[k]], axis=0)
        behind = colours[k] + transes[k] * behind
    grads = jnp.concatenate(grads, axis=1)

    placed = jnp.concatenate([jnp.where(mine, grads[c : c + 1], 0.0) for c in range(4)], axis=0)
    in_slots = dot_nt(lists, stacked(placed, 0, 2)).astype(BF16)
    channel_rows = iota((8 * GROUP, width), 0) % (4 * GROUP)
    lane_place = iota((8 * GROUP, width), 1) // samples
    per_sample = [
        dot(in_slots, ones_where(channel_rows == c * GROUP + lane_place)) for c in range(4)
    ]
    inner = functools.reduce(jnp.add, [per_sample[c] * colour[c] for c in range(3)])
    later = by_pieces(weight * inner, after)
    grad_optical = passed * inner - later - per_sample[3]
    raw_grad = [grad_optical * spacing * slope]
    for c in range(3):
        raw_grad.append(per_sample[c] * weighted[c] * (1.0 - colour[c]))
    for c in range(4):
        for half in range(halves):
            at = pl.ds(c, tiles, stride=8)
            grad_ref[half, at, :] = raw_grad[c][:, half * lanes : (half + 1) * lanes]

    head_grad_ref[...] = jnp.zeros(head_grad_ref.shape, F32)

    def backward(step, _):
        first = step * UNROLL
        products = []
        for index in range(UNROLL):
            gradient = joined(grad_ref, rows_of(first + index, 8)).astype(BF16)
            products.append(dot_nt(gradient, hidden_ref[rows_of(first + index, units), :])[:4])
        for index in range(UNROLL):
            head_grad_ref[meta_ref[0, first + index]] += products[index]
        return 0

    lax.fori_loop(0, rounds, backward, 0)


def exchange_stages(count):
    stages = []
    while count > 1:
        size = 4 if count % 4 == 0 and count > 4 else min(count, 4)
        size = 2 if count == 2 else size
        count //= size
        stages.append((count, size))
    return stages


def place(offset, stages):
    at, scale = 0, 1
    for unit, size in stages:
        at = at + ((offset // unit) % size) * scale
        scale = scale * size
    return at


def share_all(value, stages, count):
    held = [value[None]]
    for unit, size in stages:
        sent = held if (unit, size) == stages[-1] else [jnp.concatenate(held, axis=0)]
        held = list(sent)
        for other in range(1, size):
            pairs = [(i, i ^ (unit * other)) for i in range(count)]
            held += [lax.ppermute(piece, "region", pairs) for piece in sent]
    return held


def on_device(sample_points, sample_spacing, crossed, colour_grad, freq, w_hidden, w_head):
    regions = lax.axis_size("region")
    rays, crossings = crossed.shape
    samples = sample_spacing.shape[1] // crossings
    segments = rays * crossings
    tiles = (segments + (GROUP - 1) * regions) // GROUP
    tiles = -(-tiles // UNROLL) * UNROLL
    width, lanes = GROUP * samples, crossings * samples
    halves = width // lanes
    features = w_hidden.shape[1]
    hidden_units = w_hidden.shape[2]
    dims = (regions, rays, crossings, samples, tiles)
    vmem, smem = pltpu.VMEM, pltpu.SMEM
    mib = 1024 * 1024
    limit = 24 * mib

    me = lax.axis_index("region").astype(jnp.int32).reshape(1)
    meta_width = -(-tiles // 128) * 128
    slots, meta, rows, turned, small = pl.pallas_call(
        functools.partial(order_kernel, dims),
        out_shape=(
            jax.ShapeDtypeStruct((crossings, rays), F32),
            jax.ShapeDtypeStruct((2, meta_width), jnp.int32),
            jax.ShapeDtypeStruct((halves, tiles * 8, lanes), F32),
            jax.ShapeDtypeStruct((hidden_units, features), BF16),
            jax.ShapeDtypeStruct((regions, 8, hidden_units), BF16),
        ),
        in_specs=[pl.BlockSpec(memory_space=vmem)] * 6,
        out_specs=[pl.BlockSpec(memory_space=vmem)] * 5,
        compiler_params=pltpu.CompilerParams(vmem_limit_bytes=limit),
        cost_estimate=pl.CostEstimate(flops=4 * 10**9, bytes_accessed=10**7, transcendentals=0),
        name="order",
    )(
        crossed.T,
        sample_points.transpose(1, 0, 2),
        sample_spacing,
        freq[0],
        w_hidden[0],
        w_head[0],
    )

    stages = exchange_stages(regions)
    all_small = lax.all_to_all(small, "region", split_axis=0, concat_axis=0, tiled=True)
    weights = share_all(turned, stages, regions)

    steps = tiles // UNROLL
    split = steps * 7 // 10
    whole = pl.BlockSpec(memory_space=vmem)
    params = pltpu.CompilerParams(vmem_limit_bytes=limit)

    def row_block(begin=0):
        return pl.BlockSpec(
            (halves, UNROLL * 8, lanes), lambda i, m: (0, steps_used(m, i + begin), 0)
        )

    def features_of(first, last, *before):
        return pl.pallas_call(
            functools.partial(feature_kernel, first),
            out_shape=jax.ShapeDtypeStruct((tiles * features, width), BF16),
            grid_spec=pltpu.PrefetchScalarGridSpec(
                num_scalar_prefetch=1,
                grid=(last - first + 1,),
                in_specs=[row_block(first), whole]
                + [pl.BlockSpec(memory_space=pl.ANY)] * len(before),
                out_specs=pl.BlockSpec(
                    (UNROLL * features, width),
                    lambda i, m: (jnp.maximum(steps_used(m, i + first), first), 0),
                ),
            ),
            input_output_aliases={3: 0} if before else {},
            compiler_params=params,
            cost_estimate=pl.CostEstimate(flops=10**10, bytes_accessed=10**7, transcendentals=0),
            name="features",
        )(meta, rows, all_small, *before)

    feature = features_of(split, steps - 1, features_of(0, split - 1))

    kept = 2 * tiles * hidden_units * width
    kept += 4 * regions * hidden_units * features + 12 * halves * tiles * 8 * lanes
    kept = min(60 * mib, kept + 4 * UNROLL * features * width + 8 * mib)
    any_space = pl.BlockSpec(memory_space=pl.ANY)
    rendered, head_grad = pl.pallas_call(
        functools.partial(main_kernel, dims, stages, len(weights)),
        out_shape=(
            jax.ShapeDtypeStruct((3, rays), F32),
            jax.ShapeDtypeStruct((regions, 4, hidden_units), F32),
        ),
        in_specs=[pl.BlockSpec(memory_space=smem)] * 2
        + [whole] * 4
        + [any_space]
        + [whole] * len(weights),
        out_specs=[whole] * 2,
        scratch_shapes=[
            pltpu.VMEM((tiles * hidden_units, width), BF16),
            pltpu.VMEM((halves, tiles * 8, lanes), F32),
            pltpu.VMEM((halves, tiles * 8, lanes), F32),
            pltpu.VMEM((regions, hidden_units, features), BF16),
            pltpu.VMEM((2, UNROLL * features, width), BF16),
            pltpu.SemaphoreType.DMA((len(weights),)),
            pltpu.SemaphoreType.DMA((2,)),
        ],
        compiler_params=pltpu.CompilerParams(vmem_limit_bytes=kept),
        cost_estimate=pl.CostEstimate(flops=2 * 10**10, bytes_accessed=3 * 10**7, transcendentals=0),
        name="render",
    )(meta, me, slots, rows, colour_grad, all_small, feature, *weights)

    partial_sums = lax.all_to_all(head_grad, "region", split_axis=0, concat_axis=0, tiled=True)
    head_grad = jnp.sum(partial_sums, axis=0, keepdims=True)
    return (rendered, head_grad)


def solution(mesh):
    return jax.shard_map(
        on_device,
        mesh=mesh,
        in_specs=(
            P("region", None, None),
            P("region", None),
            P("region", None),
            P(None, "region"),
            P("region", None, None),
            P("region", None, None),
            P("region", None, None),
        ),
        out_specs=(P(None, "region"), P("region", None, None)),
        check_vma=False,
    )
```

```python
import functools
import jax
import jax.numpy as jnp
from jax import lax
from jax.experimental import pallas as pl
from jax.experimental.pallas import tpu as pltpu
from jax.sharding import PartitionSpec as P

F32 = jnp.float32
BF16 = jnp.bfloat16
GROUP = 8
UNROLL = 16
SIN_HALF = (4.44288292, -7.3082457, 3.60635441, -0.84611289, 0.10982699)
TURN = 0.15915494309189535
ROUNDER = 12582912.0


def pieces(value, count):
    parts = []
    for _ in range(count - 1):
        parts.append(value.astype(BF16).astype(F32))
        value = value - parts[-1]
    return parts + [value]


def stacked(value, axis, count):
    return jnp.concatenate(pieces(value, count), axis=axis).astype(BF16)


def folded(value, count):
    rows = value.shape[0] // count
    return functools.reduce(jnp.add, [value[i * rows : (i + 1) * rows] for i in range(count)])


def dot(a, b):
    return lax.dot_general(a, b, (((1,), (0,)), ((), ())), preferred_element_type=F32)


def dot_nt(a, b):
    return lax.dot_general(a, b, (((1,), (1,)), ((), ())), preferred_element_type=F32)


def iota(shape, axis):
    return lax.broadcasted_iota(jnp.int32, shape, axis)


def joined(ref, at):
    return jnp.concatenate([ref[half, at, :] for half in range(ref.shape[0])], axis=1)


def ones_where(condition):
    return jnp.where(condition, 1.0, 0.0).astype(BF16)


def order_kernel(dims, samples_ref, crossed_ref, slots_ref, meta_ref, rows_ref):
    regions, rays, crossings, samples, tiles = dims
    lanes = crossings * samples
    width = meta_ref.shape[1]
    region_at = iota((regions, rays), 0)
    named = [jnp.where(crossed_ref[k : k + 1, :] == region_at, 1.0, 0.0) for k in range(crossings)]
    listed = functools.reduce(jnp.add, named)
    earlier = ones_where(iota((rays, rays), 0) < iota((rays, rays), 1))
    rank = dot(listed.astype(BF16), earlier)
    count = jnp.sum(listed, axis=1, keepdims=True)
    tile_count = jnp.floor((count + (GROUP - 1)) * (1.0 / GROUP))
    below = ones_where(iota((regions, regions), 1) < iota((regions, regions), 0))
    tile_count = jnp.broadcast_to(tile_count, (regions, width))
    start = dot(below, tile_count.astype(BF16))
    slot = GROUP * start[:, :1] + rank
    slot_rows = [jnp.sum(one * slot, axis=0, keepdims=True) for one in named]
    slots_ref[...] = jnp.concatenate(slot_rows, axis=0)
    ended = jnp.where(start + tile_count <= iota((regions, width), 1).astype(F32), 1.0, 0.0)
    owner = jnp.minimum(jnp.sum(ended, axis=0, keepdims=True), regions - 1.0)
    used = jnp.sum(tile_count, axis=0, keepdims=True)
    meta_ref[...] = jnp.concatenate([owner, used], axis=0).astype(jnp.int32)

    slot_row = jnp.concatenate(slot_rows, axis=1)
    parts = [samples_ref[d] * TURN for d in range(3)] + [samples_ref[3]]
    lane_group = iota((rays, lanes), 1) // samples
    by_segment = []
    for k in range(crossings):
        row = jnp.zeros((rays, lanes), F32)
        for d in range(4):
            moved = pltpu.roll(parts[d], (samples * (d - k)) % lanes, 1) if d != k else parts[d]
            row = jnp.where(lane_group == d, moved, row)
        by_segment.append(row)
    source = stacked(jnp.concatenate(by_segment, axis=0), 1, 3)
    tile_row = jnp.floor(slot_row * (1.0 / GROUP))
    place_row = slot_row - GROUP * tile_row
    in_tile = ones_where(iota((tiles, rays * crossings), 0).astype(F32) == tile_row)
    out_group = iota((tiles, lanes), 1) // samples
    per_row = lanes // samples
    halves = GROUP // per_row
    dense = [[None] * halves for _ in range(4)]
    for s in range(GROUP):
        got = dot(in_tile * ones_where(place_row == s), source)
        got = got[:, :lanes] + got[:, lanes : 2 * lanes] + got[:, 2 * lanes :]
        at, half = s % per_row, s // per_row
        for d in range(4):
            moved = pltpu.roll(got, (samples * (at - d)) % lanes, 1) if d != at else got
            if at == 0:
                dense[d][half] = moved
            else:
                dense[d][half] = jnp.where(out_group == at, moved, dense[d][half])
    rows_ref[...] = jnp.zeros(rows_ref.shape, F32)
    for d in range(4):
        for half in range(halves):
            rows_ref[half, pl.ds(4 + d, tiles, stride=8), :] = dense[d][half]


def tile_rows(tile, height):
    return pl.ds(pl.multiple_of(tile * height, height), height)


def phases_of(tile, half, meta_ref, rows_ref, small_ref):
    small = small_ref[meta_ref[0, tile]][:, :128].astype(F32)
    freq = jnp.concatenate([small] * 3, axis=0).T[:half].astype(BF16)
    return dot(freq, stacked(joined(rows_ref, tile_rows(tile, 8)), 0, 3))


def store_features(turns, feature_ref, first):
    half = turns.shape[0]
    for at in range(0, half, 16):
        part = turns[at : at + 16]
        rest = part - ((part + ROUNDER) - ROUNDER)
        square = rest * rest
        sine = jnp.full_like(square, SIN_HALF[-1])
        for c in SIN_HALF[-2::-1]:
            sine = sine * square + c
        sine = sine * rest
        twice = sine * sine
        left = jnp.maximum(2.0 - twice, 1e-30)
        rows = slice(first + at, first + at + 16)
        feature_ref[rows, :] = (sine * (left * lax.rsqrt(left))).astype(BF16)
        rows = slice(first + half + at, first + half + at + 16)
        feature_ref[rows, :] = (1.0 - twice).astype(BF16)


def main_kernel(
    dims, stages, parts, meta_ref, me_ref, slots_ref, rows_ref, colour_grad_ref, small_ref, *refs
):
    part_refs = refs[:parts]
    rendered_ref, head_grad_ref, hidden_ref, raw_ref, weight_ref, slab_ref, sems = refs[parts:]
    regions, rays, crossings, samples, tiles = dims
    width = GROUP * samples
    halves, lanes = raw_ref.shape[0], raw_ref.shape[2]
    used = meta_ref[1, 0]
    me = me_ref[0]
    rounds = (used + (UNROLL - 1)) // UNROLL
    units = hidden_ref.shape[0] // tiles
    depth = slab_ref.shape[1] // UNROLL
    held = regions // parts

    copies = [
        pltpu.make_async_copy(part_refs[p], weight_ref.at[p * held : (p + 1) * held], sems.at[p])
        for p in range(parts)
    ]
    for copy in copies:
        copy.start()

    def phases(tile):
        return phases_of(tile, depth // 2, meta_ref, rows_ref, small_ref)

    ahead = phases(0)
    for index in range(UNROLL):
        turns = ahead
        if index + 1 < UNROLL:
            ahead = phases(index + 1)
        store_features(turns, slab_ref.at[0], index * depth)
    for copy in copies:
        copy.wait()

    def work(step, more):
        first = step * UNROLL
        slot = lax.rem(step, 2)

        def layer(index):
            weights = weight_ref[place(meta_ref[0, first + index] ^ me, stages)]
            return dot(weights, slab_ref[slot, index * depth : (index + 1) * depth, :])

        ahead = layer(0)
        turns_ahead = phases(first + UNROLL) if more else None
        for index in range(UNROLL):
            result, turns = ahead, turns_ahead
            if index + 1 < UNROLL:
                ahead = layer(index + 1)
                turns_ahead = phases(first + UNROLL + index + 1) if more else None
            head(jnp.maximum(first - UNROLL, 0) + index)
            if more:
                store_features(turns, slab_ref.at[1 - slot], index * depth)
            hidden_ref[tile_rows(first + index, units), :] = jnp.maximum(result.astype(BF16), 0)

    def forward(step, _):
        work(step, True)
        return 0

    def head(tile):
        raw = dot(small_ref[meta_ref[0, tile]], hidden_ref[tile_rows(tile, units), :])
        for half in range(halves):
            raw_ref[half, tile_rows(tile, 8), :] = raw[:, half * lanes : (half + 1) * lanes]

    lax.fori_loop(0, rounds - 1, forward, 0)
    work(rounds - 1, False)
    for index in range(UNROLL):
        head((rounds - 1) * UNROLL + index)

    valid = iota((tiles, width), 0) < used
    raw = [
        jnp.where(valid, joined(raw_ref, pl.ds(c, tiles, stride=8)), 0.0) for c in range(4)
    ]
    spacing = joined(rows_ref, pl.ds(7, tiles, stride=8))
    decay = jnp.exp(-jnp.abs(raw[0]))
    density = jnp.maximum(raw[0], 0.0) + jnp.log1p(decay)
    slope = jnp.where(raw[0] >= 0, 1.0, decay) / (1.0 + decay)
    colour = [1.0 / (1.0 + jnp.exp(-raw[c])) for c in (1, 2, 3)]
    optical = density * spacing
    lane_a, lane_b = iota((width, width), 0), iota((width, width), 1)
    same = (lane_a // samples) == (lane_b // samples)
    up_to = ones_where(same & (lane_a <= lane_b))
    after = ones_where(same & (lane_a > lane_b))

    def by_pieces(value, matrix):
        return functools.reduce(jnp.add, [dot(p.astype(BF16), matrix) for p in pieces(value, 2)])

    running = by_pieces(optical, up_to)
    passed = jnp.exp(-running)
    weight = jnp.exp(optical - running) * (1.0 - jnp.exp(-optical))
    weighted = [weight * one for one in colour]

    member = ones_where(iota((GROUP, width), 0) == iota((GROUP, width), 1) // samples)
    sums = []
    for value in weighted + [optical]:
        sums.append(functools.reduce(jnp.add, [dot_nt(member, p.astype(BF16)) for p in pieces(value, 2)]))
    segments = rays * crossings
    slot_row = jnp.concatenate([slots_ref[k : k + 1, :] for k in range(crossings)], axis=1)
    tile_row = jnp.floor(slot_row * (1.0 / GROUP))
    place_row = slot_row - GROUP * tile_row
    lists = ones_where(iota((tiles, segments), 0).astype(F32) == tile_row)
    mine = iota((GROUP, segments), 0).astype(F32) == place_row
    in_tile = folded(dot(stacked(jnp.concatenate(sums, axis=0), 0, 2), lists), 2)
    by_ray = [
        jnp.sum(jnp.where(mine, in_tile[c * GROUP : (c + 1) * GROUP], 0.0), axis=0, keepdims=True)
        for c in range(4)
    ]
    seg_colour = jnp.concatenate(by_ray[:3], axis=0)
    seg_trans = jnp.exp(-by_ray[3])

    upstream = colour_grad_ref[...]
    colours = [seg_colour[:, k * rays : (k + 1) * rays] for k in range(crossings)]
    transes = [seg_trans[:, k * rays : (k + 1) * rays] for k in range(crossings)]
    before = jnp.ones((1, rays), F32)
    befores = []
    rendered = jnp.zeros_like(upstream)
    for k in range(crossings):
        befores.append(before)
        rendered = rendered + before * colours[k]
        before = before * transes[k]
    rendered_ref[...] = rendered
    behind = jnp.zeros_like(upstream)
    grads = [None] * crossings
    for k in range(crossings - 1, -1, -1):
        grad_trans = befores[k] * jnp.sum(upstream * behind, axis=0, keepdims=True)
        grads[k] = jnp.concatenate([befores[k] * upstream, grad_trans * transes[k]], axis=0)
        behind = colours[k] + transes[k] * behind
    grads = jnp.concatenate(grads, axis=1)

    placed = jnp.concatenate([jnp.where(mine, grads[c : c + 1], 0.0) for c in range(4)], axis=0)
    in_slots = dot_nt(lists, stacked(placed, 0, 2)).astype(BF16)
    channel_rows = iota((8 * GROUP, width), 0) % (4 * GROUP)
    lane_place = iota((8 * GROUP, width), 1) // samples
    per_sample = [
        dot(in_slots, ones_where(channel_rows == c * GROUP + lane_place)) for c in range(4)
    ]
    inner = functools.reduce(jnp.add, [per_sample[c] * colour[c] for c in range(3)])
    later = by_pieces(weight * inner, after)
    grad_optical = passed * inner - later - per_sample[3]
    raw_grad = [grad_optical * spacing * slope]
    for c in range(3):
        raw_grad.append(per_sample[c] * weighted[c] * (1.0 - colour[c]))
    for c in range(4):
        for half in range(halves):
            at = pl.ds(c, tiles, stride=8)
            raw_ref[half, at, :] = raw_grad[c][:, half * lanes : (half + 1) * lanes]

    head_grad_ref[...] = jnp.zeros(head_grad_ref.shape, F32)

    def backward(step, _):
        first = step * UNROLL
        products = []
        for index in range(UNROLL):
            gradient = joined(raw_ref, tile_rows(first + index, 8)).astype(BF16)
            products.append(dot_nt(gradient, hidden_ref[tile_rows(first + index, units), :])[:4])
        for index in range(UNROLL):
            head_grad_ref[meta_ref[0, first + index]] += products[index]
        return 0

    lax.fori_loop(0, rounds, backward, 0)


def exchange_stages(count):
    stages = []
    while count > 1:
        size = 4 if count % 4 == 0 and count > 4 else min(count, 4)
        size = 2 if count == 2 else size
        count //= size
        stages.append((count, size))
    return stages


def place(offset, stages):
    at, scale = 0, 1
    for unit, size in stages:
        at = at + ((offset // unit) % size) * scale
        scale = scale * size
    return at


def share(block, stage, count):
    unit, size = stage
    held = [block]
    for other in range(1, size):
        pairs = [(i, i ^ (unit * other)) for i in range(count)]
        held.append(lax.ppermute(block, "region", pairs))
    return held


def on_device(sample_points, sample_spacing, crossed, colour_grad, freq, w_hidden, w_head):
    regions = lax.axis_size("region")
    rays, crossings = crossed.shape
    samples = sample_spacing.shape[1] // crossings
    segments = rays * crossings
    tiles = (segments + (GROUP - 1) * regions) // GROUP
    tiles = -(-tiles // UNROLL) * UNROLL
    width, lanes = GROUP * samples, crossings * samples
    halves = width // lanes
    features = w_hidden.shape[1]
    hidden_units = w_hidden.shape[2]
    dims = (regions, rays, crossings, samples, tiles)
    vmem, smem = pltpu.VMEM, pltpu.SMEM
    mib = 1024 * 1024
    limit = 2 * tiles * width * hidden_units + 8 * halves * tiles * 8 * lanes
    limit += 2 * regions * hidden_units * features + 4 * mib
    limit += 2 * 2 * UNROLL * features * width + 4 * mib
    small_limit = 24 * mib
    params = pltpu.CompilerParams(vmem_limit_bytes=limit)

    me = lax.axis_index("region").astype(jnp.int32).reshape(1)
    meta_width = -(-tiles // 128) * 128
    stages = exchange_stages(regions)
    all_samples = jnp.concatenate([sample_points.transpose(1, 0, 2), sample_spacing[None]], axis=0)
    weights = share(w_hidden[0].T[None], stages[0], regions)
    slots, meta, rows = pl.pallas_call(
        functools.partial(order_kernel, dims),
        out_shape=(
            jax.ShapeDtypeStruct((crossings, rays), F32),
            jax.ShapeDtypeStruct((2, meta_width), jnp.int32),
            jax.ShapeDtypeStruct((halves, tiles * 8, lanes), F32),
        ),
        in_specs=[pl.BlockSpec(memory_space=vmem)] * 2,
        out_specs=[pl.BlockSpec(memory_space=vmem)] * 3,
        compiler_params=pltpu.CompilerParams(vmem_limit_bytes=small_limit),
        cost_estimate=pl.CostEstimate(flops=4 * 10**9, bytes_accessed=10**7, transcendentals=0),
        name="order",
    )(all_samples, crossed.T)

    small = jnp.pad(freq[0], ((0, 1), (0, hidden_units - freq.shape[2])))
    small = jnp.concatenate([w_head[0], small], axis=0)
    small = jnp.broadcast_to(small[None], (regions, 8, hidden_units))
    block, small = lax.optimization_barrier((jnp.concatenate(weights, axis=0), small))
    weights = share(block, stages[1], regions)
    for stage in stages[2:-1]:
        weights = share(jnp.concatenate(weights, axis=0), stage, regions)
    own = share(weights[0], stages[-1], regions)
    own[-1], small = lax.optimization_barrier((own[-1], small))
    all_small = lax.all_to_all(small, "region", split_axis=0, concat_axis=0, tiled=True)
    all_small, *others = lax.optimization_barrier((all_small, *weights[1:]))
    swapped = [own] + [share(block, stages[-1], regions) for block in others]
    weights = [blocks[i] for i in range(stages[-1][1]) for blocks in swapped]

    whole = pl.BlockSpec(memory_space=vmem)

    rendered, head_grad = pl.pallas_call(
        functools.partial(main_kernel, dims, stages, len(weights)),
        out_shape=(
            jax.ShapeDtypeStruct((3, rays), F32),
            jax.ShapeDtypeStruct((regions, 4, hidden_units), F32),
        ),
        in_specs=[pl.BlockSpec(memory_space=smem)] * 2
        + [whole] * 4
        + [pl.BlockSpec(memory_space=pl.ANY)] * len(weights),
        out_specs=[whole] * 2,
        scratch_shapes=[
            pltpu.VMEM((tiles * hidden_units, width), BF16),
            pltpu.VMEM((halves, tiles * 8, lanes), F32),
            pltpu.VMEM((regions, hidden_units, features), BF16),
            pltpu.VMEM((2, UNROLL * features, width), BF16),
            pltpu.SemaphoreType.DMA((len(weights),)),
        ],
        compiler_params=params,
        cost_estimate=pl.CostEstimate(flops=2 * 10**10, bytes_accessed=3 * 10**7, transcendentals=0),
        name="render",
    )(meta, me, slots, rows, colour_grad, all_small, *weights)

    partial_sums = lax.all_to_all(head_grad, "region", split_axis=0, concat_axis=0, tiled=True)
    head_grad = jnp.sum(partial_sums, axis=0, keepdims=True)
    return (rendered, head_grad)


def solution(mesh):
    return jax.shard_map(
        on_device,
        mesh=mesh,
        in_specs=(
            P("region", None, None),
            P("region", None),
            P("region", None),
            P(None, "region"),
            P("region", None, None),
            P("region", None, None),
            P("region", None, None),
        ),
        out_specs=(P(None, "region"), P("region", None, None)),
        check_vma=False,
    )
```

```python
import functools
import jax
import jax.numpy as jnp
from jax import lax
from jax.experimental import pallas as pl
from jax.experimental.pallas import tpu as pltpu
from jax.sharding import PartitionSpec as P

F32 = jnp.float32
BF16 = jnp.bfloat16
GROUP = 8
UNROLL = 16
SIN_HALF = (4.44288292, -7.3082457, 3.60635441, -0.84611289, 0.10982699)
TURN = 0.15915494309189535
ROUNDER = 12582912.0


def pieces(value, count):
    parts = []
    for _ in range(count - 1):
        parts.append(value.astype(BF16).astype(F32))
        value = value - parts[-1]
    return parts + [value]


def stacked(value, axis, count):
    return jnp.concatenate(pieces(value, count), axis=axis).astype(BF16)


def folded(value, count):
    rows = value.shape[0] // count
    return functools.reduce(jnp.add, [value[i * rows : (i + 1) * rows] for i in range(count)])


def dot(a, b):
    return lax.dot_general(a, b, (((1,), (0,)), ((), ())), preferred_element_type=F32)


def dot_nt(a, b):
    return lax.dot_general(a, b, (((1,), (1,)), ((), ())), preferred_element_type=F32)


def iota(shape, axis):
    return lax.broadcasted_iota(jnp.int32, shape, axis)


def joined(ref, at):
    return jnp.concatenate([ref[half, at, :] for half in range(ref.shape[0])], axis=1)


def ones_where(condition):
    return jnp.where(condition, 1.0, 0.0).astype(BF16)


def order_kernel(dims, samples_ref, crossed_ref, slots_ref, meta_ref, rows_ref):
    regions, rays, crossings, samples, tiles = dims
    lanes = crossings * samples
    width = meta_ref.shape[1]
    region_at = iota((regions, rays), 0)
    named = [jnp.where(crossed_ref[k : k + 1, :] == region_at, 1.0, 0.0) for k in range(crossings)]
    listed = functools.reduce(jnp.add, named)
    earlier = ones_where(iota((rays, rays), 0) < iota((rays, rays), 1))
    rank = dot(listed.astype(BF16), earlier)
    count = jnp.sum(listed, axis=1, keepdims=True)
    tile_count = jnp.floor((count + (GROUP - 1)) * (1.0 / GROUP))
    below = ones_where(iota((regions, regions), 1) < iota((regions, regions), 0))
    tile_count = jnp.broadcast_to(tile_count, (regions, width))
    start = dot(below, tile_count.astype(BF16))
    slot = GROUP * start[:, :1] + rank
    slot_rows = [jnp.sum(one * slot, axis=0, keepdims=True) for one in named]
    slots_ref[...] = jnp.concatenate(slot_rows, axis=0)
    ended = jnp.where(start + tile_count <= iota((regions, width), 1).astype(F32), 1.0, 0.0)
    owner = jnp.minimum(jnp.sum(ended, axis=0, keepdims=True), regions - 1.0)
    used = jnp.sum(tile_count, axis=0, keepdims=True)
    meta_ref[...] = jnp.concatenate([owner, used], axis=0).astype(jnp.int32)

    slot_row = jnp.concatenate(slot_rows, axis=1)
    parts = [samples_ref[d] * TURN for d in range(3)] + [samples_ref[3]]
    lane_group = iota((rays, lanes), 1) // samples
    by_segment = []
    for k in range(crossings):
        row = jnp.zeros((rays, lanes), F32)
        for d in range(4):
            moved = pltpu.roll(parts[d], (samples * (d - k)) % lanes, 1) if d != k else parts[d]
            row = jnp.where(lane_group == d, moved, row)
        by_segment.append(row)
    source = stacked(jnp.concatenate(by_segment, axis=0), 1, 3)
    tile_row = jnp.floor(slot_row * (1.0 / GROUP))
    place_row = slot_row - GROUP * tile_row
    in_tile = ones_where(iota((tiles, rays * crossings), 0).astype(F32) == tile_row)
    out_group = iota((tiles, lanes), 1) // samples
    per_row = lanes // samples
    halves = GROUP // per_row
    dense = [[None] * halves for _ in range(4)]
    for s in range(GROUP):
        got = dot(in_tile * ones_where(place_row == s), source)
        got = got[:, :lanes] + got[:, lanes : 2 * lanes] + got[:, 2 * lanes :]
        at, half = s % per_row, s // per_row
        for d in range(4):
            moved = pltpu.roll(got, (samples * (at - d)) % lanes, 1) if d != at else got
            if at == 0:
                dense[d][half] = moved
            else:
                dense[d][half] = jnp.where(out_group == at, moved, dense[d][half])
    rows_ref[...] = jnp.zeros(rows_ref.shape, F32)
    for d in range(4):
        for half in range(halves):
            rows_ref[half, pl.ds(4 + d, tiles, stride=8), :] = dense[d][half]


def tile_rows(tile, height):
    return pl.ds(pl.multiple_of(tile * height, height), height)


def phases_of(tile, half, meta_ref, rows_ref, small_ref):
    small = small_ref[meta_ref[0, tile]][:, :128].astype(F32)
    freq = jnp.concatenate([small] * 3, axis=0).T[:half].astype(BF16)
    return dot(freq, stacked(joined(rows_ref, tile_rows(tile, 8)), 0, 3))


def store_features(turns, feature_ref, first):
    half = turns.shape[0]
    for at in range(0, half, 16):
        part = turns[at : at + 16]
        rest = part - ((part + ROUNDER) - ROUNDER)
        square = rest * rest
        sine = jnp.full_like(square, SIN_HALF[-1])
        for c in SIN_HALF[-2::-1]:
            sine = sine * square + c
        sine = sine * rest
        twice = sine * sine
        left = jnp.maximum(2.0 - twice, 1e-30)
        rows = slice(first + at, first + at + 16)
        feature_ref[rows, :] = (sine * (left * lax.rsqrt(left))).astype(BF16)
        rows = slice(first + half + at, first + half + at + 16)
        feature_ref[rows, :] = (1.0 - twice).astype(BF16)


def main_kernel(
    dims,
    stages,
    parts,
    moves,
    meta_ref,
    me_ref,
    slots_ref,
    rows_ref,
    colour_grad_ref,
    small_ref,
    *refs,
):
    part_refs = refs[:parts]
    rendered_ref, head_grad_ref, hidden_ref, raw_ref, weight_ref, slab_ref, sems = refs[parts:]
    regions, rays, crossings, samples, tiles = dims
    width = GROUP * samples
    halves, lanes = raw_ref.shape[0], raw_ref.shape[2]
    used = meta_ref[1, 0]
    me = me_ref[0]
    rounds = (used + (UNROLL - 1)) // UNROLL
    units = hidden_ref.shape[0] // tiles
    depth = slab_ref.shape[1] // UNROLL

    copies = []
    for at, (part, row, to, count) in enumerate(moves):
        source = part_refs[part].at[row : row + count]
        copies.append(pltpu.make_async_copy(source, weight_ref.at[to : to + count], sems.at[at]))
    for copy in copies:
        copy.start()

    def phases(tile):
        return phases_of(tile, depth // 2, meta_ref, rows_ref, small_ref)

    ahead = phases(0)
    for index in range(UNROLL):
        turns = ahead
        if index + 1 < UNROLL:
            ahead = phases(index + 1)
        store_features(turns, slab_ref.at[0], index * depth)
    for copy in copies:
        copy.wait()

    def work(step, more):
        first = step * UNROLL
        slot = lax.rem(step, 2)

        def layer(index):
            weights = weight_ref[place(meta_ref[0, first + index] ^ me, stages)]
            return dot(weights, slab_ref[slot, index * depth : (index + 1) * depth, :])

        ahead = layer(0)
        turns_ahead = phases(first + UNROLL) if more else None
        for index in range(UNROLL):
            result, turns = ahead, turns_ahead
            if index + 1 < UNROLL:
                ahead = layer(index + 1)
                turns_ahead = phases(first + UNROLL + index + 1) if more else None
            head(jnp.maximum(first - UNROLL, 0) + index)
            if more:
                store_features(turns, slab_ref.at[1 - slot], index * depth)
            hidden_ref[tile_rows(first + index, units), :] = jnp.maximum(result.astype(BF16), 0)

    def forward(step, _):
        work(step, True)
        return 0

    def head(tile):
        raw = dot(small_ref[meta_ref[0, tile]], hidden_ref[tile_rows(tile, units), :])
        for half in range(halves):
            raw_ref[half, tile_rows(tile, 8), :] = raw[:, half * lanes : (half + 1) * lanes]

    lax.fori_loop(0, rounds - 1, forward, 0)
    work(rounds - 1, False)
    for index in range(UNROLL):
        head((rounds - 1) * UNROLL + index)

    valid = iota((tiles, width), 0) < used
    raw = [
        jnp.where(valid, joined(raw_ref, pl.ds(c, tiles, stride=8)), 0.0) for c in range(4)
    ]
    spacing = joined(rows_ref, pl.ds(7, tiles, stride=8))
    decay = jnp.exp(-jnp.abs(raw[0]))
    density = jnp.maximum(raw[0], 0.0) + jnp.log1p(decay)
    slope = jnp.where(raw[0] >= 0, 1.0, decay) / (1.0 + decay)
    colour = [1.0 / (1.0 + jnp.exp(-raw[c])) for c in (1, 2, 3)]
    optical = density * spacing
    lane_a, lane_b = iota((width, width), 0), iota((width, width), 1)
    same = (lane_a // samples) == (lane_b // samples)
    up_to = ones_where(same & (lane_a <= lane_b))
    after = ones_where(same & (lane_a > lane_b))

    def by_pieces(value, matrix):
        return functools.reduce(jnp.add, [dot(p.astype(BF16), matrix) for p in pieces(value, 2)])

    running = by_pieces(optical, up_to)
    passed = jnp.exp(-running)
    weight = jnp.exp(optical - running) * (1.0 - jnp.exp(-optical))
    weighted = [weight * one for one in colour]

    member = ones_where(iota((GROUP, width), 0) == iota((GROUP, width), 1) // samples)
    sums = []
    for value in weighted + [optical]:
        sums.append(functools.reduce(jnp.add, [dot_nt(member, p.astype(BF16)) for p in pieces(value, 2)]))
    segments = rays * crossings
    slot_row = jnp.concatenate([slots_ref[k : k + 1, :] for k in range(crossings)], axis=1)
    tile_row = jnp.floor(slot_row * (1.0 / GROUP))
    place_row = slot_row - GROUP * tile_row
    lists = ones_where(iota((tiles, segments), 0).astype(F32) == tile_row)
    mine = iota((GROUP, segments), 0).astype(F32) == place_row
    in_tile = folded(dot(stacked(jnp.concatenate(sums, axis=0), 0, 2), lists), 2)
    by_ray = [
        jnp.sum(jnp.where(mine, in_tile[c * GROUP : (c + 1) * GROUP], 0.0), axis=0, keepdims=True)
        for c in range(4)
    ]
    seg_colour = jnp.concatenate(by_ray[:3], axis=0)
    seg_trans = jnp.exp(-by_ray[3])

    upstream = colour_grad_ref[...]
    colours = [seg_colour[:, k * rays : (k + 1) * rays] for k in range(crossings)]
    transes = [seg_trans[:, k * rays : (k + 1) * rays] for k in range(crossings)]
    before = jnp.ones((1, rays), F32)
    befores = []
    rendered = jnp.zeros_like(upstream)
    for k in range(crossings):
        befores.append(before)
        rendered = rendered + before * colours[k]
        before = before * transes[k]
    rendered_ref[...] = rendered
    behind = jnp.zeros_like(upstream)
    grads = [None] * crossings
    for k in range(crossings - 1, -1, -1):
        grad_trans = befores[k] * jnp.sum(upstream * behind, axis=0, keepdims=True)
        grads[k] = jnp.concatenate([befores[k] * upstream, grad_trans * transes[k]], axis=0)
        behind = colours[k] + transes[k] * behind
    grads = jnp.concatenate(grads, axis=1)

    placed = jnp.concatenate([jnp.where(mine, grads[c : c + 1], 0.0) for c in range(4)], axis=0)
    in_slots = dot_nt(lists, stacked(placed, 0, 2)).astype(BF16)
    channel_rows = iota((8 * GROUP, width), 0) % (4 * GROUP)
    lane_place = iota((8 * GROUP, width), 1) // samples
    per_sample = [
        dot(in_slots, ones_where(channel_rows == c * GROUP + lane_place)) for c in range(4)
    ]
    inner = functools.reduce(jnp.add, [per_sample[c] * colour[c] for c in range(3)])
    later = by_pieces(weight * inner, after)
    grad_optical = passed * inner - later - per_sample[3]
    raw_grad = [grad_optical * spacing * slope]
    for c in range(3):
        raw_grad.append(per_sample[c] * weighted[c] * (1.0 - colour[c]))
    for c in range(4):
        for half in range(halves):
            at = pl.ds(c, tiles, stride=8)
            raw_ref[half, at, :] = raw_grad[c][:, half * lanes : (half + 1) * lanes]

    head_grad_ref[...] = jnp.zeros(head_grad_ref.shape, F32)

    def backward(step, _):
        first = step * UNROLL
        products = []
        for index in range(UNROLL):
            gradient = joined(raw_ref, tile_rows(first + index, 8)).astype(BF16)
            products.append(dot_nt(gradient, hidden_ref[tile_rows(first + index, units), :])[:4])
        for index in range(UNROLL):
            head_grad_ref[meta_ref[0, first + index]] += products[index]
        return 0

    lax.fori_loop(0, rounds, backward, 0)


def exchange_stages(count):
    stages = []
    while count > 1:
        size = 4 if count % 4 == 0 and count > 4 else min(count, 4)
        size = 2 if count == 2 else size
        count //= size
        stages.append((count, size))
    return stages


def place(offset, stages):
    at, scale = 0, 1
    for unit, size in stages:
        at = at + ((offset // unit) % size) * scale
        scale = scale * size
    return at


def share(block, stage, count):
    unit, size = stage
    held = [block]
    for other in range(1, size):
        pairs = [(i, i ^ (unit * other)) for i in range(count)]
        held.append(lax.ppermute(block, "region", pairs))
    return held


def on_device(sample_points, sample_spacing, crossed, colour_grad, freq, w_hidden, w_head):
    regions = lax.axis_size("region")
    rays, crossings = crossed.shape
    samples = sample_spacing.shape[1] // crossings
    segments = rays * crossings
    tiles = (segments + (GROUP - 1) * regions) // GROUP
    tiles = -(-tiles // UNROLL) * UNROLL
    width, lanes = GROUP * samples, crossings * samples
    halves = width // lanes
    features = w_hidden.shape[1]
    hidden_units = w_hidden.shape[2]
    dims = (regions, rays, crossings, samples, tiles)
    vmem, smem = pltpu.VMEM, pltpu.SMEM
    mib = 1024 * 1024
    limit = 2 * tiles * width * hidden_units + 8 * halves * tiles * 8 * lanes
    limit += 2 * regions * hidden_units * features + 4 * mib
    limit += 2 * 2 * UNROLL * features * width + 4 * mib
    small_limit = 24 * mib
    params = pltpu.CompilerParams(vmem_limit_bytes=limit)

    me = lax.axis_index("region").astype(jnp.int32).reshape(1)
    meta_width = -(-tiles // 128) * 128
    stages = exchange_stages(regions)
    all_samples = jnp.concatenate([sample_points.transpose(1, 0, 2), sample_spacing[None]], axis=0)
    own = w_hidden[0].T[None]
    first = share(own, stages[0], regions)
    own_second = share(own, stages[1], regions)
    slots, meta, rows = pl.pallas_call(
        functools.partial(order_kernel, dims),
        out_shape=(
            jax.ShapeDtypeStruct((crossings, rays), F32),
            jax.ShapeDtypeStruct((2, meta_width), jnp.int32),
            jax.ShapeDtypeStruct((halves, tiles * 8, lanes), F32),
        ),
        in_specs=[pl.BlockSpec(memory_space=vmem)] * 2,
        out_specs=[pl.BlockSpec(memory_space=vmem)] * 3,
        compiler_params=pltpu.CompilerParams(vmem_limit_bytes=small_limit),
        cost_estimate=pl.CostEstimate(flops=4 * 10**9, bytes_accessed=10**7, transcendentals=0),
        name="order",
    )(all_samples, crossed.T)

    small = jnp.pad(freq[0], ((0, 1), (0, hidden_units - freq.shape[2])))
    small = jnp.concatenate([w_head[0], small], axis=0)
    small = jnp.broadcast_to(small[None], (regions, 8, hidden_units))
    others = jnp.concatenate(first[1:], axis=0)
    second = share(others, stages[1], regions)
    parts = [block for pair in zip(own_second, second) for block in pair]
    last = stages[-1]
    if len(stages) > 3:
        parts = [jnp.concatenate(parts, axis=0)]
        for stage in stages[2:-1]:
            parts = share(jnp.concatenate(parts, axis=0), stage, regions)
        groups = [[i] for i in range(len(parts))]
    else:
        groups = [[0, 1], [2, 4, 6], [3], [5], [7]]
    held = [part.shape[0] for part in parts]
    places = [sum(held[:i]) for i in range(len(parts))]

    def swap(group):
        return share(jnp.concatenate([parts[i] for i in group], axis=0), last, regions)[1:]

    swapped = [swap(groups[0])]
    swapped[0][0], small = lax.optimization_barrier((swapped[0][0], small))
    all_small = lax.all_to_all(small, "region", split_axis=0, concat_axis=0, tiled=True)
    late = sorted(i for group in groups[2:] for i in group)
    all_small, *tied = lax.optimization_barrier((all_small, *[parts[i] for i in late]))
    for i, part in zip(late, tied):
        parts[i] = part
    swapped += [swap(group) for group in groups[1:]]
    weights, moves = list(parts), [(i, 0, places[i], held[i]) for i in range(len(parts))]
    for blocks, group in zip(swapped, groups):
        for other, block in enumerate(blocks, 1):
            row = 0
            for i in group:
                moves.append((len(weights), row, other * sum(held) + places[i], held[i]))
                row += held[i]
            weights.append(block)

    whole = pl.BlockSpec(memory_space=vmem)

    rendered, head_grad = pl.pallas_call(
        functools.partial(main_kernel, dims, stages, len(weights), moves),
        out_shape=(
            jax.ShapeDtypeStruct((3, rays), F32),
            jax.ShapeDtypeStruct((regions, 4, hidden_units), F32),
        ),
        in_specs=[pl.BlockSpec(memory_space=smem)] * 2
        + [whole] * 4
        + [pl.BlockSpec(memory_space=pl.ANY)] * len(weights),
        out_specs=[whole] * 2,
        scratch_shapes=[
            pltpu.VMEM((tiles * hidden_units, width), BF16),
            pltpu.VMEM((halves, tiles * 8, lanes), F32),
            pltpu.VMEM((regions, hidden_units, features), BF16),
            pltpu.VMEM((2, UNROLL * features, width), BF16),
            pltpu.SemaphoreType.DMA((len(moves),)),
        ],
        compiler_params=params,
        cost_estimate=pl.CostEstimate(flops=2 * 10**10, bytes_accessed=3 * 10**7, transcendentals=0),
        name="render",
    )(meta, me, slots, rows, colour_grad, all_small, *weights)

    partial_sums = lax.all_to_all(head_grad, "region", split_axis=0, concat_axis=0, tiled=True)
    head_grad = jnp.sum(partial_sums, axis=0, keepdims=True)
    return (rendered, head_grad)


def solution(mesh):
    return jax.shard_map(
        on_device,
        mesh=mesh,
        in_specs=(
            P("region", None, None),
            P("region", None),
            P("region", None),
            P(None, "region"),
            P("region", None, None),
            P("region", None, None),
            P("region", None, None),
        ),
        out_specs=(P(None, "region"), P("region", None, None)),
        check_vma=False,
    )
```

```python
import functools
import jax
import jax.numpy as jnp
from jax import lax
from jax.experimental import pallas as pl
from jax.experimental.pallas import tpu as pltpu
from jax.sharding import PartitionSpec as P

F32 = jnp.float32
BF16 = jnp.bfloat16
GROUP = 8
UNROLL = 16
SIN_HALF = (4.44288292, -7.3082457, 3.60635441, -0.84611289, 0.10982699)
TURN = 0.15915494309189535
ROUNDER = 12582912.0


def pieces(value, count):
    parts = []
    for _ in range(count - 1):
        parts.append(value.astype(BF16).astype(F32))
        value = value - parts[-1]
    return parts + [value]


def stacked(value, axis, count):
    return jnp.concatenate(pieces(value, count), axis=axis).astype(BF16)


def folded(value, count):
    rows = value.shape[0] // count
    return functools.reduce(jnp.add, [value[i * rows : (i + 1) * rows] for i in range(count)])


def dot(a, b):
    return lax.dot_general(a, b, (((1,), (0,)), ((), ())), preferred_element_type=F32)


def dot_nt(a, b):
    return lax.dot_general(a, b, (((1,), (1,)), ((), ())), preferred_element_type=F32)


def iota(shape, axis):
    return lax.broadcasted_iota(jnp.int32, shape, axis)


def joined(ref, at):
    return jnp.concatenate([ref[half, at, :] for half in range(ref.shape[0])], axis=1)


def ones_where(condition):
    return jnp.where(condition, 1.0, 0.0).astype(BF16)


def order_kernel(dims, samples_ref, crossed_ref, slots_ref, meta_ref, rows_ref):
    regions, rays, crossings, samples, tiles = dims
    lanes = crossings * samples
    width = meta_ref.shape[1]
    region_at = iota((regions, rays), 0)
    named = [jnp.where(crossed_ref[k : k + 1, :] == region_at, 1.0, 0.0) for k in range(crossings)]
    listed = functools.reduce(jnp.add, named)
    earlier = ones_where(iota((rays, rays), 0) < iota((rays, rays), 1))
    rank = dot(listed.astype(BF16), earlier)
    count = jnp.sum(listed, axis=1, keepdims=True)
    tile_count = jnp.floor((count + (GROUP - 1)) * (1.0 / GROUP))
    below = ones_where(iota((regions, regions), 1) < iota((regions, regions), 0))
    tile_count = jnp.broadcast_to(tile_count, (regions, width))
    start = dot(below, tile_count.astype(BF16))
    slot = GROUP * start[:, :1] + rank
    slot_rows = [jnp.sum(one * slot, axis=0, keepdims=True) for one in named]
    slots_ref[...] = jnp.concatenate(slot_rows, axis=0)
    ended = jnp.where(start + tile_count <= iota((regions, width), 1).astype(F32), 1.0, 0.0)
    owner = jnp.minimum(jnp.sum(ended, axis=0, keepdims=True), regions - 1.0)
    used = jnp.sum(tile_count, axis=0, keepdims=True)
    meta_ref[...] = jnp.concatenate([owner, used], axis=0).astype(jnp.int32)

    slot_row = jnp.concatenate(slot_rows, axis=1)
    parts = [samples_ref[d] * TURN for d in range(3)] + [samples_ref[3]]
    lane_group = iota((rays, lanes), 1) // samples
    by_segment = []
    for k in range(crossings):
        row = jnp.zeros((rays, lanes), F32)
        for d in range(4):
            moved = pltpu.roll(parts[d], (samples * (d - k)) % lanes, 1) if d != k else parts[d]
            row = jnp.where(lane_group == d, moved, row)
        by_segment.append(row)
    source = stacked(jnp.concatenate(by_segment, axis=0), 1, 3)
    tile_row = jnp.floor(slot_row * (1.0 / GROUP))
    place_row = slot_row - GROUP * tile_row
    in_tile = ones_where(iota((tiles, rays * crossings), 0).astype(F32) == tile_row)
    out_group = iota((tiles, lanes), 1) // samples
    per_row = lanes // samples
    halves = GROUP // per_row
    dense = [[None] * halves for _ in range(4)]
    for s in range(GROUP):
        got = dot(in_tile * ones_where(place_row == s), source)
        got = got[:, :lanes] + got[:, lanes : 2 * lanes] + got[:, 2 * lanes :]
        at, half = s % per_row, s // per_row
        for d in range(4):
            moved = pltpu.roll(got, (samples * (at - d)) % lanes, 1) if d != at else got
            if at == 0:
                dense[d][half] = moved
            else:
                dense[d][half] = jnp.where(out_group == at, moved, dense[d][half])
    rows_ref[...] = jnp.zeros(rows_ref.shape, F32)
    for d in range(4):
        for half in range(halves):
            rows_ref[half, pl.ds(4 + d, tiles, stride=8), :] = dense[d][half]


def tile_rows(tile, height):
    return pl.ds(pl.multiple_of(tile * height, height), height)


def phases_of(tile, half, meta_ref, rows_ref, small_ref):
    small = small_ref[meta_ref[0, tile]][:, :128].astype(F32)
    freq = jnp.concatenate([small] * 3, axis=0).T[:half].astype(BF16)
    return dot(freq, stacked(joined(rows_ref, tile_rows(tile, 8)), 0, 3))


def store_features(turns, feature_ref, first):
    half = turns.shape[0]
    for at in range(0, half, 16):
        part = turns[at : at + 16]
        rest = part - ((part + ROUNDER) - ROUNDER)
        square = rest * rest
        sine = jnp.full_like(square, SIN_HALF[-1])
        for c in SIN_HALF[-2::-1]:
            sine = sine * square + c
        sine = sine * rest
        twice = sine * sine
        left = jnp.maximum(2.0 - twice, 1e-30)
        rows = slice(first + at, first + at + 16)
        feature_ref[rows, :] = (sine * (left * lax.rsqrt(left))).astype(BF16)
        rows = slice(first + half + at, first + half + at + 16)
        feature_ref[rows, :] = (1.0 - twice).astype(BF16)


def main_kernel(
    dims,
    stages,
    meta_ref,
    me_ref,
    slots_ref,
    rows_ref,
    colour_grad_ref,
    small_ref,
    near_ref,
    far_ref,
    rendered_ref,
    head_grad_ref,
    hidden_ref,
    raw_ref,
    slab_ref,
):
    regions, rays, crossings, samples, tiles = dims
    width = GROUP * samples
    halves, lanes = raw_ref.shape[0], raw_ref.shape[2]
    used = meta_ref[1, 0]
    me = me_ref[0]
    rounds = (used + (UNROLL - 1)) // UNROLL
    units = hidden_ref.shape[0] // tiles
    depth = slab_ref.shape[1] // UNROLL

    def phases(tile):
        return phases_of(tile, depth // 2, meta_ref, rows_ref, small_ref)

    ahead = phases(0)
    for index in range(UNROLL):
        turns = ahead
        if index + 1 < UNROLL:
            ahead = phases(index + 1)
        store_features(turns, slab_ref.at[0], index * depth)

    def weights_of(region):
        at = place(region ^ me, stages)
        held = near_ref.shape[0]
        is_near = at < held
        at = jnp.where(is_near, at, at - held)
        return jnp.where(is_near, near_ref[at], far_ref[at])

    def work(step, more):
        first = step * UNROLL
        slot = lax.rem(step, 2)

        def layer(index):
            return dot(weights_of(meta_ref[0, first + index]), slab_ref[slot, index * depth : (index + 1) * depth, :])

        ahead = layer(0)
        turns_ahead = phases(first + UNROLL) if more else None
        for index in range(UNROLL):
            result, turns = ahead, turns_ahead
            if index + 1 < UNROLL:
                ahead = layer(index + 1)
                turns_ahead = phases(first + UNROLL + index + 1) if more else None
            head(jnp.maximum(first - UNROLL, 0) + index)
            if more:
                store_features(turns, slab_ref.at[1 - slot], index * depth)
            hidden_ref[tile_rows(first + index, units), :] = jnp.maximum(result.astype(BF16), 0)

    def forward(step, _):
        work(step, True)
        return 0

    def head(tile):
        raw = dot(small_ref[meta_ref[0, tile]], hidden_ref[tile_rows(tile, units), :])
        for half in range(halves):
            raw_ref[half, tile_rows(tile, 8), :] = raw[:, half * lanes : (half + 1) * lanes]

    lax.fori_loop(0, rounds - 1, forward, 0)
    work(rounds - 1, False)
    for index in range(UNROLL):
        head((rounds - 1) * UNROLL + index)

    valid = iota((tiles, width), 0) < used
    raw = [
        jnp.where(valid, joined(raw_ref, pl.ds(c, tiles, stride=8)), 0.0) for c in range(4)
    ]
    spacing = joined(rows_ref, pl.ds(7, tiles, stride=8))
    decay = jnp.exp(-jnp.abs(raw[0]))
    density = jnp.maximum(raw[0], 0.0) + jnp.log1p(decay)
    slope = jnp.where(raw[0] >= 0, 1.0, decay) / (1.0 + decay)
    colour = [1.0 / (1.0 + jnp.exp(-raw[c])) for c in (1, 2, 3)]
    optical = density * spacing
    lane_a, lane_b = iota((width, width), 0), iota((width, width), 1)
    same = (lane_a // samples) == (lane_b // samples)
    up_to = ones_where(same & (lane_a <= lane_b))
    after = ones_where(same & (lane_a > lane_b))

    def by_pieces(value, matrix):
        return functools.reduce(jnp.add, [dot(p.astype(BF16), matrix) for p in pieces(value, 2)])

    running = by_pieces(optical, up_to)
    passed = jnp.exp(-running)
    weight = jnp.exp(optical - running) * (1.0 - jnp.exp(-optical))
    weighted = [weight * one for one in colour]

    member = ones_where(iota((GROUP, width), 0) == iota((GROUP, width), 1) // samples)
    sums = []
    for value in weighted + [optical]:
        sums.append(functools.reduce(jnp.add, [dot_nt(member, p.astype(BF16)) for p in pieces(value, 2)]))
    segments = rays * crossings
    slot_row = jnp.concatenate([slots_ref[k : k + 1, :] for k in range(crossings)], axis=1)
    tile_row = jnp.floor(slot_row * (1.0 / GROUP))
    place_row = slot_row - GROUP * tile_row
    lists = ones_where(iota((tiles, segments), 0).astype(F32) == tile_row)
    mine = iota((GROUP, segments), 0).astype(F32) == place_row
    in_tile = folded(dot(stacked(jnp.concatenate(sums, axis=0), 0, 2), lists), 2)
    by_ray = [
        jnp.sum(jnp.where(mine, in_tile[c * GROUP : (c + 1) * GROUP], 0.0), axis=0, keepdims=True)
        for c in range(4)
    ]
    seg_colour = jnp.concatenate(by_ray[:3], axis=0)
    seg_trans = jnp.exp(-by_ray[3])

    upstream = colour_grad_ref[...]
    colours = [seg_colour[:, k * rays : (k + 1) * rays] for k in range(crossings)]
    transes = [seg_trans[:, k * rays : (k + 1) * rays] for k in range(crossings)]
    before = jnp.ones((1, rays), F32)
    befores = []
    rendered = jnp.zeros_like(upstream)
    for k in range(crossings):
        befores.append(before)
        rendered = rendered + before * colours[k]
        before = before * transes[k]
    rendered_ref[...] = rendered
    behind = jnp.zeros_like(upstream)
    grads = [None] * crossings
    for k in range(crossings - 1, -1, -1):
        grad_trans = befores[k] * jnp.sum(upstream * behind, axis=0, keepdims=True)
        grads[k] = jnp.concatenate([befores[k] * upstream, grad_trans * transes[k]], axis=0)
        behind = colours[k] + transes[k] * behind
    grads = jnp.concatenate(grads, axis=1)

    placed = jnp.concatenate([jnp.where(mine, grads[c : c + 1], 0.0) for c in range(4)], axis=0)
    in_slots = dot_nt(lists, stacked(placed, 0, 2)).astype(BF16)
    channel_rows = iota((8 * GROUP, width), 0) % (4 * GROUP)
    lane_place = iota((8 * GROUP, width), 1) // samples
    per_sample = [
        dot(in_slots, ones_where(channel_rows == c * GROUP + lane_place)) for c in range(4)
    ]
    inner = functools.reduce(jnp.add, [per_sample[c] * colour[c] for c in range(3)])
    later = by_pieces(weight * inner, after)
    grad_optical = passed * inner - later - per_sample[3]
    raw_grad = [grad_optical * spacing * slope]
    for c in range(3):
        raw_grad.append(per_sample[c] * weighted[c] * (1.0 - colour[c]))
    for c in range(4):
        for half in range(halves):
            at = pl.ds(c, tiles, stride=8)
            raw_ref[half, at, :] = raw_grad[c][:, half * lanes : (half + 1) * lanes]

    head_grad_ref[...] = jnp.zeros(head_grad_ref.shape, F32)

    def backward(step, _):
        first = step * UNROLL
        products = []
        for index in range(UNROLL):
            gradient = joined(raw_ref, tile_rows(first + index, 8)).astype(BF16)
            products.append(dot_nt(gradient, hidden_ref[tile_rows(first + index, units), :])[:4])
        for index in range(UNROLL):
            head_grad_ref[meta_ref[0, first + index]] += products[index]
        return 0

    lax.fori_loop(0, rounds, backward, 0)


def exchange_stages(count):
    stages = []
    while count > 1:
        size = 4 if count % 4 == 0 and count > 4 else min(count, 4)
        size = 2 if count == 2 else size
        count //= size
        stages.append((count, size))
    return stages


def place(offset, stages):
    a, b = [(offset // unit) % size for unit, size in stages[:2]]
    at = jnp.where(b == 0, a, jnp.where(a == 0, 3 + b, 3 + 3 * b + a))
    scale = 16
    for unit, size in stages[2:]:
        at = at + ((offset // unit) % size) * scale
        scale = scale * size
    return at


def share(block, stage, count):
    unit, size = stage
    held = [block]
    for other in range(1, size):
        pairs = [(i, i ^ (unit * other)) for i in range(count)]
        held.append(lax.ppermute(block, "region", pairs))
    return held


def on_device(sample_points, sample_spacing, crossed, colour_grad, freq, w_hidden, w_head):
    regions = lax.axis_size("region")
    rays, crossings = crossed.shape
    samples = sample_spacing.shape[1] // crossings
    segments = rays * crossings
    tiles = (segments + (GROUP - 1) * regions) // GROUP
    tiles = -(-tiles // UNROLL) * UNROLL
    width, lanes = GROUP * samples, crossings * samples
    halves = width // lanes
    features = w_hidden.shape[1]
    hidden_units = w_hidden.shape[2]
    dims = (regions, rays, crossings, samples, tiles)
    vmem, smem = pltpu.VMEM, pltpu.SMEM
    mib = 1024 * 1024
    limit = 2 * tiles * width * hidden_units + 8 * halves * tiles * 8 * lanes
    limit += 2 * regions * hidden_units * features + 4 * mib
    limit += 2 * 2 * UNROLL * features * width + 4 * mib
    small_limit = 24 * mib
    params = pltpu.CompilerParams(vmem_limit_bytes=limit)

    me = lax.axis_index("region").astype(jnp.int32).reshape(1)
    meta_width = -(-tiles // 128) * 128
    stages = exchange_stages(regions)
    all_samples = jnp.concatenate([sample_points.transpose(1, 0, 2), sample_spacing[None]], axis=0)
    own = w_hidden[0].T[None]
    first = share(own, stages[0], regions)
    own_second = share(own, stages[1], regions)
    small = jnp.pad(freq[0], ((0, 1), (0, hidden_units - freq.shape[2])))
    small = jnp.concatenate([w_head[0], small], axis=0)
    small = jnp.broadcast_to(small[None], (regions, 8, hidden_units))
    others, small, listed = lax.optimization_barrier(
        (jnp.concatenate(first[1:], axis=0), small, crossed.T)
    )
    second = share(others, stages[1], regions)
    second[1], small = lax.optimization_barrier((second[1], small))
    all_small = lax.all_to_all(small, "region", split_axis=0, concat_axis=0, tiled=True)
    all_small, *second[2:] = lax.optimization_barrier((all_small, *second[2:]))
    near = jnp.concatenate([own, others, *own_second[1:], *second[1:]], axis=0)
    for stage in stages[2:-1]:
        near = jnp.concatenate(share(near, stage, regions), axis=0)
    near, far = share(near, stages[-1], regions)

    slots, meta, rows = pl.pallas_call(
        functools.partial(order_kernel, dims),
        out_shape=(
            jax.ShapeDtypeStruct((crossings, rays), F32),
            jax.ShapeDtypeStruct((2, meta_width), jnp.int32),
            jax.ShapeDtypeStruct((halves, tiles * 8, lanes), F32),
        ),
        in_specs=[pl.BlockSpec(memory_space=vmem)] * 2,
        out_specs=[pl.BlockSpec(memory_space=vmem)] * 3,
        compiler_params=pltpu.CompilerParams(vmem_limit_bytes=small_limit),
        cost_estimate=pl.CostEstimate(flops=4 * 10**9, bytes_accessed=10**7, transcendentals=0),
        name="order",
    )(all_samples, listed)

    whole = pl.BlockSpec(memory_space=vmem)

    rendered, head_grad = pl.pallas_call(
        functools.partial(main_kernel, dims, stages),
        out_shape=(
            jax.ShapeDtypeStruct((3, rays), F32),
            jax.ShapeDtypeStruct((regions, 4, hidden_units), F32),
        ),
        in_specs=[pl.BlockSpec(memory_space=smem)] * 2
        + [whole] * 6,
        out_specs=[whole] * 2,
        scratch_shapes=[
            pltpu.VMEM((tiles * hidden_units, width), BF16),
            pltpu.VMEM((halves, tiles * 8, lanes), F32),
            pltpu.VMEM((2, UNROLL * features, width), BF16),
        ],
        compiler_params=params,
        cost_estimate=pl.CostEstimate(flops=2 * 10**10, bytes_accessed=3 * 10**7, transcendentals=0),
        name="render",
    )(meta, me, slots, rows, colour_grad, all_small, near, far)

    partial_sums = lax.all_to_all(head_grad, "region", split_axis=0, concat_axis=0, tiled=True)
    head_grad = jnp.sum(partial_sums, axis=0, keepdims=True)
    return (rendered, head_grad)


def solution(mesh):
    return jax.shard_map(
        on_device,
        mesh=mesh,
        in_specs=(
            P("region", None, None),
            P("region", None),
            P("region", None),
            P(None, "region"),
            P("region", None, None),
            P("region", None, None),
            P("region", None, None),
        ),
        out_specs=(P(None, "region"), P("region", None, None)),
        check_vma=False,
    )
```

```python
import functools
import jax
import jax.numpy as jnp
from jax import lax
from jax.experimental import pallas as pl
from jax.experimental.pallas import tpu as pltpu
from jax.sharding import PartitionSpec as P

F32 = jnp.float32
BF16 = jnp.bfloat16
GROUP = 8
UNROLL = 16
SIN_HALF = (4.44288292, -7.3082457, 3.60635441, -0.84611289, 0.10982699)
TURN = 0.15915494309189535
ROUNDER = 12582912.0


def pieces(value, count):
    parts = []
    for _ in range(count - 1):
        parts.append(value.astype(BF16).astype(F32))
        value = value - parts[-1]
    return parts + [value]


def stacked(value, axis, count):
    return jnp.concatenate(pieces(value, count), axis=axis).astype(BF16)


def folded(value, count):
    rows = value.shape[0] // count
    return functools.reduce(jnp.add, [value[i * rows : (i + 1) * rows] for i in range(count)])


def dot(a, b):
    return lax.dot_general(a, b, (((1,), (0,)), ((), ())), preferred_element_type=F32)


def dot_nt(a, b):
    return lax.dot_general(a, b, (((1,), (1,)), ((), ())), preferred_element_type=F32)


def iota(shape, axis):
    return lax.broadcasted_iota(jnp.int32, shape, axis)


def joined(ref, at):
    return jnp.concatenate([ref[half, at, :] for half in range(ref.shape[0])], axis=1)


def ones_where(condition):
    return jnp.where(condition, 1.0, 0.0).astype(BF16)


def order_kernel(dims, samples_ref, crossed_ref, slots_ref, meta_ref, rows_ref):
    regions, rays, crossings, samples, tiles = dims
    lanes = crossings * samples
    width = meta_ref.shape[1]
    region_at = iota((regions, rays), 0)
    named = [jnp.where(crossed_ref[k : k + 1, :] == region_at, 1.0, 0.0) for k in range(crossings)]
    listed = functools.reduce(jnp.add, named)
    earlier = ones_where(iota((rays, rays), 0) < iota((rays, rays), 1))
    rank = dot(listed.astype(BF16), earlier)
    count = jnp.sum(listed, axis=1, keepdims=True)
    tile_count = jnp.floor((count + (GROUP - 1)) * (1.0 / GROUP))
    below = ones_where(iota((regions, regions), 1) < iota((regions, regions), 0))
    tile_count = jnp.broadcast_to(tile_count, (regions, width))
    start = dot(below, tile_count.astype(BF16))
    slot = GROUP * start[:, :1] + rank
    slot_rows = [jnp.sum(one * slot, axis=0, keepdims=True) for one in named]
    slots_ref[...] = jnp.concatenate(slot_rows, axis=0)
    ended = jnp.where(start + tile_count <= iota((regions, width), 1).astype(F32), 1.0, 0.0)
    owner = jnp.minimum(jnp.sum(ended, axis=0, keepdims=True), regions - 1.0)
    used = jnp.sum(tile_count, axis=0, keepdims=True)
    meta_ref[...] = jnp.concatenate([owner, used], axis=0).astype(jnp.int32)

    slot_row = jnp.concatenate(slot_rows, axis=1)
    parts = [samples_ref[d] * TURN for d in range(3)] + [samples_ref[3]]
    lane_group = iota((rays, lanes), 1) // samples
    by_segment = []
    for k in range(crossings):
        row = jnp.zeros((rays, lanes), F32)
        for d in range(4):
            moved = pltpu.roll(parts[d], (samples * (d - k)) % lanes, 1) if d != k else parts[d]
            row = jnp.where(lane_group == d, moved, row)
        by_segment.append(row)
    source = stacked(jnp.concatenate(by_segment, axis=0), 1, 3)
    tile_row = jnp.floor(slot_row * (1.0 / GROUP))
    place_row = slot_row - GROUP * tile_row
    in_tile = ones_where(iota((tiles, rays * crossings), 0).astype(F32) == tile_row)
    out_group = iota((tiles, lanes), 1) // samples
    per_row = lanes // samples
    halves = GROUP // per_row
    dense = [[None] * halves for _ in range(4)]
    for s in range(GROUP):
        got = dot(in_tile * ones_where(place_row == s), source)
        got = got[:, :lanes] + got[:, lanes : 2 * lanes] + got[:, 2 * lanes :]
        at, half = s % per_row, s // per_row
        for d in range(4):
            moved = pltpu.roll(got, (samples * (at - d)) % lanes, 1) if d != at else got
            if at == 0:
                dense[d][half] = moved
            else:
                dense[d][half] = jnp.where(out_group == at, moved, dense[d][half])
    rows_ref[...] = jnp.zeros(rows_ref.shape, F32)
    for d in range(4):
        for half in range(halves):
            rows_ref[half, pl.ds(4 + d, tiles, stride=8), :] = dense[d][half]


def tile_rows(tile, height):
    return pl.ds(pl.multiple_of(tile * height, height), height)


def phases_of(tile, half, small, rows_ref):
    freq = jnp.concatenate([small] * 3, axis=0).T[:half].astype(BF16)
    return dot(freq, stacked(joined(rows_ref, tile_rows(tile, 8)), 0, 3))


def store_features(turns, feature_ref, first):
    half = turns.shape[0]
    for at in range(0, half, 16):
        part = turns[at : at + 16]
        rest = part - ((part + ROUNDER) - ROUNDER)
        square = rest * rest
        sine = jnp.full_like(square, SIN_HALF[-1])
        for c in SIN_HALF[-2::-1]:
            sine = sine * square + c
        sine = sine * rest
        twice = sine * sine
        left = jnp.maximum(2.0 - twice, 1e-30)
        rows = slice(first + at, first + at + 16)
        feature_ref[rows, :] = (sine * (left * lax.rsqrt(left))).astype(BF16)
        rows = slice(first + half + at, first + half + at + 16)
        feature_ref[rows, :] = (1.0 - twice).astype(BF16)


def main_kernel(
    dims,
    stages,
    parts,
    meta_ref,
    me_ref,
    slots_ref,
    rows_ref,
    colour_grad_ref,
    *refs,
):
    part_refs = refs[:parts]
    rendered_ref, head_grad_ref, hidden_ref, raw_ref, weight_ref, slab_ref, sems = refs[parts:]
    regions, rays, crossings, samples, tiles = dims
    width = GROUP * samples
    halves, lanes = raw_ref.shape[0], raw_ref.shape[2]
    used = meta_ref[1, 0]
    me = me_ref[0]
    rounds = (used + (UNROLL - 1)) // UNROLL
    units = hidden_ref.shape[0] // tiles
    depth = slab_ref.shape[1] // UNROLL

    copies, at = [], 0
    for p in range(parts):
        count = part_refs[p].shape[0]
        copies.append(
            pltpu.make_async_copy(part_refs[p], weight_ref.at[at : at + count], sems.at[p])
        )
        at += count
    for copy in copies:
        copy.start()
    for copy in copies:
        copy.wait()

    def at_of(tile):
        return place(meta_ref[0, tile] ^ me, stages)

    def small_of(tile):
        both = weight_ref[at_of(tile), units:, :].astype(F32)
        return both[:8], both[8:]

    def phases(tile):
        return phases_of(tile, depth // 2, small_of(tile)[0], rows_ref)

    ahead = phases(0)
    for index in range(UNROLL):
        turns = ahead
        if index + 1 < UNROLL:
            ahead = phases(index + 1)
        store_features(turns, slab_ref.at[0], index * depth)

    def work(step, more):
        first = step * UNROLL
        slot = lax.rem(step, 2)

        def layer(index):
            weights = weight_ref[at_of(first + index), :units, :]
            return dot(weights, slab_ref[slot, index * depth : (index + 1) * depth, :])

        ahead = layer(0)
        turns_ahead = phases(first + UNROLL) if more else None
        for index in range(UNROLL):
            result, turns = ahead, turns_ahead
            if index + 1 < UNROLL:
                ahead = layer(index + 1)
                turns_ahead = phases(first + UNROLL + index + 1) if more else None
            head(jnp.maximum(first - UNROLL, 0) + index)
            if more:
                store_features(turns, slab_ref.at[1 - slot], index * depth)
            hidden_ref[tile_rows(first + index, units), :] = jnp.maximum(result.astype(BF16), 0)

    def forward(step, _):
        work(step, True)
        return 0

    def head(tile):
        head_w = jnp.concatenate(small_of(tile), axis=1).astype(BF16)
        raw = dot(head_w, hidden_ref[tile_rows(tile, units), :])
        for half in range(halves):
            raw_ref[half, tile_rows(tile, 8), :] = raw[:, half * lanes : (half + 1) * lanes]

    lax.fori_loop(0, rounds - 1, forward, 0)
    work(rounds - 1, False)
    for index in range(UNROLL):
        head((rounds - 1) * UNROLL + index)

    valid = iota((tiles, width), 0) < used
    raw = [
        jnp.where(valid, joined(raw_ref, pl.ds(c, tiles, stride=8)), 0.0) for c in range(4)
    ]
    spacing = joined(rows_ref, pl.ds(7, tiles, stride=8))
    decay = jnp.exp(-jnp.abs(raw[0]))
    density = jnp.maximum(raw[0], 0.0) + jnp.log1p(decay)
    slope = jnp.where(raw[0] >= 0, 1.0, decay) / (1.0 + decay)
    colour = [1.0 / (1.0 + jnp.exp(-raw[c])) for c in (1, 2, 3)]
    optical = density * spacing
    lane_a, lane_b = iota((width, width), 0), iota((width, width), 1)
    same = (lane_a // samples) == (lane_b // samples)
    up_to = ones_where(same & (lane_a <= lane_b))
    after = ones_where(same & (lane_a > lane_b))

    def by_pieces(value, matrix):
        return functools.reduce(jnp.add, [dot(p.astype(BF16), matrix) for p in pieces(value, 2)])

    running = by_pieces(optical, up_to)
    passed = jnp.exp(-running)
    weight = jnp.exp(optical - running) * (1.0 - jnp.exp(-optical))
    weighted = [weight * one for one in colour]

    member = ones_where(iota((GROUP, width), 0) == iota((GROUP, width), 1) // samples)
    sums = []
    for value in weighted + [optical]:
        sums.append(functools.reduce(jnp.add, [dot_nt(member, p.astype(BF16)) for p in pieces(value, 2)]))
    segments = rays * crossings
    slot_row = jnp.concatenate([slots_ref[k : k + 1, :] for k in range(crossings)], axis=1)
    tile_row = jnp.floor(slot_row * (1.0 / GROUP))
    place_row = slot_row - GROUP * tile_row
    lists = ones_where(iota((tiles, segments), 0).astype(F32) == tile_row)
    mine = iota((GROUP, segments), 0).astype(F32) == place_row
    in_tile = folded(dot(stacked(jnp.concatenate(sums, axis=0), 0, 2), lists), 2)
    by_ray = [
        jnp.sum(jnp.where(mine, in_tile[c * GROUP : (c + 1) * GROUP], 0.0), axis=0, keepdims=True)
        for c in range(4)
    ]
    seg_colour = jnp.concatenate(by_ray[:3], axis=0)
    seg_trans = jnp.exp(-by_ray[3])

    upstream = colour_grad_ref[...]
    colours = [seg_colour[:, k * rays : (k + 1) * rays] for k in range(crossings)]
    transes = [seg_trans[:, k * rays : (k + 1) * rays] for k in range(crossings)]
    before = jnp.ones((1, rays), F32)
    befores = []
    rendered = jnp.zeros_like(upstream)
    for k in range(crossings):
        befores.append(before)
        rendered = rendered + before * colours[k]
        before = before * transes[k]
    rendered_ref[...] = rendered
    behind = jnp.zeros_like(upstream)
    grads = [None] * crossings
    for k in range(crossings - 1, -1, -1):
        grad_trans = befores[k] * jnp.sum(upstream * behind, axis=0, keepdims=True)
        grads[k] = jnp.concatenate([befores[k] * upstream, grad_trans * transes[k]], axis=0)
        behind = colours[k] + transes[k] * behind
    grads = jnp.concatenate(grads, axis=1)

    placed = jnp.concatenate([jnp.where(mine, grads[c : c + 1], 0.0) for c in range(4)], axis=0)
    in_slots = dot_nt(lists, stacked(placed, 0, 2)).astype(BF16)
    channel_rows = iota((8 * GROUP, width), 0) % (4 * GROUP)
    lane_place = iota((8 * GROUP, width), 1) // samples
    per_sample = [
        dot(in_slots, ones_where(channel_rows == c * GROUP + lane_place)) for c in range(4)
    ]
    inner = functools.reduce(jnp.add, [per_sample[c] * colour[c] for c in range(3)])
    later = by_pieces(weight * inner, after)
    grad_optical = passed * inner - later - per_sample[3]
    raw_grad = [grad_optical * spacing * slope]
    for c in range(3):
        raw_grad.append(per_sample[c] * weighted[c] * (1.0 - colour[c]))
    for c in range(4):
        for half in range(halves):
            at = pl.ds(c, tiles, stride=8)
            raw_ref[half, at, :] = raw_grad[c][:, half * lanes : (half + 1) * lanes]

    head_grad_ref[...] = jnp.zeros(head_grad_ref.shape, F32)

    def backward(step, _):
        first = step * UNROLL
        products = []
        for index in range(UNROLL):
            gradient = joined(raw_ref, tile_rows(first + index, 8)).astype(BF16)
            products.append(dot_nt(gradient, hidden_ref[tile_rows(first + index, units), :])[:4])
        for index in range(UNROLL):
            head_grad_ref[meta_ref[0, first + index]] += products[index]
        return 0

    lax.fori_loop(0, rounds, backward, 0)


def exchange_stages(count):
    stages = []
    while count > 1:
        size = 4 if count % 4 == 0 and count > 4 else min(count, 4)
        size = 2 if count == 2 else size
        count //= size
        stages.append((count, size))
    return stages


def place(offset, stages):
    a, b = [(offset // unit) % size for unit, size in stages[:2]]
    at = jnp.where(b == 0, a, jnp.where(a == 0, 3 + b, 3 + 3 * b + a))
    scale = 16
    for unit, size in stages[2:]:
        at = at + ((offset // unit) % size) * scale
        scale = scale * size
    return at


def share(block, stage, count):
    unit, size = stage
    held = [block]
    for other in range(1, size):
        pairs = [(i, i ^ (unit * other)) for i in range(count)]
        held.append(lax.ppermute(block, "region", pairs))
    return held


def on_device(sample_points, sample_spacing, crossed, colour_grad, freq, w_hidden, w_head):
    regions = lax.axis_size("region")
    rays, crossings = crossed.shape
    samples = sample_spacing.shape[1] // crossings
    segments = rays * crossings
    tiles = (segments + (GROUP - 1) * regions) // GROUP
    tiles = -(-tiles // UNROLL) * UNROLL
    width, lanes = GROUP * samples, crossings * samples
    halves = width // lanes
    features = w_hidden.shape[1]
    hidden_units = w_hidden.shape[2]
    dims = (regions, rays, crossings, samples, tiles)
    vmem, smem = pltpu.VMEM, pltpu.SMEM
    mib = 1024 * 1024
    limit = 2 * tiles * width * hidden_units + 8 * halves * tiles * 8 * lanes
    limit += 2 * regions * hidden_units * features + 4 * mib
    limit += 2 * 2 * UNROLL * features * width + 4 * mib
    small_limit = 24 * mib
    params = pltpu.CompilerParams(vmem_limit_bytes=limit)

    me = lax.axis_index("region").astype(jnp.int32).reshape(1)
    meta_width = -(-tiles // 128) * 128
    stages = exchange_stages(regions)
    all_samples = jnp.concatenate([sample_points.transpose(1, 0, 2), sample_spacing[None]], axis=0)
    small = jnp.pad(freq[0], ((0, 1), (0, hidden_units - freq.shape[2])))
    small = jnp.concatenate([w_head[0], small], axis=0)
    halves_of_small = [small[:, i : i + features] for i in range(0, hidden_units, features)]
    own = jnp.concatenate([w_hidden[0].T, *halves_of_small], axis=0)[None]
    first = share(own, stages[0], regions)
    own_second = share(own, stages[1], regions)
    others, listed = lax.optimization_barrier((jnp.concatenate(first[1:], axis=0), crossed.T))
    second = share(others, stages[1], regions)
    slots, meta, rows = pl.pallas_call(
        functools.partial(order_kernel, dims),
        out_shape=(
            jax.ShapeDtypeStruct((crossings, rays), F32),
            jax.ShapeDtypeStruct((2, meta_width), jnp.int32),
            jax.ShapeDtypeStruct((halves, tiles * 8, lanes), F32),
        ),
        in_specs=[pl.BlockSpec(memory_space=vmem)] * 2,
        out_specs=[pl.BlockSpec(memory_space=vmem)] * 3,
        compiler_params=pltpu.CompilerParams(vmem_limit_bytes=small_limit),
        cost_estimate=pl.CostEstimate(flops=4 * 10**9, bytes_accessed=10**7, transcendentals=0),
        name="order",
    )(all_samples, listed)

    early = jnp.concatenate([own, others, *own_second[1:]], axis=0)
    if len(stages) > 3:
        near = jnp.concatenate([early, *second[1:]], axis=0)
        for stage in stages[2:-1]:
            near = jnp.concatenate(share(near, stage, regions), axis=0)
        weights = share(near, stages[-1], regions)
    else:
        early, far = share(early, stages[-1], regions)
        far, slots, *second = lax.optimization_barrier((far, slots, *second[1:]))
        late, far_late = share(jnp.concatenate(second, axis=0), stages[-1], regions)
        weights = [early, late, far, far_late]

    whole = pl.BlockSpec(memory_space=vmem)

    rendered, head_grad = pl.pallas_call(
        functools.partial(main_kernel, dims, stages, len(weights)),
        out_shape=(
            jax.ShapeDtypeStruct((3, rays), F32),
            jax.ShapeDtypeStruct((regions, 4, hidden_units), F32),
        ),
        in_specs=[pl.BlockSpec(memory_space=smem)] * 2
        + [whole] * 3
        + [pl.BlockSpec(memory_space=pl.ANY)] * len(weights),
        out_specs=[whole] * 2,
        scratch_shapes=[
            pltpu.VMEM((tiles * hidden_units, width), BF16),
            pltpu.VMEM((halves, tiles * 8, lanes), F32),
            pltpu.VMEM((regions,) + own.shape[1:], BF16),
            pltpu.VMEM((2, UNROLL * features, width), BF16),
            pltpu.SemaphoreType.DMA((len(weights),)),
        ],
        compiler_params=params,
        cost_estimate=pl.CostEstimate(flops=2 * 10**10, bytes_accessed=3 * 10**7, transcendentals=0),
        name="render",
    )(meta, me, slots, rows, colour_grad, *weights)

    partial_sums = lax.all_to_all(head_grad, "region", split_axis=0, concat_axis=0, tiled=True)
    head_grad = jnp.sum(partial_sums, axis=0, keepdims=True)
    return (rendered, head_grad)


def solution(mesh):
    return jax.shard_map(
        on_device,
        mesh=mesh,
        in_specs=(
            P("region", None, None),
            P("region", None),
            P("region", None),
            P(None, "region"),
            P("region", None, None),
            P("region", None, None),
            P("region", None, None),
        ),
        out_specs=(P(None, "region"), P("region", None, None)),
        check_vma=False,
    )
```

```python
import functools
import jax
import jax.numpy as jnp
from jax import lax
from jax.experimental import pallas as pl
from jax.experimental.pallas import tpu as pltpu
from jax.sharding import PartitionSpec as P

F32 = jnp.float32
BF16 = jnp.bfloat16
GROUP = 8
UNROLL = 16
SIN_HALF = (4.44288292, -7.3082457, 3.60635441, -0.84611289, 0.10982699)
TURN = 0.15915494309189535
ROUNDER = 12582912.0


def pieces(value, count):
    parts = []
    for _ in range(count - 1):
        parts.append(value.astype(BF16).astype(F32))
        value = value - parts[-1]
    return parts + [value]


def stacked(value, axis, count):
    return jnp.concatenate(pieces(value, count), axis=axis).astype(BF16)


def folded(value, count):
    rows = value.shape[0] // count
    return functools.reduce(jnp.add, [value[i * rows : (i + 1) * rows] for i in range(count)])


def dot(a, b):
    return lax.dot_general(a, b, (((1,), (0,)), ((), ())), preferred_element_type=F32)


def dot_nt(a, b):
    return lax.dot_general(a, b, (((1,), (1,)), ((), ())), preferred_element_type=F32)


def iota(shape, axis):
    return lax.broadcasted_iota(jnp.int32, shape, axis)


def joined(ref, at):
    return jnp.concatenate([ref[half, at, :] for half in range(ref.shape[0])], axis=1)


def ones_where(condition):
    return jnp.where(condition, 1.0, 0.0).astype(BF16)


def order_kernel(dims, samples_ref, crossed_ref, slots_ref, meta_ref, rows_ref):
    regions, rays, crossings, samples, tiles = dims
    lanes = crossings * samples
    width = meta_ref.shape[1]
    region_at = iota((regions, rays), 0)
    named = [jnp.where(crossed_ref[k : k + 1, :] == region_at, 1.0, 0.0) for k in range(crossings)]
    listed = functools.reduce(jnp.add, named)
    earlier = ones_where(iota((rays, rays), 0) < iota((rays, rays), 1))
    rank = dot(listed.astype(BF16), earlier)
    count = jnp.sum(listed, axis=1, keepdims=True)
    tile_count = jnp.floor((count + (GROUP - 1)) * (1.0 / GROUP))
    below = ones_where(iota((regions, regions), 1) < iota((regions, regions), 0))
    tile_count = jnp.broadcast_to(tile_count, (regions, width))
    start = dot(below, tile_count.astype(BF16))
    slot = GROUP * start[:, :1] + rank
    slot_rows = [jnp.sum(one * slot, axis=0, keepdims=True) for one in named]
    slots_ref[...] = jnp.concatenate(slot_rows, axis=0)
    ended = jnp.where(start + tile_count <= iota((regions, width), 1).astype(F32), 1.0, 0.0)
    owner = jnp.minimum(jnp.sum(ended, axis=0, keepdims=True), regions - 1.0)
    used = jnp.sum(tile_count, axis=0, keepdims=True)
    meta_ref[...] = jnp.concatenate([owner, used], axis=0).astype(jnp.int32)

    slot_row = jnp.concatenate(slot_rows, axis=1)
    parts = [samples_ref[d] * TURN for d in range(3)] + [samples_ref[3]]
    lane_group = iota((rays, lanes), 1) // samples
    by_segment = []
    for k in range(crossings):
        row = jnp.zeros((rays, lanes), F32)
        for d in range(4):
            moved = pltpu.roll(parts[d], (samples * (d - k)) % lanes, 1) if d != k else parts[d]
            row = jnp.where(lane_group == d, moved, row)
        by_segment.append(row)
    source = stacked(jnp.concatenate(by_segment, axis=0), 1, 3)
    tile_row = jnp.floor(slot_row * (1.0 / GROUP))
    place_row = slot_row - GROUP * tile_row
    in_tile = ones_where(iota((tiles, rays * crossings), 0).astype(F32) == tile_row)
    out_group = iota((tiles, lanes), 1) // samples
    per_row = lanes // samples
    halves = GROUP // per_row
    dense = [[None] * halves for _ in range(4)]
    for s in range(GROUP):
        got = dot(in_tile * ones_where(place_row == s), source)
        got = got[:, :lanes] + got[:, lanes : 2 * lanes] + got[:, 2 * lanes :]
        at, half = s % per_row, s // per_row
        for d in range(4):
            moved = pltpu.roll(got, (samples * (at - d)) % lanes, 1) if d != at else got
            if at == 0:
                dense[d][half] = moved
            else:
                dense[d][half] = jnp.where(out_group == at, moved, dense[d][half])
    rows_ref[...] = jnp.zeros(rows_ref.shape, F32)
    for d in range(4):
        for half in range(halves):
            rows_ref[half, pl.ds(4 + d, tiles, stride=8), :] = dense[d][half]


def tile_rows(tile, height):
    return pl.ds(pl.multiple_of(tile * height, height), height)


def store_features(turns, feature_ref, first):
    half = turns.shape[0]
    for at in range(0, half, 16):
        part = turns[at : at + 16]
        rest = part - ((part + ROUNDER) - ROUNDER)
        square = rest * rest
        sine = jnp.full_like(square, SIN_HALF[-1])
        for c in SIN_HALF[-2::-1]:
            sine = sine * square + c
        sine = sine * rest
        twice = sine * sine
        left = jnp.maximum(2.0 - twice, 1e-30)
        rows = slice(first + at, first + at + 16)
        feature_ref[rows, :] = (sine * (left * lax.rsqrt(left))).astype(BF16)
        rows = slice(first + half + at, first + half + at + 16)
        feature_ref[rows, :] = (1.0 - twice).astype(BF16)


def main_kernel(
    dims,
    stages,
    parts,
    meta_ref,
    me_ref,
    slots_ref,
    rows_ref,
    colour_grad_ref,
    *refs,
):
    part_refs = refs[:parts]
    rendered_ref, head_grad_ref, hidden_ref, raw_ref, weight_ref = refs[parts : parts + 5]
    freq_ref, head_ref, slab_ref, sems = refs[parts + 5 :]
    regions, rays, crossings, samples, tiles = dims
    width = GROUP * samples
    halves, lanes = raw_ref.shape[0], raw_ref.shape[2]
    used = meta_ref[1, 0]
    me = me_ref[0]
    rounds = (used + (UNROLL - 1)) // UNROLL
    units = hidden_ref.shape[0] // tiles
    depth = slab_ref.shape[1] // UNROLL

    places = [0]
    for part in part_refs:
        places.append(places[-1] + part.shape[0])
    copies = []
    for p, part in enumerate(part_refs):
        source, target = part.at[:, :units, :], weight_ref.at[places[p] : places[p + 1]]
        copies.append(pltpu.make_async_copy(source, target, sems.at[p]))
    for copy in copies:
        copy.start()

    def table(part, start, index):
        both = part[index, units:, :].astype(F32)
        freq_ref[start + index, :, :24] = jnp.concatenate([both[:8]] * 3, axis=0).T[: depth // 2].astype(BF16)
        head_ref[start + index] = jnp.concatenate([both[:8], both[8:]], axis=1).astype(BF16)

    for start, part in zip(places, part_refs):
        if part.shape[0] <= 16:
            for index in range(part.shape[0]):
                table(part, start, index)
        else:
            lax.fori_loop(0, part.shape[0], lambda i, _: (table(part, start, i), 0)[1], 0)

    def at_of(tile):
        return place(meta_ref[0, tile] ^ me, stages)

    def phases(tile):
        points = stacked(joined(rows_ref, tile_rows(tile, 8)), 0, 3)
        return dot(freq_ref[at_of(tile), :, :24], points)

    ahead = phases(0)
    for index in range(UNROLL):
        turns = ahead
        if index + 1 < UNROLL:
            ahead = phases(index + 1)
        store_features(turns, slab_ref.at[0], index * depth)
    for copy in copies:
        copy.wait()

    def work(step, more):
        first = step * UNROLL
        slot = lax.rem(step, 2)

        def layer(index):
            weights = weight_ref[at_of(first + index)]
            return dot(weights, slab_ref[slot, index * depth : (index + 1) * depth, :])

        ahead = layer(0)
        turns_ahead = phases(first + UNROLL) if more else None
        for index in range(UNROLL):
            result, turns = ahead, turns_ahead
            if index + 1 < UNROLL:
                ahead = layer(index + 1)
                turns_ahead = phases(first + UNROLL + index + 1) if more else None
            head(jnp.maximum(first - UNROLL, 0) + index)
            if more:
                store_features(turns, slab_ref.at[1 - slot], index * depth)
            hidden_ref[tile_rows(first + index, units), :] = jnp.maximum(result.astype(BF16), 0)

    def forward(step, _):
        work(step, True)
        return 0

    def head(tile):
        raw = dot(head_ref[at_of(tile)], hidden_ref[tile_rows(tile, units), :])
        for half in range(halves):
            raw_ref[half, tile_rows(tile, 8), :] = raw[:, half * lanes : (half + 1) * lanes]

    lax.fori_loop(0, rounds - 1, forward, 0)
    work(rounds - 1, False)
    for index in range(UNROLL):
        head((rounds - 1) * UNROLL + index)

    valid = iota((tiles, width), 0) < used
    raw = [
        jnp.where(valid, joined(raw_ref, pl.ds(c, tiles, stride=8)), 0.0) for c in range(4)
    ]
    spacing = joined(rows_ref, pl.ds(7, tiles, stride=8))
    decay = jnp.exp(-jnp.abs(raw[0]))
    density = jnp.maximum(raw[0], 0.0) + jnp.log1p(decay)
    slope = jnp.where(raw[0] >= 0, 1.0, decay) / (1.0 + decay)
    colour = [1.0 / (1.0 + jnp.exp(-raw[c])) for c in (1, 2, 3)]
    optical = density * spacing
    lane_a, lane_b = iota((width, width), 0), iota((width, width), 1)
    same = (lane_a // samples) == (lane_b // samples)
    up_to = ones_where(same & (lane_a <= lane_b))
    after = ones_where(same & (lane_a > lane_b))

    def by_pieces(value, matrix):
        return functools.reduce(jnp.add, [dot(p.astype(BF16), matrix) for p in pieces(value, 2)])

    running = by_pieces(optical, up_to)
    passed = jnp.exp(-running)
    weight = jnp.exp(optical - running) * (1.0 - jnp.exp(-optical))
    weighted = [weight * one for one in colour]

    member = ones_where(iota((GROUP, width), 0) == iota((GROUP, width), 1) // samples)
    sums = []
    for value in weighted + [optical]:
        sums.append(functools.reduce(jnp.add, [dot_nt(member, p.astype(BF16)) for p in pieces(value, 2)]))
    segments = rays * crossings
    slot_row = jnp.concatenate([slots_ref[k : k + 1, :] for k in range(crossings)], axis=1)
    tile_row = jnp.floor(slot_row * (1.0 / GROUP))
    place_row = slot_row - GROUP * tile_row
    lists = ones_where(iota((tiles, segments), 0).astype(F32) == tile_row)
    mine = iota((GROUP, segments), 0).astype(F32) == place_row
    in_tile = folded(dot(stacked(jnp.concatenate(sums, axis=0), 0, 2), lists), 2)
    by_ray = [
        jnp.sum(jnp.where(mine, in_tile[c * GROUP : (c + 1) * GROUP], 0.0), axis=0, keepdims=True)
        for c in range(4)
    ]
    seg_colour = jnp.concatenate(by_ray[:3], axis=0)
    seg_trans = jnp.exp(-by_ray[3])

    upstream = colour_grad_ref[...]
    colours = [seg_colour[:, k * rays : (k + 1) * rays] for k in range(crossings)]
    transes = [seg_trans[:, k * rays : (k + 1) * rays] for k in range(crossings)]
    before = jnp.ones((1, rays), F32)
    befores = []
    rendered = jnp.zeros_like(upstream)
    for k in range(crossings):
        befores.append(before)
        rendered = rendered + before * colours[k]
        before = before * transes[k]
    rendered_ref[...] = rendered
    behind = jnp.zeros_like(upstream)
    grads = [None] * crossings
    for k in range(crossings - 1, -1, -1):
        grad_trans = befores[k] * jnp.sum(upstream * behind, axis=0, keepdims=True)
        grads[k] = jnp.concatenate([befores[k] * upstream, grad_trans * transes[k]], axis=0)
        behind = colours[k] + transes[k] * behind
    grads = jnp.concatenate(grads, axis=1)

    placed = jnp.concatenate([jnp.where(mine, grads[c : c + 1], 0.0) for c in range(4)], axis=0)
    in_slots = dot_nt(lists, stacked(placed, 0, 2)).astype(BF16)
    channel_rows = iota((8 * GROUP, width), 0) % (4 * GROUP)
    lane_place = iota((8 * GROUP, width), 1) // samples
    per_sample = [
        dot(in_slots, ones_where(channel_rows == c * GROUP + lane_place)) for c in range(4)
    ]
    inner = functools.reduce(jnp.add, [per_sample[c] * colour[c] for c in range(3)])
    later = by_pieces(weight * inner, after)
    grad_optical = passed * inner - later - per_sample[3]
    raw_grad = [grad_optical * spacing * slope]
    for c in range(3):
        raw_grad.append(per_sample[c] * weighted[c] * (1.0 - colour[c]))
    for c in range(4):
        for half in range(halves):
            at = pl.ds(c, tiles, stride=8)
            raw_ref[half, at, :] = raw_grad[c][:, half * lanes : (half + 1) * lanes]

    head_grad_ref[...] = jnp.zeros(head_grad_ref.shape, F32)

    def backward(step, _):
        first = step * UNROLL
        products = []
        for index in range(UNROLL):
            gradient = joined(raw_ref, tile_rows(first + index, 8)).astype(BF16)
            products.append(dot_nt(gradient, hidden_ref[tile_rows(first + index, units), :])[:4])
        for index in range(UNROLL):
            head_grad_ref[meta_ref[0, first + index]] += products[index]
        return 0

    lax.fori_loop(0, rounds, backward, 0)


def exchange_stages(count):
    stages = []
    while count > 1:
        size = 4 if count % 4 == 0 and count > 4 else min(count, 4)
        size = 2 if count == 2 else size
        count //= size
        stages.append((count, size))
    return stages


def place(offset, stages):
    a, b = [(offset // unit) % size for unit, size in stages[:2]]
    at = jnp.where(b == 0, a, jnp.where(a == 0, 3 + b, 3 + 3 * b + a))
    scale = 16
    for unit, size in stages[2:]:
        at = at + ((offset // unit) % size) * scale
        scale = scale * size
    return at


def share(block, stage, count):
    unit, size = stage
    held = [block]
    for other in range(1, size):
        pairs = [(i, i ^ (unit * other)) for i in range(count)]
        held.append(lax.ppermute(block, "region", pairs))
    return held


def on_device(sample_points, sample_spacing, crossed, colour_grad, freq, w_hidden, w_head):
    regions = lax.axis_size("region")
    rays, crossings = crossed.shape
    samples = sample_spacing.shape[1] // crossings
    segments = rays * crossings
    tiles = (segments + (GROUP - 1) * regions) // GROUP
    tiles = -(-tiles // UNROLL) * UNROLL
    width, lanes = GROUP * samples, crossings * samples
    halves = width // lanes
    features = w_hidden.shape[1]
    hidden_units = w_hidden.shape[2]
    dims = (regions, rays, crossings, samples, tiles)
    vmem, smem = pltpu.VMEM, pltpu.SMEM
    mib = 1024 * 1024
    limit = 2 * tiles * width * hidden_units + 8 * halves * tiles * 8 * lanes
    limit += 2 * regions * (2 * hidden_units + 16) * features + 4 * mib
    limit += 2 * 2 * UNROLL * features * width + 4 * mib
    small_limit = 24 * mib
    params = pltpu.CompilerParams(vmem_limit_bytes=limit)

    me = lax.axis_index("region").astype(jnp.int32).reshape(1)
    meta_width = -(-tiles // 128) * 128
    stages = exchange_stages(regions)
    all_samples = jnp.concatenate([sample_points.transpose(1, 0, 2), sample_spacing[None]], axis=0)
    small = jnp.pad(freq[0], ((0, 1), (0, hidden_units - freq.shape[2])))
    small = jnp.concatenate([w_head[0], small], axis=0)
    halves_of_small = [small[:, i : i + features] for i in range(0, hidden_units, features)]
    own = jnp.concatenate([w_hidden[0].T, *halves_of_small], axis=0)[None]
    first = share(own, stages[0], regions)
    own_second = share(own, stages[1], regions)
    others, listed = lax.optimization_barrier((jnp.concatenate(first[1:], axis=0), crossed.T))
    second = share(others, stages[1], regions)
    slots, meta, rows = pl.pallas_call(
        functools.partial(order_kernel, dims),
        out_shape=(
            jax.ShapeDtypeStruct((crossings, rays), F32),
            jax.ShapeDtypeStruct((2, meta_width), jnp.int32),
            jax.ShapeDtypeStruct((halves, tiles * 8, lanes), F32),
        ),
        in_specs=[pl.BlockSpec(memory_space=vmem)] * 2,
        out_specs=[pl.BlockSpec(memory_space=vmem)] * 3,
        compiler_params=pltpu.CompilerParams(vmem_limit_bytes=small_limit),
        cost_estimate=pl.CostEstimate(flops=4 * 10**9, bytes_accessed=10**7, transcendentals=0),
        name="order",
    )(all_samples, listed)

    early = jnp.concatenate([own, others, *own_second[1:]], axis=0)
    if len(stages) > 3:
        near = jnp.concatenate([early, *second[1:]], axis=0)
        for stage in stages[2:-1]:
            near = jnp.concatenate(share(near, stage, regions), axis=0)
        weights = share(near, stages[-1], regions)
    else:
        early, far = share(early, stages[-1], regions)
        far, slots, *second = lax.optimization_barrier((far, slots, *second[1:]))
        late, far_late = share(jnp.concatenate(second, axis=0), stages[-1], regions)
        weights = [early, late, far, far_late]

    whole = pl.BlockSpec(memory_space=vmem)

    rendered, head_grad = pl.pallas_call(
        functools.partial(main_kernel, dims, stages, len(weights)),
        out_shape=(
            jax.ShapeDtypeStruct((3, rays), F32),
            jax.ShapeDtypeStruct((regions, 4, hidden_units), F32),
        ),
        in_specs=[pl.BlockSpec(memory_space=smem)] * 2
        + [whole] * (3 + len(weights)),
        out_specs=[whole] * 2,
        scratch_shapes=[
            pltpu.VMEM((tiles * hidden_units, width), BF16),
            pltpu.VMEM((halves, tiles * 8, lanes), F32),
            pltpu.VMEM((regions, hidden_units, features), BF16),
            pltpu.VMEM((regions, features // 2, 128), BF16),
            pltpu.VMEM((regions, 8, hidden_units), BF16),
            pltpu.VMEM((2, UNROLL * features, width), BF16),
            pltpu.SemaphoreType.DMA((len(weights),)),
        ],
        compiler_params=params,
        cost_estimate=pl.CostEstimate(flops=2 * 10**10, bytes_accessed=3 * 10**7, transcendentals=0),
        name="render",
    )(meta, me, slots, rows, colour_grad, *weights)

    partial_sums = lax.all_to_all(head_grad, "region", split_axis=0, concat_axis=0, tiled=True)
    head_grad = jnp.sum(partial_sums, axis=0, keepdims=True)
    return (rendered, head_grad)


def solution(mesh):
    return jax.shard_map(
        on_device,
        mesh=mesh,
        in_specs=(
            P("region", None, None),
            P("region", None),
            P("region", None),
            P(None, "region"),
            P("region", None, None),
            P("region", None, None),
            P("region", None, None),
        ),
        out_specs=(P(None, "region"), P("region", None, None)),
        check_vma=False,
    )
```

```python
import functools
import jax
import jax.numpy as jnp
from jax import lax
from jax.experimental import pallas as pl
from jax.experimental.pallas import tpu as pltpu
from jax.sharding import PartitionSpec as P

F32 = jnp.float32
BF16 = jnp.bfloat16
GROUP = 8
UNROLL = 16
SIN_HALF = (4.44288292, -7.3082457, 3.60635441, -0.84611289, 0.10982699)
TURN = 0.15915494309189535
ROUNDER = 12582912.0


def pieces(value, count):
    parts = []
    for _ in range(count - 1):
        parts.append(value.astype(BF16).astype(F32))
        value = value - parts[-1]
    return parts + [value]


def stacked(value, axis, count):
    return jnp.concatenate(pieces(value, count), axis=axis).astype(BF16)


def folded(value, count):
    rows = value.shape[0] // count
    return functools.reduce(jnp.add, [value[i * rows : (i + 1) * rows] for i in range(count)])


def dot(a, b):
    return lax.dot_general(a, b, (((1,), (0,)), ((), ())), preferred_element_type=F32)


def dot_nt(a, b):
    return lax.dot_general(a, b, (((1,), (1,)), ((), ())), preferred_element_type=F32)


def iota(shape, axis):
    return lax.broadcasted_iota(jnp.int32, shape, axis)


def joined(ref, at):
    return jnp.concatenate([ref[half, at, :] for half in range(ref.shape[0])], axis=1)


def ones_where(condition):
    return jnp.where(condition, 1.0, 0.0).astype(BF16)


def order_kernel(dims, samples_ref, crossed_ref, slots_ref, meta_ref, rows_ref):
    regions, rays, crossings, samples, tiles = dims
    lanes = crossings * samples
    width = meta_ref.shape[1]
    region_at = iota((regions, rays), 0)
    named = [jnp.where(crossed_ref[k : k + 1, :] == region_at, 1.0, 0.0) for k in range(crossings)]
    listed = functools.reduce(jnp.add, named)
    earlier = ones_where(iota((rays, rays), 0) < iota((rays, rays), 1))
    rank = dot(listed.astype(BF16), earlier)
    count = jnp.sum(listed, axis=1, keepdims=True)
    tile_count = jnp.floor((count + (GROUP - 1)) * (1.0 / GROUP))
    below = ones_where(iota((regions, regions), 1) < iota((regions, regions), 0))
    tile_count = jnp.broadcast_to(tile_count, (regions, width))
    start = dot(below, tile_count.astype(BF16))
    slot = GROUP * start[:, :1] + rank
    slot_rows = [jnp.sum(one * slot, axis=0, keepdims=True) for one in named]
    slots_ref[...] = jnp.concatenate(slot_rows, axis=0)
    ended = jnp.where(start + tile_count <= iota((regions, width), 1).astype(F32), 1.0, 0.0)
    owner = jnp.minimum(jnp.sum(ended, axis=0, keepdims=True), regions - 1.0)
    used = jnp.sum(tile_count, axis=0, keepdims=True)
    meta_ref[...] = jnp.concatenate([owner, used], axis=0).astype(jnp.int32)

    slot_row = jnp.concatenate(slot_rows, axis=1)
    parts = [samples_ref[d] * TURN for d in range(3)] + [samples_ref[3]]
    lane_group = iota((rays, lanes), 1) // samples
    by_segment = []
    for k in range(crossings):
        row = jnp.zeros((rays, lanes), F32)
        for d in range(4):
            moved = pltpu.roll(parts[d], (samples * (d - k)) % lanes, 1) if d != k else parts[d]
            row = jnp.where(lane_group == d, moved, row)
        by_segment.append(row)
    source = stacked(jnp.concatenate(by_segment, axis=0), 1, 3)
    tile_row = jnp.floor(slot_row * (1.0 / GROUP))
    place_row = slot_row - GROUP * tile_row
    in_tile = ones_where(iota((tiles, rays * crossings), 0).astype(F32) == tile_row)
    out_group = iota((tiles, lanes), 1) // samples
    per_row = lanes // samples
    halves = GROUP // per_row
    dense = [[None] * halves for _ in range(4)]
    for s in range(GROUP):
        got = dot(in_tile * ones_where(place_row == s), source)
        got = got[:, :lanes] + got[:, lanes : 2 * lanes] + got[:, 2 * lanes :]
        at, half = s % per_row, s // per_row
        for d in range(4):
            moved = pltpu.roll(got, (samples * (at - d)) % lanes, 1) if d != at else got
            if at == 0:
                dense[d][half] = moved
            else:
                dense[d][half] = jnp.where(out_group == at, moved, dense[d][half])
    rows_ref[...] = jnp.zeros(rows_ref.shape, F32)
    for d in range(4):
        for half in range(halves):
            rows_ref[half, pl.ds(4 + d, tiles, stride=8), :] = dense[d][half]


def tile_rows(tile, height):
    return pl.ds(pl.multiple_of(tile * height, height), height)


def store_features(turns, feature_ref, first):
    half = turns.shape[0]
    for at in range(0, half, 16):
        part = turns[at : at + 16]
        rest = part - ((part + ROUNDER) - ROUNDER)
        square = rest * rest
        sine = jnp.full_like(square, SIN_HALF[-1])
        for c in SIN_HALF[-2::-1]:
            sine = sine * square + c
        sine = sine * rest
        twice = sine * sine
        left = jnp.maximum(2.0 - twice, 1e-30)
        rows = slice(first + at, first + at + 16)
        feature_ref[rows, :] = (sine * (left * lax.rsqrt(left))).astype(BF16)
        rows = slice(first + half + at, first + half + at + 16)
        feature_ref[rows, :] = (1.0 - twice).astype(BF16)


def main_kernel(
    dims,
    stages,
    parts,
    meta_ref,
    me_ref,
    slots_ref,
    rows_ref,
    colour_grad_ref,
    *refs,
):
    part_refs = refs[:parts]
    rendered_ref, head_grad_ref, hidden_ref, raw_ref, weight_ref = refs[parts : parts + 5]
    freq_ref, head_ref, slab_ref, sems = refs[parts + 5 :]
    regions, rays, crossings, samples, tiles = dims
    width = GROUP * samples
    halves, lanes = raw_ref.shape[0], raw_ref.shape[2]
    used = meta_ref[1, 0]
    me = me_ref[0]
    rounds = (used + (UNROLL - 1)) // UNROLL
    units = hidden_ref.shape[0] // tiles
    depth = slab_ref.shape[1] // UNROLL

    places = [0]
    for part in part_refs:
        places.append(places[-1] + part.shape[0])
    copies = []
    for p, part in enumerate(part_refs):
        source, target = part.at[:, :units, :], weight_ref.at[places[p] : places[p + 1]]
        copies.append(pltpu.make_async_copy(source, target, sems.at[p]))
    for copy in copies:
        copy.start()

    def table(part, start, index):
        both = part[index, units:, :].astype(F32)
        freq_ref[start + index, :, :24] = jnp.concatenate([both[:8]] * 3, axis=0).T[: depth // 2].astype(BF16)
        head_ref[start + index] = jnp.concatenate([both[:8], both[8:]], axis=1).astype(BF16)

    for start, part in zip(places, part_refs):
        if part.shape[0] <= 16:
            for index in range(part.shape[0]):
                table(part, start, index)
        else:
            lax.fori_loop(0, part.shape[0], lambda i, _: (table(part, start, i), 0)[1], 0)

    def at_of(tile):
        return place(meta_ref[0, tile] ^ me, stages)

    def phases(tile):
        points = stacked(joined(rows_ref, tile_rows(tile, 8)), 0, 3)
        return dot(freq_ref[at_of(tile), :, :24], points)

    ahead = phases(0)
    for index in range(UNROLL):
        turns = ahead
        if index + 1 < UNROLL:
            ahead = phases(index + 1)
        store_features(turns, slab_ref.at[0], index * depth)
    for copy in copies:
        copy.wait()

    def work(step, more):
        first = step * UNROLL
        slot = lax.rem(step, 2)

        def layer(index):
            weights = weight_ref[at_of(first + index)]
            return dot(weights, slab_ref[slot, index * depth : (index + 1) * depth, :])

        ahead = layer(0)
        turns_ahead = phases(first + UNROLL) if more else None
        for index in range(UNROLL):
            result, turns = ahead, turns_ahead
            if index + 1 < UNROLL:
                ahead = layer(index + 1)
                turns_ahead = phases(first + UNROLL + index + 1) if more else None
            head(jnp.maximum(first - UNROLL, 0) + index)
            if more:
                store_features(turns, slab_ref.at[1 - slot], index * depth)
            hidden_ref[tile_rows(first + index, units), :] = jnp.maximum(result.astype(BF16), 0)

    def forward(step, _):
        work(step, True)
        return 0

    def head(tile):
        raw = dot(head_ref[at_of(tile)], hidden_ref[tile_rows(tile, units), :])
        for half in range(halves):
            raw_ref[half, tile_rows(tile, 8), :] = raw[:, half * lanes : (half + 1) * lanes]

    lax.fori_loop(0, rounds - 1, forward, 0)
    work(rounds - 1, False)
    for index in range(UNROLL):
        head((rounds - 1) * UNROLL + index)

    valid = iota((tiles, width), 0) < used
    raw = [
        jnp.where(valid, joined(raw_ref, pl.ds(c, tiles, stride=8)), 0.0) for c in range(4)
    ]
    spacing = joined(rows_ref, pl.ds(7, tiles, stride=8))
    decay = jnp.exp(-jnp.abs(raw[0]))
    density = jnp.maximum(raw[0], 0.0) + jnp.log1p(decay)
    slope = jnp.where(raw[0] >= 0, 1.0, decay) / (1.0 + decay)
    colour = [1.0 / (1.0 + jnp.exp(-raw[c])) for c in (1, 2, 3)]
    optical = density * spacing
    lane_a, lane_b = iota((width, width), 0), iota((width, width), 1)
    same = (lane_a // samples) == (lane_b // samples)
    up_to = ones_where(same & (lane_a <= lane_b))
    after = ones_where(same & (lane_a > lane_b))

    def by_pieces(value, matrix):
        return functools.reduce(jnp.add, [dot(p.astype(BF16), matrix) for p in pieces(value, 2)])

    running = by_pieces(optical, up_to)
    passed = jnp.exp(-running)
    weight = jnp.exp(optical - running) * (1.0 - jnp.exp(-optical))
    weighted = [weight * one for one in colour]

    member = ones_where(iota((GROUP, width), 0) == iota((GROUP, width), 1) // samples)
    sums = []
    for value in weighted + [optical]:
        sums.append(functools.reduce(jnp.add, [dot_nt(member, p.astype(BF16)) for p in pieces(value, 2)]))
    segments = rays * crossings
    slot_row = jnp.concatenate([slots_ref[k : k + 1, :] for k in range(crossings)], axis=1)
    tile_row = jnp.floor(slot_row * (1.0 / GROUP))
    place_row = slot_row - GROUP * tile_row
    lists = ones_where(iota((tiles, segments), 0).astype(F32) == tile_row)
    mine = iota((GROUP, segments), 0).astype(F32) == place_row
    in_tile = folded(dot(stacked(jnp.concatenate(sums, axis=0), 0, 2), lists), 2)
    by_ray = [
        jnp.sum(jnp.where(mine, in_tile[c * GROUP : (c + 1) * GROUP], 0.0), axis=0, keepdims=True)
        for c in range(4)
    ]
    seg_colour = jnp.concatenate(by_ray[:3], axis=0)
    seg_trans = jnp.exp(-by_ray[3])

    upstream = colour_grad_ref[...]
    colours = [seg_colour[:, k * rays : (k + 1) * rays] for k in range(crossings)]
    transes = [seg_trans[:, k * rays : (k + 1) * rays] for k in range(crossings)]
    before = jnp.ones((1, rays), F32)
    befores = []
    rendered = jnp.zeros_like(upstream)
    for k in range(crossings):
        befores.append(before)
        rendered = rendered + before * colours[k]
        before = before * transes[k]
    rendered_ref[...] = rendered
    behind = jnp.zeros_like(upstream)
    grads = [None] * crossings
    for k in range(crossings - 1, -1, -1):
        grad_trans = befores[k] * jnp.sum(upstream * behind, axis=0, keepdims=True)
        grads[k] = jnp.concatenate([befores[k] * upstream, grad_trans * transes[k]], axis=0)
        behind = colours[k] + transes[k] * behind
    grads = jnp.concatenate(grads, axis=1)

    placed = jnp.concatenate([jnp.where(mine, grads[c : c + 1], 0.0) for c in range(4)], axis=0)
    in_slots = dot_nt(lists, stacked(placed, 0, 2)).astype(BF16)
    channel_rows = iota((8 * GROUP, width), 0) % (4 * GROUP)
    lane_place = iota((8 * GROUP, width), 1) // samples
    per_sample = [
        dot(in_slots, ones_where(channel_rows == c * GROUP + lane_place)) for c in range(4)
    ]
    inner = functools.reduce(jnp.add, [per_sample[c] * colour[c] for c in range(3)])
    later = by_pieces(weight * inner, after)
    grad_optical = passed * inner - later - per_sample[3]
    raw_grad = [grad_optical * spacing * slope]
    for c in range(3):
        raw_grad.append(per_sample[c] * weighted[c] * (1.0 - colour[c]))
    for c in range(4):
        for half in range(halves):
            at = pl.ds(c, tiles, stride=8)
            raw_ref[half, at, :] = raw_grad[c][:, half * lanes : (half + 1) * lanes]

    head_grad_ref[...] = jnp.zeros(head_grad_ref.shape, F32)

    def backward(step, _):
        first = step * UNROLL
        products = []
        for index in range(UNROLL):
            gradient = joined(raw_ref, tile_rows(first + index, 8)).astype(BF16)
            products.append(dot_nt(gradient, hidden_ref[tile_rows(first + index, units), :])[:4])
        for index in range(UNROLL):
            head_grad_ref[meta_ref[0, first + index]] += products[index]
        return 0

    lax.fori_loop(0, rounds, backward, 0)


def exchange_stages(count):
    stages = []
    while count > 1:
        size = 4 if count % 4 == 0 and count > 4 else min(count, 4)
        size = 2 if count == 2 else size
        count //= size
        stages.append((count, size))
    return stages


def place(offset, stages):
    a, b = [(offset // unit) % size for unit, size in stages[:2]]
    at = jnp.where(b == 0, a, jnp.where(a == 0, 3 + b, 3 + 3 * b + a))
    scale = 16
    for unit, size in stages[2:]:
        at = at + ((offset // unit) % size) * scale
        scale = scale * size
    return at


def share(block, stage, count):
    unit, size = stage
    held = [block]
    for other in range(1, size):
        pairs = [(i, i ^ (unit * other)) for i in range(count)]
        held.append(lax.ppermute(block, "region", pairs))
    return held


def on_device(sample_points, sample_spacing, crossed, colour_grad, freq, w_hidden, w_head):
    regions = lax.axis_size("region")
    rays, crossings = crossed.shape
    samples = sample_spacing.shape[1] // crossings
    segments = rays * crossings
    tiles = (segments + (GROUP - 1) * regions) // GROUP
    tiles = -(-tiles // UNROLL) * UNROLL
    width, lanes = GROUP * samples, crossings * samples
    halves = width // lanes
    features = w_hidden.shape[1]
    hidden_units = w_hidden.shape[2]
    dims = (regions, rays, crossings, samples, tiles)
    vmem, smem = pltpu.VMEM, pltpu.SMEM
    mib = 1024 * 1024
    limit = 2 * tiles * width * hidden_units + 8 * halves * tiles * 8 * lanes
    limit += 2 * regions * (2 * hidden_units + 16) * features + 4 * mib
    limit += 2 * 2 * UNROLL * features * width + 4 * mib
    small_limit = 24 * mib
    params = pltpu.CompilerParams(vmem_limit_bytes=limit)

    me = lax.axis_index("region").astype(jnp.int32).reshape(1)
    meta_width = -(-tiles // 128) * 128
    stages = exchange_stages(regions)
    all_samples = jnp.concatenate([sample_points.transpose(1, 0, 2), sample_spacing[None]], axis=0)
    small = jnp.pad(freq[0], ((0, 1), (0, hidden_units - freq.shape[2])))
    small = jnp.concatenate([w_head[0], small], axis=0)
    halves_of_small = [small[:, i : i + features] for i in range(0, hidden_units, features)]
    own = jnp.concatenate([w_hidden[0].T, *halves_of_small], axis=0)[None]
    first = share(own, stages[0], regions)
    own_second = share(own, stages[1], regions)
    others, listed = lax.optimization_barrier((jnp.concatenate(first[1:], axis=0), crossed.T))
    second = share(others, stages[1], regions)
    slots, meta, rows = pl.pallas_call(
        functools.partial(order_kernel, dims),
        out_shape=(
            jax.ShapeDtypeStruct((crossings, rays), F32),
            jax.ShapeDtypeStruct((2, meta_width), jnp.int32),
            jax.ShapeDtypeStruct((halves, tiles * 8, lanes), F32),
        ),
        in_specs=[pl.BlockSpec(memory_space=vmem)] * 2,
        out_specs=[pl.BlockSpec(memory_space=vmem)] * 3,
        compiler_params=pltpu.CompilerParams(vmem_limit_bytes=small_limit),
        cost_estimate=pl.CostEstimate(flops=4 * 10**9, bytes_accessed=10**7, transcendentals=0),
        name="order",
    )(all_samples, listed)

    slots, *own_second = lax.optimization_barrier((slots, *own_second[1:]))
    early = jnp.concatenate([own, others, *own_second], axis=0)
    if len(stages) > 3:
        near = jnp.concatenate([early, *second[1:]], axis=0)
        for stage in stages[2:-1]:
            near = jnp.concatenate(share(near, stage, regions), axis=0)
        weights = share(near, stages[-1], regions)
    else:
        early, far = share(early, stages[-1], regions)
        far, second[1] = lax.optimization_barrier((far, second[1]))
        late = [share(block, stages[-1], regions) for block in second[1:]]
        weights = [early] + [block for block, _ in late] + [far] + [block for _, block in late]

    whole = pl.BlockSpec(memory_space=vmem)

    rendered, head_grad = pl.pallas_call(
        functools.partial(main_kernel, dims, stages, len(weights)),
        out_shape=(
            jax.ShapeDtypeStruct((3, rays), F32),
            jax.ShapeDtypeStruct((regions, 4, hidden_units), F32),
        ),
        in_specs=[pl.BlockSpec(memory_space=smem)] * 2
        + [whole] * (3 + len(weights)),
        out_specs=[whole] * 2,
        scratch_shapes=[
            pltpu.VMEM((tiles * hidden_units, width), BF16),
            pltpu.VMEM((halves, tiles * 8, lanes), F32),
            pltpu.VMEM((regions, hidden_units, features), BF16),
            pltpu.VMEM((regions, features // 2, 128), BF16),
            pltpu.VMEM((regions, 8, hidden_units), BF16),
            pltpu.VMEM((2, UNROLL * features, width), BF16),
            pltpu.SemaphoreType.DMA((len(weights),)),
        ],
        compiler_params=params,
        cost_estimate=pl.CostEstimate(flops=2 * 10**10, bytes_accessed=3 * 10**7, transcendentals=0),
        name="render",
    )(meta, me, slots, rows, colour_grad, *weights)

    partial_sums = lax.all_to_all(head_grad, "region", split_axis=0, concat_axis=0, tiled=True)
    head_grad = jnp.sum(partial_sums, axis=0, keepdims=True)
    return (rendered, head_grad)


def solution(mesh):
    return jax.shard_map(
        on_device,
        mesh=mesh,
        in_specs=(
            P("region", None, None),
            P("region", None),
            P("region", None),
            P(None, "region"),
            P("region", None, None),
            P("region", None, None),
            P("region", None, None),
        ),
        out_specs=(P(None, "region"), P("region", None, None)),
        check_vma=False,
    )
```

```python
import functools
import jax
import jax.numpy as jnp
from jax import lax
from jax.experimental import pallas as pl
from jax.experimental.pallas import tpu as pltpu
from jax.sharding import PartitionSpec as P

F32 = jnp.float32
BF16 = jnp.bfloat16
GROUP = 8
UNROLL = 16
SIN_HALF = (4.44288292, -7.3082457, 3.60635441, -0.84611289, 0.10982699)
TURN = 0.15915494309189535
ROUNDER = 12582912.0


def pieces(value, count):
    parts = []
    for _ in range(count - 1):
        parts.append(value.astype(BF16).astype(F32))
        value = value - parts[-1]
    return parts + [value]


def stacked(value, axis, count):
    return jnp.concatenate(pieces(value, count), axis=axis).astype(BF16)


def folded(value, count):
    rows = value.shape[0] // count
    return functools.reduce(jnp.add, [value[i * rows : (i + 1) * rows] for i in range(count)])


def dot(a, b):
    return lax.dot_general(a, b, (((1,), (0,)), ((), ())), preferred_element_type=F32)


def dot_nt(a, b):
    return lax.dot_general(a, b, (((1,), (1,)), ((), ())), preferred_element_type=F32)


def iota(shape, axis):
    return lax.broadcasted_iota(jnp.int32, shape, axis)


def joined(ref, at):
    return jnp.concatenate([ref[half, at, :] for half in range(ref.shape[0])], axis=1)


def ones_where(condition):
    return jnp.where(condition, 1.0, 0.0).astype(BF16)


def order_kernel(dims, samples_ref, crossed_ref, slots_ref, meta_ref, rows_ref):
    regions, rays, crossings, samples, tiles = dims
    lanes = crossings * samples
    width = meta_ref.shape[1]
    region_at = iota((regions, rays), 0)
    named = [jnp.where(crossed_ref[k : k + 1, :] == region_at, 1.0, 0.0) for k in range(crossings)]
    listed = functools.reduce(jnp.add, named)
    earlier = ones_where(iota((rays, rays), 0) < iota((rays, rays), 1))
    rank = dot(listed.astype(BF16), earlier)
    count = jnp.sum(listed, axis=1, keepdims=True)
    tile_count = jnp.floor((count + (GROUP - 1)) * (1.0 / GROUP))
    below = ones_where(iota((regions, regions), 1) < iota((regions, regions), 0))
    tile_count = jnp.broadcast_to(tile_count, (regions, width))
    start = dot(below, tile_count.astype(BF16))
    slot = GROUP * start[:, :1] + rank
    slot_rows = [jnp.sum(one * slot, axis=0, keepdims=True) for one in named]
    slots_ref[...] = jnp.concatenate(slot_rows, axis=0)
    ended = jnp.where(start + tile_count <= iota((regions, width), 1).astype(F32), 1.0, 0.0)
    owner = jnp.minimum(jnp.sum(ended, axis=0, keepdims=True), regions - 1.0)
    used = jnp.sum(tile_count, axis=0, keepdims=True)
    meta_ref[...] = jnp.concatenate([owner, used], axis=0).astype(jnp.int32)

    slot_row = jnp.concatenate(slot_rows, axis=1)
    parts = [samples_ref[d] * TURN for d in range(3)] + [samples_ref[3]]
    lane_group = iota((rays, lanes), 1) // samples
    by_segment = []
    for k in range(crossings):
        row = jnp.zeros((rays, lanes), F32)
        for d in range(4):
            moved = pltpu.roll(parts[d], (samples * (d - k)) % lanes, 1) if d != k else parts[d]
            row = jnp.where(lane_group == d, moved, row)
        by_segment.append(row)
    source = stacked(jnp.concatenate(by_segment, axis=0), 1, 3)
    tile_row = jnp.floor(slot_row * (1.0 / GROUP))
    place_row = slot_row - GROUP * tile_row
    in_tile = ones_where(iota((tiles, rays * crossings), 0).astype(F32) == tile_row)
    out_group = iota((tiles, lanes), 1) // samples
    per_row = lanes // samples
    halves = GROUP // per_row
    dense = [[None] * halves for _ in range(4)]
    for s in range(GROUP):
        got = dot(in_tile * ones_where(place_row == s), source)
        got = got[:, :lanes] + got[:, lanes : 2 * lanes] + got[:, 2 * lanes :]
        at, half = s % per_row, s // per_row
        for d in range(4):
            moved = pltpu.roll(got, (samples * (at - d)) % lanes, 1) if d != at else got
            if at == 0:
                dense[d][half] = moved
            else:
                dense[d][half] = jnp.where(out_group == at, moved, dense[d][half])
    rows_ref[...] = jnp.zeros(rows_ref.shape, F32)
    for d in range(4):
        for half in range(halves):
            rows_ref[half, pl.ds(4 + d, tiles, stride=8), :] = dense[d][half]


def tile_rows(tile, height):
    return pl.ds(pl.multiple_of(tile * height, height), height)


def store_features(turns, feature_ref, first):
    half = turns.shape[0]
    for at in range(0, half, 16):
        part = turns[at : at + 16]
        rest = part - ((part + ROUNDER) - ROUNDER)
        square = rest * rest
        sine = jnp.full_like(square, SIN_HALF[-1])
        for c in SIN_HALF[-2::-1]:
            sine = sine * square + c
        sine = sine * rest
        twice = sine * sine
        left = jnp.maximum(2.0 - twice, 1e-30)
        rows = slice(first + at, first + at + 16)
        feature_ref[rows, :] = (sine * (left * lax.rsqrt(left))).astype(BF16)
        rows = slice(first + half + at, first + half + at + 16)
        feature_ref[rows, :] = (1.0 - twice).astype(BF16)


def main_kernel(
    dims,
    stages,
    parts,
    meta_ref,
    me_ref,
    slots_ref,
    rows_ref,
    colour_grad_ref,
    *refs,
):
    part_refs = refs[:parts]
    rendered_ref, head_grad_ref, hidden_ref, raw_ref, weight_ref = refs[parts : parts + 5]
    freq_ref, head_ref, slab_ref, sems = refs[parts + 5 :]
    regions, rays, crossings, samples, tiles = dims
    width = GROUP * samples
    halves, lanes = raw_ref.shape[0], raw_ref.shape[2]
    used = meta_ref[1, 0]
    me = me_ref[0]
    rounds = (used + (UNROLL - 1)) // UNROLL
    units = hidden_ref.shape[0] // tiles
    depth = slab_ref.shape[1] // UNROLL

    places = [0]
    for part in part_refs:
        places.append(places[-1] + part.shape[0])
    copies = []
    for p, part in enumerate(part_refs):
        source, target = part.at[:, :units, :], weight_ref.at[places[p] : places[p + 1]]
        copies.append(pltpu.make_async_copy(source, target, sems.at[p]))
    for copy in copies:
        copy.start()

    def table(part, start, index):
        both = part[index, units:, :].astype(F32)
        freq_ref[start + index, :, :24] = jnp.concatenate([both[:8]] * 3, axis=0).T[: depth // 2].astype(BF16)
        head_ref[start + index] = jnp.concatenate([both[:8], both[8:]], axis=1).astype(BF16)

    for start, part in zip(places, part_refs):
        if part.shape[0] <= 16:
            for index in range(part.shape[0]):
                table(part, start, index)
        else:
            lax.fori_loop(0, part.shape[0], lambda i, _: (table(part, start, i), 0)[1], 0)

    def at_of(tile):
        return place(meta_ref[0, tile] ^ me, stages)

    def phases(tile):
        points = stacked(joined(rows_ref, tile_rows(tile, 8)), 0, 3)
        return dot(freq_ref[at_of(tile), :, :24], points)

    ahead = phases(0)
    for index in range(UNROLL):
        turns = ahead
        if index + 1 < UNROLL:
            ahead = phases(index + 1)
        store_features(turns, slab_ref.at[0], index * depth)
    for copy in copies:
        copy.wait()

    def work(step, more):
        first = step * UNROLL
        slot = lax.rem(step, 2)

        def layer(index):
            weights = weight_ref[at_of(first + index)]
            return dot(weights, slab_ref[slot, index * depth : (index + 1) * depth, :])

        ahead = layer(0)
        turns_ahead = phases(first + UNROLL) if more else None
        for index in range(UNROLL):
            result, turns = ahead, turns_ahead
            if index + 1 < UNROLL:
                ahead = layer(index + 1)
                turns_ahead = phases(first + UNROLL + index + 1) if more else None
            head(jnp.maximum(first - UNROLL, 0) + index)
            if more:
                store_features(turns, slab_ref.at[1 - slot], index * depth)
            hidden_ref[tile_rows(first + index, units), :] = jnp.maximum(result.astype(BF16), 0)

    def forward(step, _):
        work(step, True)
        return 0

    def head(tile):
        raw = dot(head_ref[at_of(tile)], hidden_ref[tile_rows(tile, units), :])
        for half in range(halves):
            raw_ref[half, tile_rows(tile, 8), :] = raw[:, half * lanes : (half + 1) * lanes]

    lax.fori_loop(0, rounds - 1, forward, 0)
    work(rounds - 1, False)
    for index in range(UNROLL):
        head((rounds - 1) * UNROLL + index)

    valid = iota((tiles, width), 0) < used
    raw = [
        jnp.where(valid, joined(raw_ref, pl.ds(c, tiles, stride=8)), 0.0) for c in range(4)
    ]
    spacing = joined(rows_ref, pl.ds(7, tiles, stride=8))
    decay = jnp.exp(-jnp.abs(raw[0]))
    density = jnp.maximum(raw[0], 0.0) + jnp.log1p(decay)
    slope = jnp.where(raw[0] >= 0, 1.0, decay) / (1.0 + decay)
    colour = [1.0 / (1.0 + jnp.exp(-raw[c])) for c in (1, 2, 3)]
    optical = density * spacing
    lane_a, lane_b = iota((width, width), 0), iota((width, width), 1)
    same = (lane_a // samples) == (lane_b // samples)
    up_to = ones_where(same & (lane_a <= lane_b))
    after = ones_where(same & (lane_a > lane_b))

    def by_pieces(value, matrix):
        return functools.reduce(jnp.add, [dot(p.astype(BF16), matrix) for p in pieces(value, 2)])

    running = by_pieces(optical, up_to)
    passed = jnp.exp(-running)
    weight = jnp.exp(optical - running) * (1.0 - jnp.exp(-optical))
    weighted = [weight * one for one in colour]

    member = ones_where(iota((GROUP, width), 0) == iota((GROUP, width), 1) // samples)
    sums = []
    for value in weighted + [optical]:
        sums.append(functools.reduce(jnp.add, [dot_nt(member, p.astype(BF16)) for p in pieces(value, 2)]))
    segments = rays * crossings
    slot_row = jnp.concatenate([slots_ref[k : k + 1, :] for k in range(crossings)], axis=1)
    tile_row = jnp.floor(slot_row * (1.0 / GROUP))
    place_row = slot_row - GROUP * tile_row
    lists = ones_where(iota((tiles, segments), 0).astype(F32) == tile_row)
    mine = iota((GROUP, segments), 0).astype(F32) == place_row
    in_tile = folded(dot(stacked(jnp.concatenate(sums, axis=0), 0, 2), lists), 2)
    by_ray = [
        jnp.sum(jnp.where(mine, in_tile[c * GROUP : (c + 1) * GROUP], 0.0), axis=0, keepdims=True)
        for c in range(4)
    ]
    seg_colour = jnp.concatenate(by_ray[:3], axis=0)
    seg_trans = jnp.exp(-by_ray[3])

    upstream = colour_grad_ref[...]
    colours = [seg_colour[:, k * rays : (k + 1) * rays] for k in range(crossings)]
    transes = [seg_trans[:, k * rays : (k + 1) * rays] for k in range(crossings)]
    before = jnp.ones((1, rays), F32)
    befores = []
    rendered = jnp.zeros_like(upstream)
    for k in range(crossings):
        befores.append(before)
        rendered = rendered + before * colours[k]
        before = before * transes[k]
    rendered_ref[...] = rendered
    behind = jnp.zeros_like(upstream)
    grads = [None] * crossings
    for k in range(crossings - 1, -1, -1):
        grad_trans = befores[k] * jnp.sum(upstream * behind, axis=0, keepdims=True)
        grads[k] = jnp.concatenate([befores[k] * upstream, grad_trans * transes[k]], axis=0)
        behind = colours[k] + transes[k] * behind
    grads = jnp.concatenate(grads, axis=1)

    placed = jnp.concatenate([jnp.where(mine, grads[c : c + 1], 0.0) for c in range(4)], axis=0)
    in_slots = dot_nt(lists, stacked(placed, 0, 2)).astype(BF16)
    channel_rows = iota((8 * GROUP, width), 0) % (4 * GROUP)
    lane_place = iota((8 * GROUP, width), 1) // samples
    per_sample = [
        dot(in_slots, ones_where(channel_rows == c * GROUP + lane_place)) for c in range(4)
    ]
    inner = functools.reduce(jnp.add, [per_sample[c] * colour[c] for c in range(3)])
    later = by_pieces(weight * inner, after)
    grad_optical = passed * inner - later - per_sample[3]
    raw_grad = [grad_optical * spacing * slope]
    for c in range(3):
        raw_grad.append(per_sample[c] * weighted[c] * (1.0 - colour[c]))
    for c in range(4):
        for half in range(halves):
            at = pl.ds(c, tiles, stride=8)
            raw_ref[half, at, :] = raw_grad[c][:, half * lanes : (half + 1) * lanes]

    head_grad_ref[...] = jnp.zeros(head_grad_ref.shape, F32)

    def backward(step, _):
        first = step * UNROLL
        products = []
        for index in range(UNROLL):
            gradient = joined(raw_ref, tile_rows(first + index, 8)).astype(BF16)
            products.append(dot_nt(gradient, hidden_ref[tile_rows(first + index, units), :])[:4])
        for index in range(UNROLL):
            head_grad_ref[meta_ref[0, first + index]] += products[index]
        return 0

    lax.fori_loop(0, rounds, backward, 0)


def exchange_stages(count):
    stages = []
    while count > 1:
        size = 4 if count % 4 == 0 and count > 4 else min(count, 4)
        size = 2 if count == 2 else size
        count //= size
        stages.append((count, size))
    return stages


def place(offset, stages):
    a, b = [(offset // unit) % size for unit, size in stages[:2]]
    at = jnp.where(b == 0, a, jnp.where(a == 0, 3 + b, 3 + 3 * b + a))
    scale = 16
    for unit, size in stages[2:]:
        at = at + ((offset // unit) % size) * scale
        scale = scale * size
    return at


def share(block, stage, count):
    unit, size = stage
    held = [block]
    for other in range(1, size):
        pairs = [(i, i ^ (unit * other)) for i in range(count)]
        held.append(lax.ppermute(block, "region", pairs))
    return held


def on_device(sample_points, sample_spacing, crossed, colour_grad, freq, w_hidden, w_head):
    regions = lax.axis_size("region")
    rays, crossings = crossed.shape
    samples = sample_spacing.shape[1] // crossings
    segments = rays * crossings
    tiles = (segments + (GROUP - 1) * regions) // GROUP
    tiles = -(-tiles // UNROLL) * UNROLL
    width, lanes = GROUP * samples, crossings * samples
    halves = width // lanes
    features = w_hidden.shape[1]
    hidden_units = w_hidden.shape[2]
    dims = (regions, rays, crossings, samples, tiles)
    vmem, smem = pltpu.VMEM, pltpu.SMEM
    mib = 1024 * 1024
    limit = 2 * tiles * width * hidden_units + 8 * halves * tiles * 8 * lanes
    limit += 2 * regions * (2 * hidden_units + 16) * features + 4 * mib
    limit += 2 * 2 * UNROLL * features * width + 4 * mib
    small_limit = 24 * mib
    params = pltpu.CompilerParams(vmem_limit_bytes=limit)

    me = lax.axis_index("region").astype(jnp.int32).reshape(1)
    meta_width = -(-tiles // 128) * 128
    stages = exchange_stages(regions)
    all_samples = jnp.concatenate([sample_points.transpose(1, 0, 2), sample_spacing[None]], axis=0)
    small = jnp.pad(freq[0], ((0, 1), (0, hidden_units - freq.shape[2])))
    small = jnp.concatenate([w_head[0], small], axis=0)
    halves_of_small = [small[:, i : i + features] for i in range(0, hidden_units, features)]
    own = jnp.concatenate([w_hidden[0].T, *halves_of_small], axis=0)[None]
    first = share(own, stages[0], regions)
    own_second = share(own, stages[1], regions)
    others, listed, own_second[1] = lax.optimization_barrier(
        (jnp.concatenate(first[1:], axis=0), crossed.T, own_second[1])
    )
    second = share(others, stages[1], regions)
    slots, meta, rows = pl.pallas_call(
        functools.partial(order_kernel, dims),
        out_shape=(
            jax.ShapeDtypeStruct((crossings, rays), F32),
            jax.ShapeDtypeStruct((2, meta_width), jnp.int32),
            jax.ShapeDtypeStruct((halves, tiles * 8, lanes), F32),
        ),
        in_specs=[pl.BlockSpec(memory_space=vmem)] * 2,
        out_specs=[pl.BlockSpec(memory_space=vmem)] * 3,
        compiler_params=pltpu.CompilerParams(vmem_limit_bytes=small_limit),
        cost_estimate=pl.CostEstimate(flops=4 * 10**9, bytes_accessed=10**7, transcendentals=0),
        name="order",
    )(all_samples, listed)

    early = jnp.concatenate([own, others], axis=0)
    if len(stages) > 3:
        near = jnp.concatenate([early, *own_second[1:], *second[1:]], axis=0)
        for stage in stages[2:-1]:
            near = jnp.concatenate(share(near, stage, regions), axis=0)
        weights = share(near, stages[-1], regions)
    else:
        early, far = share(early, stages[-1], regions)
        far, slots, *second = lax.optimization_barrier((far, slots, *second[1:]))
        late = jnp.concatenate([*own_second[1:], *second], axis=0)
        late, far_late = share(late, stages[-1], regions)
        weights = [early, late, far, far_late]

    whole = pl.BlockSpec(memory_space=vmem)

    rendered, head_grad = pl.pallas_call(
        functools.partial(main_kernel, dims, stages, len(weights)),
        out_shape=(
            jax.ShapeDtypeStruct((3, rays), F32),
            jax.ShapeDtypeStruct((regions, 4, hidden_units), F32),
        ),
        in_specs=[pl.BlockSpec(memory_space=smem)] * 2
        + [whole] * (3 + len(weights)),
        out_specs=[whole] * 2,
        scratch_shapes=[
            pltpu.VMEM((tiles * hidden_units, width), BF16),
            pltpu.VMEM((halves, tiles * 8, lanes), F32),
            pltpu.VMEM((regions, hidden_units, features), BF16),
            pltpu.VMEM((regions, features // 2, 128), BF16),
            pltpu.VMEM((regions, 8, hidden_units), BF16),
            pltpu.VMEM((2, UNROLL * features, width), BF16),
            pltpu.SemaphoreType.DMA((len(weights),)),
        ],
        compiler_params=params,
        cost_estimate=pl.CostEstimate(flops=2 * 10**10, bytes_accessed=3 * 10**7, transcendentals=0),
        name="render",
    )(meta, me, slots, rows, colour_grad, *weights)

    partial_sums = lax.all_to_all(head_grad, "region", split_axis=0, concat_axis=0, tiled=True)
    head_grad = jnp.sum(partial_sums, axis=0, keepdims=True)
    return (rendered, head_grad)


def solution(mesh):
    return jax.shard_map(
        on_device,
        mesh=mesh,
        in_specs=(
            P("region", None, None),
            P("region", None),
            P("region", None),
            P(None, "region"),
            P("region", None, None),
            P("region", None, None),
            P("region", None, None),
        ),
        out_specs=(P(None, "region"), P("region", None, None)),
        check_vma=False,
    )
```

```python
import functools
import jax
import jax.numpy as jnp
from jax import lax
from jax.experimental import pallas as pl
from jax.experimental.pallas import tpu as pltpu
from jax.sharding import PartitionSpec as P

F32 = jnp.float32
BF16 = jnp.bfloat16
GROUP = 8
UNROLL = 16
SIN_HALF = (4.44288292, -7.3082457, 3.60635441, -0.84611289, 0.10982699)
TURN = 0.15915494309189535
ROUNDER = 12582912.0


def pieces(value, count):
    parts = []
    for _ in range(count - 1):
        parts.append(value.astype(BF16).astype(F32))
        value = value - parts[-1]
    return parts + [value]


def stacked(value, axis, count):
    return jnp.concatenate(pieces(value, count), axis=axis).astype(BF16)


def folded(value, count):
    rows = value.shape[0] // count
    return functools.reduce(jnp.add, [value[i * rows : (i + 1) * rows] for i in range(count)])


def dot(a, b):
    return lax.dot_general(a, b, (((1,), (0,)), ((), ())), preferred_element_type=F32)


def dot_nt(a, b):
    return lax.dot_general(a, b, (((1,), (1,)), ((), ())), preferred_element_type=F32)


def iota(shape, axis):
    return lax.broadcasted_iota(jnp.int32, shape, axis)


def joined(ref, at):
    return jnp.concatenate([ref[half, at, :] for half in range(ref.shape[0])], axis=1)


def ones_where(condition):
    return jnp.where(condition, 1.0, 0.0).astype(BF16)


def order_kernel(dims, samples_ref, crossed_ref, slots_ref, meta_ref, rows_ref):
    regions, rays, crossings, samples, tiles = dims
    lanes = crossings * samples
    width = meta_ref.shape[1]
    region_at = iota((regions, rays), 0)
    named = [jnp.where(crossed_ref[k : k + 1, :] == region_at, 1.0, 0.0) for k in range(crossings)]
    listed = functools.reduce(jnp.add, named)
    earlier = ones_where(iota((rays, rays), 0) < iota((rays, rays), 1))
    rank = dot(listed.astype(BF16), earlier)
    count = jnp.sum(listed, axis=1, keepdims=True)
    tile_count = jnp.floor((count + (GROUP - 1)) * (1.0 / GROUP))
    below = ones_where(iota((regions, regions), 1) < iota((regions, regions), 0))
    tile_count = jnp.broadcast_to(tile_count, (regions, width))
    start = dot(below, tile_count.astype(BF16))
    slot = GROUP * start[:, :1] + rank
    slot_rows = [jnp.sum(one * slot, axis=0, keepdims=True) for one in named]
    slots_ref[...] = jnp.concatenate(slot_rows, axis=0)
    ended = jnp.where(start + tile_count <= iota((regions, width), 1).astype(F32), 1.0, 0.0)
    owner = jnp.minimum(jnp.sum(ended, axis=0, keepdims=True), regions - 1.0)
    used = jnp.sum(tile_count, axis=0, keepdims=True)
    meta_ref[...] = jnp.concatenate([owner, used], axis=0).astype(jnp.int32)

    slot_row = jnp.concatenate(slot_rows, axis=1)
    parts = [samples_ref[d] * TURN for d in range(3)] + [samples_ref[3]]
    lane_group = iota((rays, lanes), 1) // samples
    by_segment = []
    for k in range(crossings):
        row = jnp.zeros((rays, lanes), F32)
        for d in range(4):
            moved = pltpu.roll(parts[d], (samples * (d - k)) % lanes, 1) if d != k else parts[d]
            row = jnp.where(lane_group == d, moved, row)
        by_segment.append(row)
    source = stacked(jnp.concatenate(by_segment, axis=0), 1, 3)
    tile_row = jnp.floor(slot_row * (1.0 / GROUP))
    place_row = slot_row - GROUP * tile_row
    in_tile = ones_where(iota((tiles, rays * crossings), 0).astype(F32) == tile_row)
    out_group = iota((tiles, lanes), 1) // samples
    per_row = lanes // samples
    halves = GROUP // per_row
    dense = [[None] * halves for _ in range(4)]
    for s in range(GROUP):
        got = dot(in_tile * ones_where(place_row == s), source)
        got = got[:, :lanes] + got[:, lanes : 2 * lanes] + got[:, 2 * lanes :]
        at, half = s % per_row, s // per_row
        for d in range(4):
            moved = pltpu.roll(got, (samples * (at - d)) % lanes, 1) if d != at else got
            if at == 0:
                dense[d][half] = moved
            else:
                dense[d][half] = jnp.where(out_group == at, moved, dense[d][half])
    rows_ref[...] = jnp.zeros(rows_ref.shape, F32)
    for d in range(4):
        for half in range(halves):
            rows_ref[half, pl.ds(4 + d, tiles, stride=8), :] = dense[d][half]


def tile_rows(tile, height):
    return pl.ds(pl.multiple_of(tile * height, height), height)


def store_features(turns, feature_ref, first):
    half = turns.shape[0]
    for at in range(0, half, 16):
        part = turns[at : at + 16]
        rest = part - ((part + ROUNDER) - ROUNDER)
        square = rest * rest
        sine = jnp.full_like(square, SIN_HALF[-1])
        for c in SIN_HALF[-2::-1]:
            sine = sine * square + c
        sine = sine * rest
        twice = sine * sine
        left = jnp.maximum(2.0 - twice, 1e-30)
        rows = slice(first + at, first + at + 16)
        feature_ref[rows, :] = (sine * (left * lax.rsqrt(left))).astype(BF16)
        rows = slice(first + half + at, first + half + at + 16)
        feature_ref[rows, :] = (1.0 - twice).astype(BF16)


def main_kernel(
    dims,
    stages,
    parts,
    meta_ref,
    me_ref,
    slots_ref,
    rows_ref,
    colour_grad_ref,
    *refs,
):
    part_refs = refs[:parts]
    rendered_ref, head_grad_ref, hidden_ref, raw_ref, weight_ref = refs[parts : parts + 5]
    freq_ref, head_ref, slab_ref, sems = refs[parts + 5 :]
    regions, rays, crossings, samples, tiles = dims
    width = GROUP * samples
    halves, lanes = raw_ref.shape[0], raw_ref.shape[2]
    used = meta_ref[1, 0]
    me = me_ref[0]
    rounds = (used + (UNROLL - 1)) // UNROLL
    units = hidden_ref.shape[0] // tiles
    depth = slab_ref.shape[1] // UNROLL

    places = [0]
    for part in part_refs:
        places.append(places[-1] + part.shape[0])
    copies = []
    for p, part in enumerate(part_refs):
        source, target = part.at[:, :units, :], weight_ref.at[places[p] : places[p + 1]]
        copies.append(pltpu.make_async_copy(source, target, sems.at[p]))
    for copy in copies:
        copy.start()

    def table(part, start, index):
        both = part[index, units:, :].astype(F32)
        freq_ref[start + index, :, :24] = jnp.concatenate([both[:8]] * 3, axis=0).T[: depth // 2].astype(BF16)
        head_ref[start + index] = jnp.concatenate([both[:8], both[8:]], axis=1).astype(BF16)

    for start, part in zip(places, part_refs):
        if part.shape[0] <= 16:
            for index in range(part.shape[0]):
                table(part, start, index)
        else:
            lax.fori_loop(0, part.shape[0], lambda i, _: (table(part, start, i), 0)[1], 0)

    def at_of(tile):
        return place(meta_ref[0, tile] ^ me, stages)

    def phases(tile):
        points = stacked(joined(rows_ref, tile_rows(tile, 8)), 0, 3)
        return dot(freq_ref[at_of(tile), :, :24], points)

    ahead = phases(0)
    for index in range(UNROLL):
        turns = ahead
        if index + 1 < UNROLL:
            ahead = phases(index + 1)
        store_features(turns, slab_ref.at[0], index * depth)
    for copy in copies:
        copy.wait()

    def work(step, more):
        first = step * UNROLL
        slot = lax.rem(step, 2)

        def layer(index):
            weights = weight_ref[at_of(first + index)]
            return dot(weights, slab_ref[slot, index * depth : (index + 1) * depth, :])

        ahead = layer(0)
        turns_ahead = phases(first + UNROLL) if more else None
        for index in range(UNROLL):
            result, turns = ahead, turns_ahead
            if index + 1 < UNROLL:
                ahead = layer(index + 1)
                turns_ahead = phases(first + UNROLL + index + 1) if more else None
            head(jnp.maximum(first - UNROLL, 0) + index)
            if more:
                store_features(turns, slab_ref.at[1 - slot], index * depth)
            hidden_ref[tile_rows(first + index, units), :] = jnp.maximum(result.astype(BF16), 0)

    def forward(step, _):
        work(step, True)
        return 0

    def head(tile):
        raw = dot(head_ref[at_of(tile)], hidden_ref[tile_rows(tile, units), :])
        for half in range(halves):
            raw_ref[half, tile_rows(tile, 8), :] = raw[:, half * lanes : (half + 1) * lanes]

    lax.fori_loop(0, rounds - 1, forward, 0)
    work(rounds - 1, False)
    for index in range(UNROLL):
        head((rounds - 1) * UNROLL + index)

    valid = iota((tiles, width), 0) < used
    raw = [
        jnp.where(valid, joined(raw_ref, pl.ds(c, tiles, stride=8)), 0.0) for c in range(4)
    ]
    spacing = joined(rows_ref, pl.ds(7, tiles, stride=8))
    decay = jnp.exp(-jnp.abs(raw[0]))
    density = jnp.maximum(raw[0], 0.0) + jnp.log1p(decay)
    slope = jnp.where(raw[0] >= 0, 1.0, decay) / (1.0 + decay)
    colour = [1.0 / (1.0 + jnp.exp(-raw[c])) for c in (1, 2, 3)]
    optical = density * spacing
    lane_a, lane_b = iota((width, width), 0), iota((width, width), 1)
    same = (lane_a // samples) == (lane_b // samples)
    up_to = ones_where(same & (lane_a <= lane_b))
    after = ones_where(same & (lane_a > lane_b))

    def by_pieces(value, matrix):
        return functools.reduce(jnp.add, [dot(p.astype(BF16), matrix) for p in pieces(value, 2)])

    running = by_pieces(optical, up_to)
    passed = jnp.exp(-running)
    weight = jnp.exp(optical - running) * (1.0 - jnp.exp(-optical))
    weighted = [weight * one for one in colour]

    member = ones_where(iota((GROUP, width), 0) == iota((GROUP, width), 1) // samples)
    sums = []
    for value in weighted + [optical]:
        sums.append(functools.reduce(jnp.add, [dot_nt(member, p.astype(BF16)) for p in pieces(value, 2)]))
    segments = rays * crossings
    slot_row = jnp.concatenate([slots_ref[k : k + 1, :] for k in range(crossings)], axis=1)
    tile_row = jnp.floor(slot_row * (1.0 / GROUP))
    place_row = slot_row - GROUP * tile_row
    lists = ones_where(iota((tiles, segments), 0).astype(F32) == tile_row)
    mine = iota((GROUP, segments), 0).astype(F32) == place_row
    in_tile = folded(dot(stacked(jnp.concatenate(sums, axis=0), 0, 2), lists), 2)
    by_ray = [
        jnp.sum(jnp.where(mine, in_tile[c * GROUP : (c + 1) * GROUP], 0.0), axis=0, keepdims=True)
        for c in range(4)
    ]
    seg_colour = jnp.concatenate(by_ray[:3], axis=0)
    seg_trans = jnp.exp(-by_ray[3])

    upstream = colour_grad_ref[...]
    colours = [seg_colour[:, k * rays : (k + 1) * rays] for k in range(crossings)]
    transes = [seg_trans[:, k * rays : (k + 1) * rays] for k in range(crossings)]
    before = jnp.ones((1, rays), F32)
    befores = []
    rendered = jnp.zeros_like(upstream)
    for k in range(crossings):
        befores.append(before)
        rendered = rendered + before * colours[k]
        before = before * transes[k]
    rendered_ref[...] = rendered
    behind = jnp.zeros_like(upstream)
    grads = [None] * crossings
    for k in range(crossings - 1, -1, -1):
        grad_trans = befores[k] * jnp.sum(upstream * behind, axis=0, keepdims=True)
        grads[k] = jnp.concatenate([befores[k] * upstream, grad_trans * transes[k]], axis=0)
        behind = colours[k] + transes[k] * behind
    grads = jnp.concatenate(grads, axis=1)

    placed = jnp.concatenate([jnp.where(mine, grads[c : c + 1], 0.0) for c in range(4)], axis=0)
    in_slots = dot_nt(lists, stacked(placed, 0, 2)).astype(BF16)
    channel_rows = iota((8 * GROUP, width), 0) % (4 * GROUP)
    lane_place = iota((8 * GROUP, width), 1) // samples
    per_sample = [
        dot(in_slots, ones_where(channel_rows == c * GROUP + lane_place)) for c in range(4)
    ]
    inner = functools.reduce(jnp.add, [per_sample[c] * colour[c] for c in range(3)])
    later = by_pieces(weight * inner, after)
    grad_optical = passed * inner - later - per_sample[3]
    raw_grad = [grad_optical * spacing * slope]
    for c in range(3):
        raw_grad.append(per_sample[c] * weighted[c] * (1.0 - colour[c]))
    for c in range(4):
        for half in range(halves):
            at = pl.ds(c, tiles, stride=8)
            raw_ref[half, at, :] = raw_grad[c][:, half * lanes : (half + 1) * lanes]

    head_grad_ref[...] = jnp.zeros(head_grad_ref.shape, F32)

    def backward(step, _):
        first = step * UNROLL
        products = []
        for index in range(UNROLL):
            gradient = joined(raw_ref, tile_rows(first + index, 8)).astype(BF16)
            products.append(dot_nt(gradient, hidden_ref[tile_rows(first + index, units), :])[:4])
        for index in range(UNROLL):
            head_grad_ref[meta_ref[0, first + index]] += products[index]
        return 0

    lax.fori_loop(0, rounds, backward, 0)


def exchange_stages(count):
    stages = []
    while count > 1:
        size = 4 if count % 4 == 0 and count > 4 else min(count, 4)
        size = 2 if count == 2 else size
        count //= size
        stages.append((count, size))
    return stages


def place(offset, stages):
    a, b = [(offset // unit) % size for unit, size in stages[:2]]
    at = jnp.where(b == 0, a, jnp.where(a == 0, 3 + b, 3 + 3 * b + a))
    scale = 16
    for unit, size in stages[2:]:
        at = at + ((offset // unit) % size) * scale
        scale = scale * size
    return at


def share(block, stage, count):
    unit, size = stage
    held = [block]
    for other in range(1, size):
        pairs = [(i, i ^ (unit * other)) for i in range(count)]
        held.append(lax.ppermute(block, "region", pairs))
    return held


def on_device(sample_points, sample_spacing, crossed, colour_grad, freq, w_hidden, w_head):
    regions = lax.axis_size("region")
    rays, crossings = crossed.shape
    samples = sample_spacing.shape[1] // crossings
    segments = rays * crossings
    tiles = (segments + (GROUP - 1) * regions) // GROUP
    tiles = -(-tiles // UNROLL) * UNROLL
    width, lanes = GROUP * samples, crossings * samples
    halves = width // lanes
    features = w_hidden.shape[1]
    hidden_units = w_hidden.shape[2]
    dims = (regions, rays, crossings, samples, tiles)
    vmem, smem = pltpu.VMEM, pltpu.SMEM
    mib = 1024 * 1024
    limit = 2 * tiles * width * hidden_units + 8 * halves * tiles * 8 * lanes
    limit += 2 * regions * (2 * hidden_units + 16) * features + 4 * mib
    limit += 2 * 2 * UNROLL * features * width + 4 * mib
    small_limit = 24 * mib
    params = pltpu.CompilerParams(vmem_limit_bytes=limit)

    me = lax.axis_index("region").astype(jnp.int32).reshape(1)
    meta_width = -(-tiles // 128) * 128
    stages = exchange_stages(regions)
    all_samples = jnp.concatenate([sample_points.transpose(1, 0, 2), sample_spacing[None]], axis=0)
    small = jnp.pad(freq[0], ((0, 1), (0, hidden_units - freq.shape[2])))
    small = jnp.concatenate([w_head[0], small], axis=0)
    halves_of_small = [small[:, i : i + features] for i in range(0, hidden_units, features)]
    own = jnp.concatenate([w_hidden[0].T, *halves_of_small], axis=0)[None]
    first = share(own, stages[0], regions)
    own_second = share(own, stages[1], regions)
    others, own_second[1] = lax.optimization_barrier(
        (jnp.concatenate(first[1:], axis=0), own_second[1])
    )
    second = share(others, stages[1], regions)
    second[1], listed = lax.optimization_barrier((second[1], crossed.T))
    slots, meta, rows = pl.pallas_call(
        functools.partial(order_kernel, dims),
        out_shape=(
            jax.ShapeDtypeStruct((crossings, rays), F32),
            jax.ShapeDtypeStruct((2, meta_width), jnp.int32),
            jax.ShapeDtypeStruct((halves, tiles * 8, lanes), F32),
        ),
        in_specs=[pl.BlockSpec(memory_space=vmem)] * 2,
        out_specs=[pl.BlockSpec(memory_space=vmem)] * 3,
        compiler_params=pltpu.CompilerParams(vmem_limit_bytes=small_limit),
        cost_estimate=pl.CostEstimate(flops=4 * 10**9, bytes_accessed=10**7, transcendentals=0),
        name="order",
    )(all_samples, listed)

    early = jnp.concatenate([own, others], axis=0)
    if len(stages) > 3:
        near = jnp.concatenate([early, *own_second[1:], *second[1:]], axis=0)
        for stage in stages[2:-1]:
            near = jnp.concatenate(share(near, stage, regions), axis=0)
        weights = share(near, stages[-1], regions)
    else:
        early, far = share(early, stages[-1], regions)
        far, slots, *second = lax.optimization_barrier((far, slots, *second[1:]))
        late = jnp.concatenate([*own_second[1:], *second], axis=0)
        late, far_late = share(late, stages[-1], regions)
        weights = [early, late, far, far_late]

    whole = pl.BlockSpec(memory_space=vmem)

    rendered, head_grad = pl.pallas_call(
        functools.partial(main_kernel, dims, stages, len(weights)),
        out_shape=(
            jax.ShapeDtypeStruct((3, rays), F32),
            jax.ShapeDtypeStruct((regions, 4, hidden_units), F32),
        ),
        in_specs=[pl.BlockSpec(memory_space=smem)] * 2
        + [whole] * (3 + len(weights)),
        out_specs=[whole] * 2,
        scratch_shapes=[
            pltpu.VMEM((tiles * hidden_units, width), BF16),
            pltpu.VMEM((halves, tiles * 8, lanes), F32),
            pltpu.VMEM((regions, hidden_units, features), BF16),
            pltpu.VMEM((regions, features // 2, 128), BF16),
            pltpu.VMEM((regions, 8, hidden_units), BF16),
            pltpu.VMEM((2, UNROLL * features, width), BF16),
            pltpu.SemaphoreType.DMA((len(weights),)),
        ],
        compiler_params=params,
        cost_estimate=pl.CostEstimate(flops=2 * 10**10, bytes_accessed=3 * 10**7, transcendentals=0),
        name="render",
    )(meta, me, slots, rows, colour_grad, *weights)

    partial_sums = lax.all_to_all(head_grad, "region", split_axis=0, concat_axis=0, tiled=True)
    head_grad = jnp.sum(partial_sums, axis=0, keepdims=True)
    return (rendered, head_grad)


def solution(mesh):
    return jax.shard_map(
        on_device,
        mesh=mesh,
        in_specs=(
            P("region", None, None),
            P("region", None),
            P("region", None),
            P(None, "region"),
            P("region", None, None),
            P("region", None, None),
            P("region", None, None),
        ),
        out_specs=(P(None, "region"), P("region", None, None)),
        check_vma=False,
    )
```

```python
import functools
import jax
import jax.numpy as jnp
from jax import lax
from jax.experimental import pallas as pl
from jax.experimental.pallas import tpu as pltpu
from jax.sharding import PartitionSpec as P

F32 = jnp.float32
BF16 = jnp.bfloat16
GROUP = 8
UNROLL = 16
SIN_HALF = (4.44288292, -7.3082457, 3.60635441, -0.84611289, 0.10982699)
TURN = 0.15915494309189535
ROUNDER = 12582912.0


def pieces(value, count):
    parts = []
    for _ in range(count - 1):
        parts.append(value.astype(BF16).astype(F32))
        value = value - parts[-1]
    return parts + [value]


def stacked(value, axis, count):
    return jnp.concatenate(pieces(value, count), axis=axis).astype(BF16)


def folded(value, count):
    rows = value.shape[0] // count
    return functools.reduce(jnp.add, [value[i * rows : (i + 1) * rows] for i in range(count)])


def dot(a, b):
    return lax.dot_general(a, b, (((1,), (0,)), ((), ())), preferred_element_type=F32)


def dot_nt(a, b):
    return lax.dot_general(a, b, (((1,), (1,)), ((), ())), preferred_element_type=F32)


def iota(shape, axis):
    return lax.broadcasted_iota(jnp.int32, shape, axis)


def joined(ref, at):
    return jnp.concatenate([ref[half, at, :] for half in range(ref.shape[0])], axis=1)


def ones_where(condition):
    return jnp.where(condition, 1.0, 0.0).astype(BF16)


def order_kernel(dims, samples_ref, crossed_ref, slots_ref, meta_ref, rows_ref):
    regions, rays, crossings, samples, tiles = dims
    lanes = crossings * samples
    width = meta_ref.shape[1]
    region_at = iota((regions, rays), 0)
    named = [jnp.where(crossed_ref[k : k + 1, :] == region_at, 1.0, 0.0) for k in range(crossings)]
    listed = functools.reduce(jnp.add, named)
    earlier = ones_where(iota((rays, rays), 0) < iota((rays, rays), 1))
    rank = dot(listed.astype(BF16), earlier)
    count = jnp.sum(listed, axis=1, keepdims=True)
    tile_count = jnp.floor((count + (GROUP - 1)) * (1.0 / GROUP))
    below = ones_where(iota((regions, regions), 1) < iota((regions, regions), 0))
    tile_count = jnp.broadcast_to(tile_count, (regions, width))
    start = dot(below, tile_count.astype(BF16))
    slot = GROUP * start[:, :1] + rank
    slot_rows = [jnp.sum(one * slot, axis=0, keepdims=True) for one in named]
    slots_ref[...] = jnp.concatenate(slot_rows, axis=0)
    ended = jnp.where(start + tile_count <= iota((regions, width), 1).astype(F32), 1.0, 0.0)
    owner = jnp.minimum(jnp.sum(ended, axis=0, keepdims=True), regions - 1.0)
    used = jnp.sum(tile_count, axis=0, keepdims=True)
    meta_ref[...] = jnp.concatenate([owner, used], axis=0).astype(jnp.int32)

    slot_row = jnp.concatenate(slot_rows, axis=1)
    parts = [samples_ref[d] * TURN for d in range(3)] + [samples_ref[3]]
    lane_group = iota((rays, lanes), 1) // samples
    by_segment = []
    for k in range(crossings):
        row = jnp.zeros((rays, lanes), F32)
        for d in range(4):
            moved = pltpu.roll(parts[d], (samples * (d - k)) % lanes, 1) if d != k else parts[d]
            row = jnp.where(lane_group == d, moved, row)
        by_segment.append(row)
    source = stacked(jnp.concatenate(by_segment, axis=0), 1, 3)
    tile_row = jnp.floor(slot_row * (1.0 / GROUP))
    place_row = slot_row - GROUP * tile_row
    in_tile = ones_where(iota((tiles, rays * crossings), 0).astype(F32) == tile_row)
    out_group = iota((tiles, lanes), 1) // samples
    per_row = lanes // samples
    halves = GROUP // per_row
    dense = [[None] * halves for _ in range(4)]
    for s in range(GROUP):
        got = dot(in_tile * ones_where(place_row == s), source)
        got = got[:, :lanes] + got[:, lanes : 2 * lanes] + got[:, 2 * lanes :]
        at, half = s % per_row, s // per_row
        for d in range(4):
            moved = pltpu.roll(got, (samples * (at - d)) % lanes, 1) if d != at else got
            if at == 0:
                dense[d][half] = moved
            else:
                dense[d][half] = jnp.where(out_group == at, moved, dense[d][half])
    rows_ref[...] = jnp.zeros(rows_ref.shape, F32)
    for d in range(4):
        for half in range(halves):
            rows_ref[half, pl.ds(4 + d, tiles, stride=8), :] = dense[d][half]


def tile_rows(tile, height):
    return pl.ds(pl.multiple_of(tile * height, height), height)


def store_features(turns, feature_ref, first):
    half = turns.shape[0]
    for at in range(0, half, 16):
        part = turns[at : at + 16]
        rest = part - ((part + ROUNDER) - ROUNDER)
        square = rest * rest
        sine = jnp.full_like(square, SIN_HALF[-1])
        for c in SIN_HALF[-2::-1]:
            sine = sine * square + c
        sine = sine * rest
        twice = sine * sine
        left = jnp.maximum(2.0 - twice, 1e-30)
        rows = slice(first + at, first + at + 16)
        feature_ref[rows, :] = (sine * (left * lax.rsqrt(left))).astype(BF16)
        rows = slice(first + half + at, first + half + at + 16)
        feature_ref[rows, :] = (1.0 - twice).astype(BF16)


def main_kernel(
    dims,
    stages,
    parts,
    meta_ref,
    me_ref,
    slots_ref,
    rows_ref,
    colour_grad_ref,
    *refs,
):
    part_refs = refs[:parts]
    rendered_ref, head_grad_ref, hidden_ref, raw_ref, weight_ref = refs[parts : parts + 5]
    freq_ref, head_ref, slab_ref, sems = refs[parts + 5 :]
    regions, rays, crossings, samples, tiles = dims
    width = GROUP * samples
    halves, lanes = raw_ref.shape[0], raw_ref.shape[2]
    used = meta_ref[1, 0]
    me = me_ref[0]
    rounds = (used + (UNROLL - 1)) // UNROLL
    units = hidden_ref.shape[0] // tiles
    depth = slab_ref.shape[1] // UNROLL

    places = [0]
    for part in part_refs:
        places.append(places[-1] + part.shape[0])
    copies = []
    for p, part in enumerate(part_refs):
        source, target = part.at[:, :units, :], weight_ref.at[places[p] : places[p + 1]]
        copies.append(pltpu.make_async_copy(source, target, sems.at[p]))
    for copy in copies:
        copy.start()

    def table(part, start, index):
        both = part[index, units:, :].astype(F32)
        freq_ref[start + index, :, :24] = jnp.concatenate([both[:8]] * 3, axis=0).T[: depth // 2].astype(BF16)
        head_ref[start + index] = jnp.concatenate([both[:8], both[8:]], axis=1).astype(BF16)

    for start, part in zip(places, part_refs):
        if part.shape[0] <= 16:
            for index in range(part.shape[0]):
                table(part, start, index)
        else:
            lax.fori_loop(0, part.shape[0], lambda i, _: (table(part, start, i), 0)[1], 0)

    def at_of(tile):
        return place(meta_ref[0, tile] ^ me, stages)

    def phases(tile):
        points = stacked(joined(rows_ref, tile_rows(tile, 8)), 0, 3)
        return dot(freq_ref[at_of(tile), :, :24], points)

    ahead = phases(0)
    for index in range(UNROLL):
        turns = ahead
        if index + 1 < UNROLL:
            ahead = phases(index + 1)
        store_features(turns, slab_ref.at[0], index * depth)
    for copy in copies:
        copy.wait()

    def work(step, more):
        first = step * UNROLL
        slot = lax.rem(step, 2)

        def layer(index):
            weights = weight_ref[at_of(first + index)]
            return dot(weights, slab_ref[slot, index * depth : (index + 1) * depth, :])

        ahead = layer(0)
        turns_ahead = phases(first + UNROLL) if more else None
        for index in range(UNROLL):
            result, turns = ahead, turns_ahead
            if index + 1 < UNROLL:
                ahead = layer(index + 1)
                turns_ahead = phases(first + UNROLL + index + 1) if more else None
            head(jnp.maximum(first - UNROLL, 0) + index)
            if more:
                store_features(turns, slab_ref.at[1 - slot], index * depth)
            hidden_ref[tile_rows(first + index, units), :] = jnp.maximum(result.astype(BF16), 0)

    def forward(step, _):
        work(step, True)
        return 0

    def head(tile):
        raw = dot(head_ref[at_of(tile)], hidden_ref[tile_rows(tile, units), :])
        for half in range(halves):
            raw_ref[half, tile_rows(tile, 8), :] = raw[:, half * lanes : (half + 1) * lanes]

    lax.fori_loop(0, rounds - 1, forward, 0)
    work(rounds - 1, False)
    for index in range(UNROLL):
        head((rounds - 1) * UNROLL + index)

    valid = iota((tiles, width), 0) < used
    raw = [
        jnp.where(valid, joined(raw_ref, pl.ds(c, tiles, stride=8)), 0.0) for c in range(4)
    ]
    spacing = joined(rows_ref, pl.ds(7, tiles, stride=8))
    decay = jnp.exp(-jnp.abs(raw[0]))
    density = jnp.maximum(raw[0], 0.0) + jnp.log1p(decay)
    slope = jnp.where(raw[0] >= 0, 1.0, decay) / (1.0 + decay)
    colour = [1.0 / (1.0 + jnp.exp(-raw[c])) for c in (1, 2, 3)]
    optical = density * spacing
    lane_a, lane_b = iota((width, width), 0), iota((width, width), 1)
    same = (lane_a // samples) == (lane_b // samples)
    up_to = ones_where(same & (lane_a <= lane_b))
    after = ones_where(same & (lane_a > lane_b))

    def by_pieces(value, matrix):
        return functools.reduce(jnp.add, [dot(p.astype(BF16), matrix) for p in pieces(value, 2)])

    running = by_pieces(optical, up_to)
    passed = jnp.exp(-running)
    weight = jnp.exp(optical - running) * (1.0 - jnp.exp(-optical))
    weighted = [weight * one for one in colour]

    member = ones_where(iota((GROUP, width), 0) == iota((GROUP, width), 1) // samples)
    sums = []
    for value in weighted + [optical]:
        sums.append(functools.reduce(jnp.add, [dot_nt(member, p.astype(BF16)) for p in pieces(value, 2)]))
    segments = rays * crossings
    slot_row = jnp.concatenate([slots_ref[k : k + 1, :] for k in range(crossings)], axis=1)
    tile_row = jnp.floor(slot_row * (1.0 / GROUP))
    place_row = slot_row - GROUP * tile_row
    lists = ones_where(iota((tiles, segments), 0).astype(F32) == tile_row)
    mine = iota((GROUP, segments), 0).astype(F32) == place_row
    in_tile = folded(dot(stacked(jnp.concatenate(sums, axis=0), 0, 2), lists), 2)
    by_ray = [
        jnp.sum(jnp.where(mine, in_tile[c * GROUP : (c + 1) * GROUP], 0.0), axis=0, keepdims=True)
        for c in range(4)
    ]
    seg_colour = jnp.concatenate(by_ray[:3], axis=0)
    seg_trans = jnp.exp(-by_ray[3])

    upstream = colour_grad_ref[...]
    colours = [seg_colour[:, k * rays : (k + 1) * rays] for k in range(crossings)]
    transes = [seg_trans[:, k * rays : (k + 1) * rays] for k in range(crossings)]
    before = jnp.ones((1, rays), F32)
    befores = []
    rendered = jnp.zeros_like(upstream)
    for k in range(crossings):
        befores.append(before)
        rendered = rendered + before * colours[k]
        before = before * transes[k]
    rendered_ref[...] = rendered
    behind = jnp.zeros_like(upstream)
    grads = [None] * crossings
    for k in range(crossings - 1, -1, -1):
        grad_trans = befores[k] * jnp.sum(upstream * behind, axis=0, keepdims=True)
        grads[k] = jnp.concatenate([befores[k] * upstream, grad_trans * transes[k]], axis=0)
        behind = colours[k] + transes[k] * behind
    grads = jnp.concatenate(grads, axis=1)

    placed = jnp.concatenate([jnp.where(mine, grads[c : c + 1], 0.0) for c in range(4)], axis=0)
    in_slots = dot_nt(lists, stacked(placed, 0, 2)).astype(BF16)
    channel_rows = iota((8 * GROUP, width), 0) % (4 * GROUP)
    lane_place = iota((8 * GROUP, width), 1) // samples
    per_sample = [
        dot(in_slots, ones_where(channel_rows == c * GROUP + lane_place)) for c in range(4)
    ]
    inner = functools.reduce(jnp.add, [per_sample[c] * colour[c] for c in range(3)])
    later = by_pieces(weight * inner, after)
    grad_optical = passed * inner - later - per_sample[3]
    raw_grad = [grad_optical * spacing * slope]
    for c in range(3):
        raw_grad.append(per_sample[c] * weighted[c] * (1.0 - colour[c]))
    for c in range(4):
        for half in range(halves):
            at = pl.ds(c, tiles, stride=8)
            raw_ref[half, at, :] = raw_grad[c][:, half * lanes : (half + 1) * lanes]

    head_grad_ref[...] = jnp.zeros(head_grad_ref.shape, F32)

    def backward(step, _):
        first = step * UNROLL
        products = []
        for index in range(UNROLL):
            gradient = joined(raw_ref, tile_rows(first + index, 8)).astype(BF16)
            products.append(dot_nt(gradient, hidden_ref[tile_rows(first + index, units), :])[:4])
        for index in range(UNROLL):
            head_grad_ref[meta_ref[0, first + index]] += products[index]
        return 0

    lax.fori_loop(0, rounds, backward, 0)


def exchange_stages(count):
    stages = []
    while count > 1:
        size = 4 if count % 4 == 0 and count > 4 else min(count, 4)
        size = 2 if count == 2 else size
        count //= size
        stages.append((count, size))
    return stages


def place(offset, stages):
    a, b = [(offset // unit) % size for unit, size in stages[:2]]
    at = jnp.where(b == 0, a, jnp.where(a == 0, 3 + b, 3 + 3 * b + a))
    scale = 16
    for unit, size in stages[2:]:
        at = at + ((offset // unit) % size) * scale
        scale = scale * size
    return at


def share(block, stage, count):
    unit, size = stage
    held = [block]
    for other in range(1, size):
        pairs = [(i, i ^ (unit * other)) for i in range(count)]
        held.append(lax.ppermute(block, "region", pairs))
    return held


def on_device(sample_points, sample_spacing, crossed, colour_grad, freq, w_hidden, w_head):
    regions = lax.axis_size("region")
    rays, crossings = crossed.shape
    samples = sample_spacing.shape[1] // crossings
    segments = rays * crossings
    tiles = (segments + (GROUP - 1) * regions) // GROUP
    tiles = -(-tiles // UNROLL) * UNROLL
    width, lanes = GROUP * samples, crossings * samples
    halves = width // lanes
    features = w_hidden.shape[1]
    hidden_units = w_hidden.shape[2]
    dims = (regions, rays, crossings, samples, tiles)
    vmem, smem = pltpu.VMEM, pltpu.SMEM
    mib = 1024 * 1024
    limit = 2 * tiles * width * hidden_units + 8 * halves * tiles * 8 * lanes
    limit += 2 * regions * (2 * hidden_units + 16) * features + 4 * mib
    limit += 2 * 2 * UNROLL * features * width + 4 * mib
    small_limit = 24 * mib
    params = pltpu.CompilerParams(vmem_limit_bytes=limit)

    me = lax.axis_index("region").astype(jnp.int32).reshape(1)
    meta_width = -(-tiles // 128) * 128
    stages = exchange_stages(regions)
    all_samples = jnp.concatenate([sample_points.transpose(1, 0, 2), sample_spacing[None]], axis=0)
    small = jnp.pad(freq[0], ((0, 1), (0, hidden_units - freq.shape[2])))
    small = jnp.concatenate([w_head[0], small], axis=0)
    halves_of_small = [small[:, i : i + features] for i in range(0, hidden_units, features)]
    own = jnp.concatenate([w_hidden[0].T, *halves_of_small], axis=0)[None]
    first = share(own, stages[0], regions)
    own_second = share(own, stages[1], regions)
    others, own_second[1] = lax.optimization_barrier(
        (jnp.concatenate(first[1:], axis=0), own_second[1])
    )
    second = share(others, stages[1], regions)
    listed = crossed.T
    early = jnp.concatenate([own, others], axis=0)
    if len(stages) > 3:
        near = jnp.concatenate([early, *own_second[1:], *second[1:]], axis=0)
        for stage in stages[2:-1]:
            near = jnp.concatenate(share(near, stage, regions), axis=0)
        weights = share(near, stages[-1], regions)
    else:
        early, far = share(early, stages[-1], regions)
        far, listed, *second = lax.optimization_barrier((far, listed, *second[1:]))
        late = jnp.concatenate([*own_second[1:], *second], axis=0)
        late, far_late = share(late, stages[-1], regions)
        weights = [early, late, far, far_late]

    slots, meta, rows = pl.pallas_call(
        functools.partial(order_kernel, dims),
        out_shape=(
            jax.ShapeDtypeStruct((crossings, rays), F32),
            jax.ShapeDtypeStruct((2, meta_width), jnp.int32),
            jax.ShapeDtypeStruct((halves, tiles * 8, lanes), F32),
        ),
        in_specs=[pl.BlockSpec(memory_space=vmem)] * 2,
        out_specs=[pl.BlockSpec(memory_space=vmem)] * 3,
        compiler_params=pltpu.CompilerParams(vmem_limit_bytes=small_limit),
        cost_estimate=pl.CostEstimate(flops=4 * 10**9, bytes_accessed=10**7, transcendentals=0),
        name="order",
    )(all_samples, listed)

    whole = pl.BlockSpec(memory_space=vmem)

    rendered, head_grad = pl.pallas_call(
        functools.partial(main_kernel, dims, stages, len(weights)),
        out_shape=(
            jax.ShapeDtypeStruct((3, rays), F32),
            jax.ShapeDtypeStruct((regions, 4, hidden_units), F32),
        ),
        in_specs=[pl.BlockSpec(memory_space=smem)] * 2
        + [whole] * (3 + len(weights)),
        out_specs=[whole] * 2,
        scratch_shapes=[
            pltpu.VMEM((tiles * hidden_units, width), BF16),
            pltpu.VMEM((halves, tiles * 8, lanes), F32),
            pltpu.VMEM((regions, hidden_units, features), BF16),
            pltpu.VMEM((regions, features // 2, 128), BF16),
            pltpu.VMEM((regions, 8, hidden_units), BF16),
            pltpu.VMEM((2, UNROLL * features, width), BF16),
            pltpu.SemaphoreType.DMA((len(weights),)),
        ],
        compiler_params=params,
        cost_estimate=pl.CostEstimate(flops=2 * 10**10, bytes_accessed=3 * 10**7, transcendentals=0),
        name="render",
    )(meta, me, slots, rows, colour_grad, *weights)

    partial_sums = lax.all_to_all(head_grad, "region", split_axis=0, concat_axis=0, tiled=True)
    head_grad = jnp.sum(partial_sums, axis=0, keepdims=True)
    return (rendered, head_grad)


def solution(mesh):
    return jax.shard_map(
        on_device,
        mesh=mesh,
        in_specs=(
            P("region", None, None),
            P("region", None),
            P("region", None),
            P(None, "region"),
            P("region", None, None),
            P("region", None, None),
            P("region", None, None),
        ),
        out_specs=(P(None, "region"), P("region", None, None)),
        check_vma=False,
    )
```
